32 devices in a mesh: section: 2 (over core), ctx: 8 (over z, x), shard: 2 (over y).
Axes of the slice: x: 2, y: 2, z: 4, core: 2. Of those that a mesh axis runs over, the one named last changes fastest.
Arguments:
- ends_in: bfloat16 [2, 2, 2, 512, 1536], P('section', None, 'shard', 'ctx'), may hold values from -6 to 6
- pair_table: int32 [8], replicated, may hold values from 0 to 7, each once
- norm_attn: bfloat16 [2, 1536], P('section', ('ctx', 'shard')), may hold values from 0.5 to 1.5
- w_query: bfloat16 [2, 1536, 1536], P('section', ('ctx', 'shard')), may hold values from -0.15625 to 0.15625
- w_key: bfloat16 [2, 1536, 768], P('section', ('ctx', 'shard')), may hold values from -0.15625 to 0.15625
- w_value: bfloat16 [2, 1536, 768], P('section', ('ctx', 'shard')), may hold values from -0.15625 to 0.15625
- w_out: bfloat16 [2, 1536, 1536], P('section', ('ctx', 'shard')), may hold values from -1.5 to 1.5
- norm_mlp: bfloat16 [2, 1536], P('section', ('ctx', 'shard')), may hold values from 0.5 to 1.5
- w_gate: bfloat16 [2, 1536, 4096], P('section', ('ctx', 'shard')), may hold values from -0.15625 to 0.15625
- w_up: bfloat16 [2, 1536, 4096], P('section', ('ctx', 'shard')), may hold values from -0.15625 to 0.15625
- w_down: bfloat16 [2, 4096, 1536], P('section', ('ctx', 'shard')), may hold values from -0.09375 to 0.09375
Outputs:
- ends_out: bfloat16 [2, 2, 2, 512, 1536], P('section', None, 'shard', 'ctx')
- norm_attn_grad: float32 [2, 1536], P('section', ('ctx', 'shard'))
- w_query_grad: float32 [2, 1536, 1536], P('section', ('ctx', 'shard'))
- w_key_grad: float32 [2, 1536, 768], P('section', ('ctx', 'shard'))
- w_value_grad: float32 [2, 1536, 768], P('section', ('ctx', 'shard'))
- w_out_grad: float32 [2, 1536, 1536], P('section', ('ctx', 'shard'))
- norm_mlp_grad: float32 [2, 1536], P('section', ('ctx', 'shard'))
- w_gate_grad: float32 [2, 1536, 4096], P('section', ('ctx', 'shard'))
- w_up_grad: float32 [2, 1536, 4096], P('section', ('ctx', 'shard'))
- w_down_grad: float32 [2, 4096, 1536], P('section', ('ctx', 'shard'))
The draws below stay inside these ranges and needn't reach their ends.
Inputs may be any that keep to these rules, and one draw needn't show every extreme that they name: `pair_table`: each value once.
All inputs are finite; a program needn't handle non-finite values.
Results may differ from the reference program's by a relative error of at most 0.024.
Values may be sent and summed in bfloat16 or wider, within the bound.
No kernel may reach another device: no remote copies, remote signals or barrier semaphores. Data moves between devices by JAX's collectives and lax.ppermute only.
A program may use at most 320 MiB of HBM per device.

```python
import math
import jax
import jax.numpy as jnp
from jax import lax

D = 1536
HEADS = 16
KV_HEADS = 8
HEAD_DIM = 96
FF = 4096
BLK = 32
MB = 2
SEQS = 2
LEN = 512
KV_WIDTH = 768
N_SECTION = 2
N_CTX = 8


def block_scale(stream_key, dims, split, least, largest):
    loudness = 1.0
    for position, shards_of in split:
        steps = jax.random.uniform(jax.random.fold_in(jax.random.fold_in(stream_key, 6), position), (shards_of,), jnp.float32, least / len(split), largest / len(split))
        loudness = loudness * jnp.repeat(jnp.exp(steps), dims[position] // shards_of).reshape((-1,) + (1,) * (len(dims) - 1 - position))
    return loudness


def gaussian(rng, shape, spread, limit, cuts=(), kind=jnp.bfloat16):
    drawn = spread * jax.random.normal(rng, shape, jnp.float32)
    if cuts:
        drawn = drawn * block_scale(rng, shape, cuts, -0.22, 0.18)
    return jnp.clip(drawn, -limit, limit).astype(kind)


def setup_inputs(seed: int = 0) -> dict:
    arg_keys = jax.random.split(jax.random.key(seed), 12)
    ends_in = gaussian(arg_keys[0], (N_SECTION, MB, SEQS, LEN, D), 1.0, 6.0, ((0, 2), (2, 2), (3, 8)))
    pair_table = jax.random.permutation(arg_keys[1], N_CTX).astype(jnp.int32)
    norm_attn = jnp.clip(1.0 + 0.1 * jax.random.normal(arg_keys[2], (N_SECTION, D), jnp.float32), 0.5, 1.5).astype(jnp.bfloat16)
    w_query = gaussian(arg_keys[3], (N_SECTION, D, D), D ** -0.5, 0.15625, ((0, 2), (1, 16)))
    w_key = gaussian(arg_keys[4], (N_SECTION, D, KV_WIDTH), D ** -0.5, 0.15625, ((0, 2), (1, 16)))
    w_value = gaussian(arg_keys[5], (N_SECTION, D, KV_WIDTH), D ** -0.5, 0.15625, ((0, 2), (1, 16)))
    w_out = gaussian(arg_keys[6], (N_SECTION, D, D), (max(1, 5 * D // LEN)) ** -0.5, 1.5, ((0, 2), (1, 16)))
    norm_mlp = jnp.clip(1.0 + 0.1 * jax.random.normal(arg_keys[7], (N_SECTION, D), jnp.float32), 0.5, 1.5).astype(jnp.bfloat16)
    w_gate = gaussian(arg_keys[8], (N_SECTION, D, FF), D ** -0.5, 0.15625, ((0, 2), (1, 16)))
    w_up = gaussian(arg_keys[9], (N_SECTION, D, FF), D ** -0.5, 0.15625, ((0, 2), (1, 16)))
    w_down = gaussian(arg_keys[10], (N_SECTION, FF, D), FF ** -0.5, 0.09375, ((0, 2), (1, 16)))
    return {"ends_in": ends_in, "pair_table": pair_table, "norm_attn": norm_attn, "w_query": w_query, "w_key": w_key, "w_value": w_value, "w_out": w_out, "norm_mlp": norm_mlp, "w_gate": w_gate, "w_up": w_up, "w_down": w_down}


NORM_EPS = 1e-05
ROPE_BASE = 100000.0
MASK_FILL = -1e+30

@jax.custom_vjp
def low(v):
    return lax.optimization_barrier(v.astype(jnp.bfloat16)).astype(jnp.float32)

@jax.custom_vjp
def low_back(v):
    return v

def low_keep(v):
    return (low(v), None)

def low_pass(kept, grad):
    return (grad,)

def back_keep(v):
    return (v, None)

def back_low(kept, grad):
    return (low(grad),)
low.defvjp(low_keep, low_pass)
low_back.defvjp(back_keep, back_low)

def rms_norm(inputs, gain_vec):
    return inputs * lax.rsqrt(lax.optimization_barrier(jnp.mean(inputs * inputs, -1, keepdims=True)) + NORM_EPS) * gain_vec

def layout_positions(pair_table, block_rows, ctx_count):
    row_ids = jnp.arange(2 * block_rows * ctx_count, dtype=jnp.int32)
    device_ids = row_ids // (2 * block_rows)
    upper_half = row_ids // block_rows % 2
    offset_in = row_ids % block_rows
    owned_pair = pair_table[device_ids].astype(jnp.int32)
    block_ids = jnp.where(upper_half == 0, owned_pair, 2 * ctx_count - 1 - owned_pair)
    return (block_ids * block_rows + offset_in).astype(jnp.int32)

def rope_tables(positions):
    half_dim = HEAD_DIM // 2
    freq_idx = jnp.arange(half_dim, dtype=jnp.float32)
    inverse = ROPE_BASE ** (-2.0 * freq_idx / HEAD_DIM)
    angles = positions.astype(jnp.float32)[:, None] * inverse[None, :]
    return (jnp.cos(angles), jnp.sin(angles))

def rotate(vectors, cosine_table, sine_table):
    half_dim = vectors.shape[-1] // 2
    first_half = vectors[..., :half_dim]
    second_half = vectors[..., half_dim:]
    cosine = cosine_table[:, None, :]
    sine_part = sine_table[:, None, :]
    return jnp.concatenate([first_half * cosine - second_half * sine_part, second_half * cosine + first_half * sine_part], -1)

def layer_forward(inputs, weights_in, positions, cosine_table, sine_table):
    norm_gain, query_w, key_w, value_w, out_w, gain_two, gate_w, up_w, down_w = weights_in
    highest = lax.Precision.HIGHEST
    group_size = HEADS // KV_HEADS
    normed = low(rms_norm(inputs, norm_gain))
    query_raw = low_back(jnp.dot(normed, query_w, precision=highest)).reshape(LEN, HEADS, HEAD_DIM)
    queries = low(rotate(query_raw, cosine_table, sine_table)).reshape(LEN, KV_HEADS, group_size, HEAD_DIM)
    key_raw = low_back(jnp.dot(normed, key_w, precision=highest)).reshape(LEN, KV_HEADS, HEAD_DIM)
    key_rows = low(rotate(key_raw, cosine_table, sine_table))
    value_rows = low(low_back(jnp.dot(normed, value_w, precision=highest))).reshape(LEN, KV_HEADS, HEAD_DIM)
    query_rows = math.gcd(LEN, 512)
    block_count = LEN // query_rows
    query_blocks = queries.reshape(block_count, query_rows, KV_HEADS, group_size, HEAD_DIM)
    pos_blocks = positions.reshape(block_count, query_rows)

    def score_block(block_in):
        query_block, block_pos = block_in
        scores = jnp.einsum('qkgd,tkd->kgqt', query_block, key_rows, precision=highest) * HEAD_DIM ** (-0.5)
        scores = low_back(scores)
        causal_mask = block_pos[:, None] >= positions[None, :]
        scores = jnp.where(causal_mask, scores, MASK_FILL)
        attn_probs = low(jax.nn.softmax(scores, -1))
        return jnp.einsum('kgqt,tkd->qkgd', attn_probs, value_rows, precision=highest)
    attn_out = lax.map(jax.checkpoint(score_block), (query_blocks, pos_blocks)).reshape(LEN, D)
    attn_out = low(low_back(attn_out))
    mid_stream = inputs + low_back(jnp.dot(attn_out, out_w, precision=highest))
    normed_mid = low(rms_norm(mid_stream, gain_two))
    gate_pre = low_back(jnp.dot(normed_mid, gate_w, precision=highest))
    up_pre = low_back(jnp.dot(normed_mid, up_w, precision=highest))
    hidden = low(jax.nn.silu(gate_pre) * up_pre)
    return mid_stream + low_back(jnp.dot(hidden, down_w, precision=highest))

def reference(ends_in, pair_table, norm_attn, w_query, w_key, w_value, w_out, norm_mlp, w_gate, w_up, w_down):
    positions = layout_positions(pair_table, BLK, N_CTX)
    cosine_table, sine_table = rope_tables(positions)
    seq_count = MB * SEQS
    inputs = ends_in[0].astype(jnp.float32).reshape(seq_count, LEN, D)
    cotangent = ends_in[1].astype(jnp.float32).reshape(seq_count, LEN, D)
    params = tuple((array_in.astype(jnp.float32) for array_in in (norm_attn, w_query, w_key, w_value, w_out, norm_mlp, w_gate, w_up, w_down)))

    def forward(inputs, params):

        def one_sequence(sequence):
            first_out = layer_forward(sequence, tuple((array_in[0] for array_in in params)), positions, cosine_table, sine_table)
            first_out = low_back(low(first_out))
            return layer_forward(first_out, tuple((array_in[1] for array_in in params)), positions, cosine_table, sine_table)
        return lax.map(one_sequence, inputs)
    outputs, pullback = jax.vjp(forward, inputs, params)
    input_grad, param_grads = pullback(cotangent)
    ends_out = jnp.stack([input_grad, outputs]).reshape(2, MB, SEQS, LEN, D).astype(jnp.bfloat16)
    return (ends_out, param_grads[0], param_grads[1], param_grads[2], param_grads[3], param_grads[4], param_grads[5], param_grads[6], param_grads[7], param_grads[8])
```

```python
import jax
import jax.numpy as jnp
from jax import lax
from jax.experimental import pallas as pl
from jax.experimental.pallas import tpu as pltpu
from jax.sharding import PartitionSpec as P

HEADS = 16
KV_HEADS = 8
HEAD_DIM = 96
HALF = HEAD_DIM // 2
LANES = 128
HALF_LANES = LANES // 2

NORM_EPS = 1e-05
ROPE_BASE = 100000.0
MASK_FILL = -1e30

MESH_AXES = ("section", "ctx", "shard")
F32 = jnp.float32
BF16 = jnp.bfloat16


class Layout:
    def __init__(self):
        self.sections = lax.axis_size("section")
        self.ctx = lax.axis_size("ctx")
        self.shards = lax.axis_size("shard")
        self.halves = 2
        self.group = self.ctx // self.halves
        ctx_index = lax.axis_index("ctx")
        self.section_index = lax.axis_index("section")
        self.ctx_index = ctx_index
        self.half = ctx_index // self.group
        self.member = ctx_index % self.group
        self.shard = lax.axis_index("shard")

    def move(self, block, sections, target):
        pairs = []
        for sec in sections:
            for c in range(self.ctx):
                for s in range(self.shards):
                    new_sec, new_c, new_s = target(sec, c, s)
                    pairs.append((self.flat(sec, c, s), self.flat(new_sec, new_c, new_s)))
        return lax.ppermute(block, MESH_AXES, pairs)

    def flat(self, sec, c, s):
        return (sec * self.ctx + c) * self.shards + s

    def to_member(self, block, sections, step):
        return self.move(block, sections, lambda sec, c, s: (sec, c ^ step, s))

    def to_half(self, block, sections):
        return self.move(block, sections, lambda sec, c, s: (sec, c ^ self.group, s))

    def to_shard(self, block, sections):
        return self.move(block, sections, lambda sec, c, s: (sec, c, s ^ 1))

    def to_section(self, block, source):
        pairs = []
        for c in range(self.ctx):
            for s in range(self.shards):
                pairs.append((self.flat(source, c, s), self.flat(1 - source, c, s)))
        return lax.ppermute(block, MESH_AXES, pairs)


def pick(parts, index):
    return lax.dynamic_index_in_dim(parts, index, 0, False)


def split_blocks(weight, lay, unit):
    rows = weight.shape[0]
    parts = weight.reshape(rows, lay.halves, lay.group, unit)
    return parts.transpose(2, 0, 1, 3).reshape(lay.group, rows, lay.halves * unit)


def merge_blocks(parts, lay, unit):
    rows = parts.shape[1]
    parts = parts.reshape(lay.group, rows, lay.halves, unit)
    return parts.transpose(1, 2, 0, 3).reshape(rows, lay.halves * lay.group * unit)


def aligned(lay, block_rows):
    return block_rows == HEAD_DIM and KV_HEADS % lay.group == 0


def split_query(weight, lay):
    if aligned(lay, weight.shape[0]):
        return split_blocks(weight, lay, lay.shards * HEAD_DIM)
    rows = weight.shape[0]
    return weight.reshape(rows, lay.group, -1).transpose(1, 0, 2)


def merge_query(parts, lay):
    rows = parts.shape[1]
    if aligned(lay, rows):
        return merge_blocks(parts, lay, lay.shards * HEAD_DIM)
    return parts.transpose(1, 0, 2).reshape(rows, -1)


def split_key(weight, lay):
    rows = weight.shape[0]
    if aligned(lay, rows):
        return split_blocks(weight, lay, HEAD_DIM)
    copies = max(1, lay.group // KV_HEADS)
    parts = weight.reshape(rows, lay.group // copies, -1).transpose(1, 0, 2)
    return jnp.repeat(parts, copies, axis=0)


def merge_key(parts, lay):
    rows = parts.shape[1]
    if aligned(lay, rows):
        return merge_blocks(parts, lay, HEAD_DIM)
    copies = max(1, lay.group // KV_HEADS)
    parts = jnp.sum(parts.reshape(lay.group // copies, copies, rows, -1), 1)
    return parts.transpose(1, 0, 2).reshape(rows, -1)


def place(own, others, member):
    group = 1 + len(others)
    stacked = jnp.zeros((group,) + own.shape, own.dtype)
    for step, block in enumerate((own,) + tuple(others)):
        stacked = lax.dynamic_update_index_in_dim(stacked, block, member ^ step, 0)
    return stacked


def swap_columns(parts, lay, secs):
    others = [
        lay.to_member(pick(parts, lay.member ^ step), secs, step) for step in range(1, lay.group)
    ]
    return place(pick(parts, lay.member), others, lay.member)


def join_two(own, other, index, axis):
    first = jnp.where(index == 0, own, other)
    second = jnp.where(index == 0, other, own)
    return jnp.stack([first, second], axis)


def spread(block, lay, secs):
    over_half = join_two(block, lay.to_half(block, secs), lay.half, 0)
    return join_two(over_half, lay.to_shard(over_half, secs), lay.shard, 2)


def collect(sums, lay, secs, wire):
    own = lax.dynamic_index_in_dim(sums, lay.shard, 2, False)
    sent = lax.dynamic_index_in_dim(sums, 1 - lay.shard, 2, False).astype(wire)
    own = own + lay.to_shard(sent, secs).astype(F32)
    kept = pick(own, lay.half)
    sent = pick(own, 1 - lay.half).astype(wire)
    return kept + lay.to_half(sent, secs).astype(F32)


def return_columns(parts, lay, secs, wire):
    others = [
        lay.to_member(pick(parts, lay.member ^ step).astype(wire), secs, step).astype(F32)
        for step in range(1, lay.group)
    ]
    return place(pick(parts, lay.member), others, lay.member)


def lane_matrix(heads):
    source = jnp.arange(heads * HEAD_DIM)
    head, offset = source // HEAD_DIM, source % HEAD_DIM
    target = head * LANES + (offset // HALF) * HALF_LANES + offset % HALF
    return (target[:, None] == jnp.arange(heads * LANES)[None, :]).astype(BF16)


def rot(vec, cos_t, sin_t):
    return vec * cos_t + pltpu.roll(vec, HALF_LANES, 1) * sin_t


def rot_back(vec, cos_t, sin_t):
    return vec * cos_t - pltpu.roll(vec, HALF_LANES, 1) * sin_t


def mm(a, b):
    return lax.dot_general(a, b, (((1,), (0,)), ((), ())), preferred_element_type=F32)


def mm_nt(a, b):
    return lax.dot_general(a, b, (((1,), (1,)), ((), ())), preferred_element_type=F32)


def mm_tn(a, b):
    return lax.dot_general(a, b, (((0,), (0,)), ((), ())), preferred_element_type=F32)


def attend_kernel(per_key, q_raw, k_raw, v_raw, cos_t, sin_t, pos_q, pos_k, q_out, k_out, v_out, o_out, lse_out):
    scale = HEAD_DIM ** (-0.5)
    cos_v, sin_v = cos_t[...], sin_t[...]
    key = rot(k_raw[...], cos_v, sin_v).astype(BF16)
    value = v_raw[...].astype(BF16)
    k_out[...] = key
    v_out[...] = value
    mask = pos_q[...] >= pos_k[...]
    for head in range(per_key):
        lanes = slice(head * LANES, (head + 1) * LANES)
        query = rot(q_raw[:, lanes], cos_v, sin_v).astype(BF16)
        q_out[:, lanes] = query
        scores = jnp.where(mask, mm_nt(query, key) * scale, MASK_FILL)
        row_max = jnp.max(scores, -1, keepdims=True)
        weights = jnp.exp(scores - row_max)
        total = jnp.sum(weights, -1, keepdims=True)
        probs = (weights * (1.0 / total)).astype(BF16)
        o_out[:, lanes] = mm(probs, value).astype(BF16)
        lse_out[head] = row_max + jnp.log(total)


def attend(raw, tables, n_query, n_key):
    rows = raw.shape[0]
    per_key = n_query // n_key
    cos_t, sin_t, pos_q, pos_k = tables
    full = lambda g: (0, 0)
    wide = pl.BlockSpec((rows, per_key * LANES), lambda g: (0, g))
    slim = pl.BlockSpec((rows, LANES), lambda g: (0, g))
    return pl.pallas_call(
        lambda *refs: attend_kernel(per_key, *refs),
        grid=(n_key,),
        in_specs=[
            wide,
            pl.BlockSpec((rows, LANES), lambda g: (0, n_query + g)),
            pl.BlockSpec((rows, LANES), lambda g: (0, n_query + n_key + g)),
            pl.BlockSpec((rows, LANES), full),
            pl.BlockSpec((rows, LANES), full),
            pl.BlockSpec((rows, 1), full),
            pl.BlockSpec((1, rows), full),
        ],
        out_specs=[
            wide,
            slim,
            slim,
            wide,
            pl.BlockSpec((per_key, rows, 1), lambda g: (g, 0, 0)),
        ],
        out_shape=[
            jax.ShapeDtypeStruct((rows, n_query * LANES), BF16),
            jax.ShapeDtypeStruct((rows, n_key * LANES), BF16),
            jax.ShapeDtypeStruct((rows, n_key * LANES), BF16),
            jax.ShapeDtypeStruct((rows, n_query * LANES), BF16),
            jax.ShapeDtypeStruct((n_query, rows, 1), F32),
        ],
        compiler_params=pltpu.CompilerParams(vmem_limit_bytes=56 * 1024 * 1024),
        cost_estimate=pl.CostEstimate(
            flops=4 * n_query * rows * rows * LANES,
            bytes_accessed=rows * (n_query + 2 * n_key) * LANES * 8,
            transcendentals=n_query * rows * rows,
        ),
        name="attend",
    )(raw, raw, raw, cos_t, sin_t, pos_q, pos_k)


def attend_back_kernel(per_key, q, k, v, do, lse, cos_t, sin_t, pos_q, pos_k, dq_out, dk_out, dv_out):
    scale = HEAD_DIM ** (-0.5)
    cos_v, sin_v = cos_t[...], sin_t[...]
    key, value = k[...], v[...]
    mask = pos_q[...] >= pos_k[...]
    key_grad = None
    value_grad = None
    for head in range(per_key):
        lanes = slice(head * LANES, (head + 1) * LANES)
        query = q[:, lanes]
        grad = do[:, lanes]
        scores = jnp.where(mask, mm_nt(query, key) * scale, MASK_FILL)
        probs = jnp.exp(scores - lse[head])
        prob_grad = mm_nt(grad, value)
        delta = jnp.sum(probs * prob_grad, -1, keepdims=True)
        score_grad = (probs * (prob_grad - delta)).astype(BF16)
        dq_out[:, lanes] = rot_back(mm(score_grad, key) * scale, cos_v, sin_v).astype(BF16)
        dk = mm_tn(score_grad, query)
        dv = mm_tn(probs.astype(BF16), grad)
        key_grad = dk if key_grad is None else key_grad + dk
        value_grad = dv if value_grad is None else value_grad + dv
    dk_out[...] = rot_back(key_grad * scale, cos_v, sin_v).astype(BF16)
    dv_out[...] = value_grad.astype(BF16)


def attend_back(kept, out_grad, tables, n_query, n_key):
    queries, keys, values, lse = kept
    rows = queries.shape[0]
    per_key = n_query // n_key
    cos_t, sin_t, pos_q, pos_k = tables
    full = lambda g: (0, 0)
    wide = pl.BlockSpec((rows, per_key * LANES), lambda g: (0, g))
    slim = pl.BlockSpec((rows, LANES), lambda g: (0, g))
    return pl.pallas_call(
        lambda *refs: attend_back_kernel(per_key, *refs),
        grid=(n_key,),
        in_specs=[
            wide,
            slim,
            slim,
            wide,
            pl.BlockSpec((per_key, rows, 1), lambda g: (g, 0, 0)),
            pl.BlockSpec((rows, LANES), full),
            pl.BlockSpec((rows, LANES), full),
            pl.BlockSpec((rows, 1), full),
            pl.BlockSpec((1, rows), full),
        ],
        out_specs=[wide, slim, slim],
        out_shape=[
            jax.ShapeDtypeStruct((rows, n_query * LANES), BF16),
            jax.ShapeDtypeStruct((rows, n_key * LANES), BF16),
            jax.ShapeDtypeStruct((rows, n_key * LANES), BF16),
        ],
        compiler_params=pltpu.CompilerParams(vmem_limit_bytes=56 * 1024 * 1024),
        cost_estimate=pl.CostEstimate(
            flops=10 * n_query * rows * rows * LANES,
            bytes_accessed=rows * (n_query + n_key) * LANES * 8,
            transcendentals=n_query * rows * rows,
        ),
        name="attend_back",
    )(queries, keys, values, out_grad, lse, cos_t, sin_t, pos_q, pos_k)


def gather_rows(block, lay, secs):
    others = [lay.to_member(block, secs, step) for step in range(1, lay.group)]
    return jnp.concatenate([block] + others, 0)


def scatter_rows(partial, lay, secs):
    rows = partial.shape[0] // lay.group
    parts = partial.reshape(lay.group, rows, -1)
    total = parts[0]
    for step in range(1, lay.group):
        total = total + lay.to_member(parts[step].astype(BF16), secs, step).astype(F32)
    return total


def norm_forward(inputs, gain_vec):
    inverse_rms = lax.rsqrt(jnp.mean(inputs * inputs, -1, keepdims=True) + NORM_EPS)
    return (inputs * inverse_rms * gain_vec).astype(BF16), inverse_rms


def norm_backward(inputs, inverse_rms, gain_vec, upstream):
    scaled = upstream * gain_vec
    input_grad = inverse_rms * scaled - inputs * inverse_rms**3 * jnp.mean(
        scaled * inputs, -1, keepdims=True
    )
    gain_grad = jnp.sum(upstream * inputs * inverse_rms, 0)
    return input_grad, gain_grad


def layer_forward(inputs, weights, tables, lay, secs):
    gain_one, gain_two, qkv_w, out_w, gate_up_w, down_w, n_query, n_key = weights
    normed_own, inverse_first = norm_forward(inputs, gain_one)
    normed = gather_rows(normed_own, lay, secs)
    raw = jnp.dot(normed, qkv_w, preferred_element_type=F32)
    queries, keys, values, attn_out, lse = attend(raw, tables, n_query, n_key)
    mid_stream = inputs + scatter_rows(
        jnp.dot(attn_out, out_w, preferred_element_type=F32), lay, secs
    )
    mid_own, inverse_second = norm_forward(mid_stream, gain_two)
    normed_mid = gather_rows(mid_own, lay, secs)
    gate_up = jnp.dot(normed_mid, gate_up_w, preferred_element_type=F32)
    ff = gate_up.shape[1] // 2
    gate_pre, up_pre = gate_up[:, :ff], gate_up[:, ff:]
    hidden = (jax.nn.silu(gate_pre) * up_pre).astype(BF16)
    outputs = mid_stream + scatter_rows(
        jnp.dot(hidden, down_w, preferred_element_type=F32), lay, secs
    )
    kept = (
        inputs,
        inverse_first,
        normed,
        (queries, keys, values, lse),
        attn_out,
        mid_stream,
        inverse_second,
        normed_mid,
        gate_pre,
        up_pre,
        hidden,
    )
    return outputs, kept


def layer_backward(out_grad, kept, weights, tables, lay, secs):
    gain_one, gain_two, qkv_w, out_w, gate_up_w, down_w, n_query, n_key = weights
    (
        inputs,
        inverse_first,
        normed,
        attn_kept,
        attn_out,
        mid_stream,
        inverse_second,
        normed_mid,
        gate_pre,
        up_pre,
        hidden,
    ) = kept
    down_in = gather_rows(out_grad.astype(BF16), lay, secs)
    hidden_grad = jnp.einsum("rd,fd->rf", down_in, down_w, preferred_element_type=F32)
    sigmoid_gate = jax.nn.sigmoid(gate_pre)
    gate_grad_in = (
        hidden_grad * up_pre * sigmoid_gate * (1.0 + gate_pre * (1.0 - sigmoid_gate))
    ).astype(BF16)
    up_grad_in = (hidden_grad * gate_pre * sigmoid_gate).astype(BF16)
    gate_up_grad = jnp.concatenate([gate_grad_in, up_grad_in], 1)
    normed_mid_grad = scatter_rows(
        jnp.einsum("rf,df->rd", gate_up_grad, gate_up_w, preferred_element_type=F32), lay, secs
    )
    mid_part, gain_two_grad = norm_backward(mid_stream, inverse_second, gain_two, normed_mid_grad)
    mid_grad = out_grad + mid_part
    mid_low = gather_rows(mid_grad.astype(BF16), lay, secs)
    attn_grad = jnp.einsum("rd,ed->re", mid_low, out_w, preferred_element_type=F32).astype(BF16)
    lows = jnp.concatenate(attend_back(attn_kept, attn_grad, tables, n_query, n_key), 1)
    normed_grad = scatter_rows(
        jnp.einsum("re,de->rd", lows, qkv_w, preferred_element_type=F32), lay, secs
    )
    input_part, gain_one_grad = norm_backward(inputs, inverse_first, gain_one, normed_grad)
    input_grad = mid_grad + input_part
    operands = (hidden, down_in, normed_mid, gate_up_grad, attn_out, mid_low, normed, lows)
    return input_grad, jnp.stack([gain_one_grad, gain_two_grad]), operands


def weight_grads(operands, lay, secs, spread_out, spread_lanes, n_query, n_key):
    hidden, down_in, normed_mid, gate_up_grad, attn_out, mid_low, normed, lows = operands
    halves, group, shards = lay.halves, lay.group, lay.shards
    wire = BF16
    width = normed.shape[1]
    row_block = width // (halves * group * shards)
    down_grad = mm_tn(hidden, down_in)
    down_grad = down_grad.reshape(halves, 1, shards, -1, width)
    down_grad = collect(down_grad, lay, secs, wire)[0]
    gate_up = mm_tn(normed_mid, gate_up_grad).reshape(halves, group, shards, row_block, -1)
    gate_up = return_columns(collect(gate_up, lay, secs, wire), lay, secs, wire)
    ff = gate_up.shape[2] // 2
    unit = ff // halves
    gate_grad = merge_blocks(gate_up[:, :, :ff], lay, unit)
    up_grad = merge_blocks(gate_up[:, :, ff:], lay, unit)
    attn_low = mm_nt(attn_out, spread_out).astype(BF16)
    out_grad = mm_tn(attn_low, mid_low)
    if aligned(lay, row_block):
        out_grad = out_grad.reshape(halves, 1, shards, row_block, width)
        out_grad = collect(out_grad, lay, secs, wire)[0]
    else:
        all_rows = jnp.zeros((lay.group,) + out_grad.shape, F32)
        all_rows = lax.dynamic_update_index_in_dim(all_rows, out_grad, lay.member, 0)
        out_grad = lax.psum_scatter(
            all_rows.reshape(width, width), ("ctx", "shard"), scatter_dimension=0, tiled=True
        )
    low = mm_nt(lows, spread_lanes).astype(BF16)
    qkv = mm_tn(normed, low).reshape(halves, group, shards, row_block, -1)
    qkv = return_columns(collect(qkv, lay, secs, wire), lay, secs, wire)
    q_cols, k_cols = n_query * HEAD_DIM, n_key * HEAD_DIM
    query_grad = merge_query(qkv[:, :, :q_cols], lay)
    key_grad = merge_key(qkv[:, :, q_cols : q_cols + k_cols], lay)
    value_grad = merge_key(qkv[:, :, q_cols + k_cols :], lay)
    return query_grad, key_grad, value_grad, out_grad, gate_grad, up_grad, down_grad


def gain_sums(gains, lay, secs):
    parts = gains.reshape(2, lay.halves, lay.group, lay.shards, -1).transpose(1, 2, 3, 0, 4)
    parts = collect(parts, lay, secs, F32)
    total = pick(parts, lay.member)
    for step in range(1, lay.group):
        total = total + lay.to_member(pick(parts, lay.member ^ step), secs, step)
    return total


def group_tables(pair_table, block_rows, lay, head_dim):
    ctx_ids = []
    for step in range(lay.group):
        for half in range(lay.halves):
            ctx_ids.append((lay.half ^ half) * lay.group + (lay.member ^ step))
    ctx_ids = jnp.stack(ctx_ids)
    owned = jnp.sum(
        jnp.where(ctx_ids[:, None] == jnp.arange(lay.ctx)[None, :], pair_table[None, :], 0), 1
    )
    blocks = jnp.stack([owned, 2 * lay.ctx - 1 - owned], 1)
    positions = (blocks[:, :, None] * block_rows + jnp.arange(block_rows)[None, None, :]).reshape(-1)
    freq_idx = jnp.arange(HALF, dtype=F32)
    inverse = ROPE_BASE ** (-2.0 * freq_idx / head_dim)
    angles = positions.astype(F32)[:, None] * inverse[None, :]
    pad = ((0, 0), (0, HALF_LANES - HALF))
    cos_h, sin_h = jnp.pad(jnp.cos(angles), pad), jnp.pad(jnp.sin(angles), pad)
    cos_t = jnp.concatenate([cos_h, cos_h], 1)
    sin_t = jnp.concatenate([-sin_h, sin_h], 1)
    return cos_t, sin_t, positions[:, None], positions[None, :]


def body(
    ends_in, pair_table, norm_attn, w_query, w_key, w_value, w_out, norm_mlp, w_gate, w_up, w_down
):
    lay = Layout()
    both = tuple(range(lay.sections))
    is_first = lay.section_index == 0
    rows = ends_in.shape[3]
    width = ends_in.shape[4]
    row_block = w_query.shape[1]
    n_query = HEADS // lay.group
    n_key = max(1, KV_HEADS // lay.group)
    tables = group_tables(pair_table, rows // 2, lay, HEAD_DIM)

    local = ends_in[0, :, 0]
    local = jnp.concatenate(
        [pick(local, lay.half), lay.to_half(pick(local, 1 - lay.half), both)], 0
    )

    gains = jnp.stack([norm_attn[0], norm_mlp[0]])
    gains = place(
        gains, [lay.to_member(gains, both, step) for step in range(1, lay.group)], lay.member
    )
    gains = spread(gains, lay, both)
    gains = gains.transpose(3, 0, 1, 2, 4).reshape(2, width).astype(F32)

    qkv_parts = jnp.concatenate(
        [split_query(w_query[0], lay), split_key(w_key[0], lay), split_key(w_value[0], lay)], 2
    )
    ff_unit = lay.shards * w_down.shape[1]
    gate_up_parts = jnp.concatenate(
        [split_blocks(w_gate[0], lay, ff_unit), split_blocks(w_up[0], lay, ff_unit)], 2
    )
    spread_lanes = lane_matrix(n_query + 2 * n_key)
    spread_out = lane_matrix(n_query)

    def fetch(secs):
        qkv = spread(swap_columns(qkv_parts, lay, secs), lay, secs)
        if aligned(lay, row_block):
            out_w = spread(w_out, lay, secs).reshape(-1, width)
        else:
            out_w = lax.all_gather(w_out[0], ("ctx", "shard"), axis=0, tiled=True)
            out_w = pick(out_w.reshape(lay.group, -1, width), lay.member)
        gate_up = spread(swap_columns(gate_up_parts, lay, secs), lay, secs)
        down_w = spread(w_down, lay, secs)
        return qkv, out_w, gate_up, down_w

    fetched = [fetch((sec,)) for sec in both]
    qkv_w, out_w, gate_up_w, down_w = jax.tree.map(
        lambda a, b: jnp.where(is_first, a, b), fetched[0], fetched[1]
    )
    qkv_w = mm(qkv_w.reshape(width, -1), spread_lanes).astype(BF16)
    out_w = mm_tn(spread_out, out_w).astype(BF16)
    gate_up_w = gate_up_w.reshape(width, -1)
    down_w = down_w.reshape(-1, width)
    weights = (gains[0], gains[1], qkv_w, out_w, gate_up_w, down_w, n_query, n_key)

    first_out, first_kept = layer_forward(local.astype(F32), weights, tables, lay, (0,))
    second_in = lay.to_section(first_out.astype(BF16), 0).astype(F32)
    second_out, second_kept = layer_forward(second_in, weights, tables, lay, (1,))
    second_grad, second_gains, second_ops = layer_backward(
        local.astype(F32), second_kept, weights, tables, lay, (1,)
    )
    second_w = weight_grads(second_ops, lay, (1,), spread_out, spread_lanes, n_query, n_key)
    second_g = gain_sums(second_gains, lay, (1,))
    first_in = lay.to_section(second_grad.astype(BF16), 1).astype(F32)
    first_grad, first_gains, first_ops = layer_backward(
        first_in, first_kept, weights, tables, lay, (0,)
    )
    first_w = weight_grads(first_ops, lay, (0,), spread_out, spread_lanes, n_query, n_key)
    first_g = gain_sums(first_gains, lay, (0,))

    ends = jnp.where(is_first, first_grad.astype(BF16), second_out.astype(BF16))
    ends = ends.reshape(2, rows, width)
    other = lay.to_half(ends[1], both)
    ends = join_two(ends[0], other, lay.half, 0)[None, :, None]
    query_g, key_g, value_g, out_g, gate_g, up_g, down_g = (
        jnp.where(is_first, a, b)[None] for a, b in zip(first_w, second_w)
    )
    gain_g = jnp.where(is_first, first_g, second_g)
    return (
        ends,
        gain_g[0][None],
        query_g,
        key_g,
        value_g,
        out_g,
        gain_g[1][None],
        gate_g,
        up_g,
        down_g,
    )


def solution(mesh):
    rows = P("section", None, "shard", "ctx", None)
    vector = P("section", ("ctx", "shard"))
    matrix = P("section", ("ctx", "shard"), None)
    return jax.shard_map(
        body,
        mesh=mesh,
        in_specs=(rows, P(), vector, matrix, matrix, matrix, matrix, vector, matrix, matrix, matrix),
        out_specs=(rows, vector, matrix, matrix, matrix, matrix, vector, matrix, matrix, matrix),
        check_vma=False,
    )
```

```python
import jax
import jax.numpy as jnp
from jax import lax
from jax.experimental import pallas as pl
from jax.experimental.pallas import tpu as pltpu
from jax.sharding import PartitionSpec as P

HEADS = 16
KV_HEADS = 8
HEAD_DIM = 96
HALF = HEAD_DIM // 2
LANES = 128
HALF_LANES = LANES // 2

NORM_EPS = 1e-05
ROPE_BASE = 100000.0
MASK_FILL = -1e30

MESH_AXES = ("section", "ctx", "shard")
F32 = jnp.float32
BF16 = jnp.bfloat16
VMEM_LIMIT = pltpu.CompilerParams(vmem_limit_bytes=56 * 1024 * 1024)


class Layout:
    def __init__(self):
        self.cores = lax.axis_size("section")
        self.ctx = lax.axis_size("ctx")
        self.shards = lax.axis_size("shard")
        self.halves = 2
        self.group = self.ctx // self.halves
        ctx_index = lax.axis_index("ctx")
        self.core = lax.axis_index("section")
        self.half = ctx_index // self.group
        self.member = ctx_index % self.group
        self.shard = lax.axis_index("shard")

    def move(self, block, target):
        pairs = []
        for core in range(self.cores):
            for half in range(self.halves):
                for member in range(self.group):
                    for shard in range(self.shards):
                        to = target(core, half, member, shard)
                        pairs.append((self.flat(core, half, member, shard), self.flat(*to)))
        return lax.ppermute(block, MESH_AXES, pairs)

    def move_some(self, block, sends, target):
        pairs = []
        for core in range(self.cores):
            for half in range(self.halves):
                for member in range(self.group):
                    for shard in range(self.shards):
                        if sends(core, half, member, shard):
                            to = target(core, half, member, shard)
                            pairs.append((self.flat(core, half, member, shard), self.flat(*to)))
        return lax.ppermute(block, MESH_AXES, pairs)

    def flat(self, core, half, member, shard):
        return (core * self.ctx + half * self.group + member) * self.shards + shard

    def to_member(self, block, step):
        return self.move(block, lambda core, half, member, shard: (core, half, member ^ step, shard))

    def to_half(self, block):
        return self.move(block, lambda core, half, member, shard: (core, 1 - half, member, shard))

    def to_shard(self, block):
        return self.move(block, lambda core, half, member, shard: (core, half, member, 1 - shard))

    def to_core(self, block):
        return self.move(block, lambda core, half, member, shard: (1 - core, half, member, shard))


def pick(parts, index):
    return lax.dynamic_index_in_dim(parts, index, 0, False)


def after(block, *earlier):
    return lax.optimization_barrier((block,) + earlier)[0] if earlier else block


class Wire:
    def __init__(self, move):
        self.move = move
        self.last = ()

    def send(self, block, deps=(), move=None, beside=False):
        block = after(block, *(() if beside else self.last), *deps)
        got = (move or self.move)(block)
        self.last = self.last + (got,) if beside else (got,)
        return got, block


def two_way(index, own, other, axis):
    first = jnp.where(index == 0, own, other)
    second = jnp.where(index == 0, other, own)
    return jnp.stack([first, second], axis)


def rearrange_kernel(plans, count, *refs):
    sources, outs = refs[:count], refs[count:]
    for out, plan in zip(outs, plans):
        for index, pieces in plan:
            blocks = [
                sources[source][place + (slice(None), slice(column, column + width))]
                for source, place, column, width in pieces
            ]
            out[index] = jnp.concatenate(blocks, 1) if len(blocks) > 1 else blocks[0]


def rearrange(sources, shapes, plans):
    dtype = sources[0].dtype
    moved = sum(source.size for source in sources) * dtype.itemsize
    return pl.pallas_call(
        lambda *refs: rearrange_kernel(plans, len(sources), *refs),
        out_shape=[jax.ShapeDtypeStruct(shape, dtype) for shape in shapes],
        compiler_params=VMEM_LIMIT,
        cost_estimate=pl.CostEstimate(flops=0, bytes_accessed=2 * moved, transcendentals=0),
        name="rearrange",
    )(*sources)


def kernel_width(width):
    return width % HEAD_DIM == 0 or width % LANES == 0


def to_inner(block, lay, inner=True):
    blocks = lay.shards * lay.halves * lay.group
    width = block.shape[-1] // blocks
    outer_order = [
        ((half * lay.group + member) * lay.shards + shard) * width
        for shard in range(lay.shards)
        for half in range(lay.halves)
        for member in range(lay.group)
    ]
    if kernel_width(width):
        columns = outer_order
        if not inner:
            columns = [outer_order.index(i * width) * width for i in range(blocks)]
        flat = block.reshape(-1, block.shape[-1])
        plan = [((slice(None), slice(None)), [(0, (), column, width) for column in columns])]
        return rearrange([flat], [flat.shape], [plan])[0].reshape(block.shape)
    if inner:
        parts = block.reshape(block.shape[:-1] + (lay.halves, lay.group, lay.shards, -1))
        return jnp.moveaxis(parts, -2, -4).reshape(block.shape)
    parts = block.reshape(block.shape[:-1] + (lay.shards, lay.halves, lay.group, -1))
    return jnp.moveaxis(parts, -4, -2).reshape(block.shape)


def to_outer(block, lay):
    return to_inner(block, lay, False)


def relative(block, lay):
    width = block.shape[-1] // 4
    parts = [block[..., i * width : (i + 1) * width] for i in range(4)]
    parts = [jnp.where(lay.half == 0, parts[i], parts[i ^ 1]) for i in range(4)]
    parts = [jnp.where(lay.shard == 0, parts[i], parts[i ^ 2]) for i in range(4)]
    return jnp.concatenate(parts, -1)


def head_copies(lay):
    return max(1, lay.cores * lay.group // HEADS)


def split_heads(weight, lay, heads):
    rows = weight.shape[0]
    pairs = lay.cores * lay.group
    distinct = min(pairs, heads)
    parts = weight.reshape(rows, distinct, -1).transpose(1, 0, 2)
    parts = jnp.repeat(parts, pairs // distinct, axis=0) if pairs > distinct else parts
    return parts.reshape((lay.cores, lay.group) + parts.shape[1:])


def merge_heads(parts, lay, heads):
    pairs = lay.cores * lay.group
    distinct = min(pairs, heads)
    rows = parts.shape[2]
    parts = parts.reshape(distinct, pairs // distinct, rows, -1)
    parts = jnp.sum(parts, 1) if pairs > distinct else parts[:, 0]
    return parts.transpose(1, 0, 2).reshape(rows, -1)


def split_ff(weight, lay, unit):
    rows = weight.shape[0]
    parts = weight.reshape(rows, lay.halves, lay.group, lay.shards, lay.cores, unit)
    return parts.transpose(4, 2, 0, 3, 1, 5).reshape(lay.cores, lay.group, rows, -1)


def merge_ff(parts, lay, unit):
    rows = parts.shape[2]
    parts = parts.reshape(lay.cores, lay.group, rows, lay.shards, lay.halves, unit)
    return parts.transpose(2, 4, 1, 3, 0, 5).reshape(rows, -1)


def pack_heads(query, key, value, lay):
    pairs = lay.cores * lay.group
    if pairs != KV_HEADS or query.shape[0] % 16:
        sides = [(query, HEADS), (key, KV_HEADS), (value, KV_HEADS)]
        return jnp.concatenate([split_heads(block, lay, heads) for block, heads in sides], -1)
    wide, slim = query.shape[1] // pairs, key.shape[1] // pairs
    plan = []
    for pair in range(pairs):
        pieces = [(0, (), pair * wide, wide), (1, (), pair * slim, slim), (2, (), pair * slim, slim)]
        plan.append(((pair // lay.group, pair % lay.group), pieces))
    shape = (lay.cores, lay.group, query.shape[0], wide + 2 * slim)
    return rearrange([query, key, value], [shape], [plan])[0]


def unpack_heads(parts, lay):
    pairs = lay.cores * lay.group
    q_cols = max(1, HEADS // pairs) * HEAD_DIM
    k_cols = max(1, KV_HEADS // pairs) * HEAD_DIM
    if pairs != KV_HEADS:
        sides = [(0, q_cols, HEADS), (q_cols, k_cols, KV_HEADS), (q_cols + k_cols, k_cols, KV_HEADS)]
        return [merge_heads(parts[..., at : at + cols], lay, heads) for at, cols, heads in sides]
    rows = parts.shape[2]
    plans, shapes = [], []
    for first, cols in ((0, q_cols), (q_cols, k_cols), (q_cols + k_cols, k_cols)):
        pieces = [(0, (pair // lay.group, pair % lay.group), first, cols) for pair in range(pairs)]
        plans.append([((slice(None), slice(None)), pieces)])
        shapes.append((rows, pairs * cols))
    return rearrange([parts], shapes, plans)


def ff_columns(lay, core, member, unit):
    for shard in range(lay.shards):
        for half in range(lay.halves):
            block = (half * lay.group + member) * lay.shards + shard
            yield (block * lay.cores + core) * unit, shard * lay.halves + half


def pack_ff(gate, up, lay, unit):
    if not kernel_width(unit):
        return jnp.concatenate([split_ff(gate, lay, unit), split_ff(up, lay, unit)], -1)
    plan = []
    for core in range(lay.cores):
        for member in range(lay.group):
            columns = [column for column, _ in ff_columns(lay, core, member, unit)]
            pieces = [(side, (), column, unit) for side in (0, 1) for column in columns]
            plan.append(((core, member), pieces))
    shape = (lay.cores, lay.group, gate.shape[0], 8 * unit)
    return rearrange([gate, up], [shape], [plan])[0]


def unpack_ff(parts, lay, unit):
    ff = 4 * unit
    if not kernel_width(unit):
        return [merge_ff(parts[..., :ff], lay, unit), merge_ff(parts[..., ff:], lay, unit)]
    rows = parts.shape[2]
    plans = []
    for side in (0, 1):
        found = {}
        for core in range(lay.cores):
            for member in range(lay.group):
                for column, place in ff_columns(lay, core, member, unit):
                    found[column] = (0, (core, member), side * ff + place * unit, unit)
        pieces = [found[column] for column in sorted(found)]
        plans.append([((slice(None), slice(None)), pieces)])
    return rearrange([parts], [(rows, len(found) * unit)] * 2, plans)


def place(own, others, member):
    group = 1 + len(others)
    stacked = jnp.zeros((group,) + own.shape, own.dtype)
    for step, block in enumerate((own,) + tuple(others)):
        stacked = lax.dynamic_update_index_in_dim(stacked, block, member ^ step, 0)
    return stacked


def split_cores(parts, lay, deps=()):
    kept = pick(parts, lay.core)
    other = lay.to_core(after(pick(parts, 1 - lay.core), *deps))
    return jnp.where(lay.core == 0, kept, other), jnp.where(lay.core == 0, other, kept)


def swap_columns(parts, lay, deps=()):
    sent = [after(pick(parts, lay.member ^ step), *deps) for step in range(1, lay.group)]
    others = [lay.to_member(block, step) for step, block in enumerate(sent, 1)]
    placed = place(pick(parts, lay.member), others, lay.member)
    return placed.reshape(-1, parts.shape[-1]), sent[-1]


class Spread:
    def __init__(self, block):
        self.block = block

    def over_half(self, wire, deps=()):
        self.got, sent = wire.send(self.block, deps)
        return sent

    def over_shard(self, wire, deps=()):
        self.pair = jnp.concatenate([self.block, after(self.got, *deps)], 0)
        self.got, sent = wire.send(self.pair)
        return sent

    def full(self):
        return jnp.concatenate([self.pair, self.got], 0)


class Collect:
    def __init__(self, left, right):
        self.left, self.right = left, right
        self.rows = left.shape[1] // 4

    def over_shard(self, wire, deps=(), **how):
        block = mm_tn(self.left[:, 2 * self.rows :], self.right).astype(BF16)
        self.got, sent = wire.send(block, deps, **how)
        return sent

    def over_half(self, wire, deps=(), **how):
        rows = self.rows
        kept = mm_tn(self.left[:, : 2 * rows], self.right)
        got = after(self.got, *deps).astype(F32)
        self.kept = kept[:rows] + got[:rows]
        self.arrived, sent = wire.send((kept[rows:] + got[rows:]).astype(BF16), **how)
        return sent

    def total(self, deps=()):
        return self.kept + after(self.arrived, *deps).astype(F32)


def return_columns(parts, lay, deps):
    others = [
        lay.to_member(after(pick(parts, lay.member ^ step).astype(BF16), *deps), step)
        for step in range(1, lay.group)
    ]
    placed = place(pick(parts, lay.member), [block.astype(F32) for block in others], lay.member)
    return placed, others


def join_cores(first, second, lay):
    kept = jnp.where(lay.core == 0, first, second)
    sent = jnp.where(lay.core == 0, second, first).astype(BF16)
    return two_way(lay.core, kept, lay.to_core(sent).astype(F32), 0)


def out_aligned(lay, block_rows):
    return block_rows == HEAD_DIM and lay.cores * lay.group == KV_HEADS and lay.cores == lay.halves


class SpreadOut:
    def __init__(self, w_out, lay, deps):
        self.lay, self.width = lay, w_out.shape[-1]
        self.aligned = out_aligned(lay, w_out.shape[0])
        if not self.aligned:
            w_out = lax.all_gather(w_out, ("ctx", "shard"), axis=0, tiled=True)
        w_out = after(w_out, *deps)
        other = lay.to_core(w_out)
        layers = [jnp.where(lay.core == 0, w_out, other), jnp.where(lay.core == 0, other, w_out)]
        self.block = jnp.stack(layers)

    def over_half(self, wire, deps=()):
        lay = self.lay
        if not self.aligned:
            return self.block
        move = lambda block: lay.move_some(
            block,
            lambda core, half, member, shard: half == core,
            lambda core, half, member, shard: (core, 1 - half, member, shard),
        )
        self.got, sent = wire.send(self.block, deps, move)
        return sent

    def over_shard(self, wire, deps=()):
        lay = self.lay
        if not self.aligned:
            return self.block
        self.block = jnp.where(lay.half == lay.core, self.block, after(self.got, *deps))
        self.got, sent = wire.send(self.block)
        return sent

    def full(self):
        if self.aligned:
            return jnp.concatenate([self.block, self.got], 1)
        head = (self.lay.core * self.lay.group + self.lay.member) // head_copies(self.lay)
        count = max(1, HEADS // (self.lay.cores * self.lay.group)) * HEAD_DIM
        return lax.dynamic_slice_in_dim(self.block, head * count, count, 1)


class CollectOut:
    def __init__(self, left, right, lay, block_rows):
        self.left, self.right, self.lay = left, right, lay
        self.aligned = out_aligned(lay, block_rows)
        self.rows = left.shape[1] // 2

    def over_shard(self, wire, deps=(), **how):
        if not self.aligned:
            self.kept = mm_tn(self.left, self.right)
            return self.kept
        block = mm_tn(self.left[:, self.rows :], self.right).astype(BF16)
        self.got, sent = wire.send(block, deps, **how)
        return sent

    def over_half(self, wire, deps=(), **how):
        lay = self.lay
        if not self.aligned:
            return self.kept
        self.kept = mm_tn(self.left[:, : self.rows], self.right) + after(self.got, *deps).astype(F32)
        move = lambda block: lay.move_some(
            block,
            lambda core, half, member, shard: half != core,
            lambda core, half, member, shard: (core, 1 - half, member, shard),
        )
        self.arrived, sent = wire.send(self.kept.astype(BF16), (), move, **how)
        return sent

    def total(self, deps=()):
        return self.kept + after(self.arrived, *deps).astype(F32) if self.aligned else self.kept


def join_out(first, second, lay, block_rows):
    if not out_aligned(lay, block_rows):
        width = first.shape[1]
        head = (lay.core * lay.group + lay.member) // head_copies(lay)
        full = jnp.zeros((2, HEADS * HEAD_DIM, width), F32)
        full = lax.dynamic_update_slice_in_dim(
            full, jnp.stack([first, second]), head * first.shape[0], 1
        )
        full = pick(lax.psum(full, MESH_AXES), lay.core)
        block = (lay.half * lay.group + lay.member) * lay.shards + lay.shard
        return lax.dynamic_slice_in_dim(full, block * block_rows, block_rows, 0)
    kept = jnp.where(lay.core == 0, first, second)
    sent = jnp.where(lay.core == 0, second, first).astype(BF16)
    other = lay.to_core(sent).astype(F32)
    return jnp.where(lay.half == lay.core, kept, other)


def lane_matrix(heads):
    source = jnp.arange(heads * HEAD_DIM)
    head, offset = source // HEAD_DIM, source % HEAD_DIM
    target = head * LANES + (offset // HALF) * HALF_LANES + offset % HALF
    return (target[:, None] == jnp.arange(heads * LANES)[None, :]).astype(BF16)


def rot(vec, cos_t, sin_t):
    return vec * cos_t + pltpu.roll(vec, HALF_LANES, 1) * sin_t


def rot_back(vec, cos_t, sin_t):
    return vec * cos_t - pltpu.roll(vec, HALF_LANES, 1) * sin_t


def mm(a, b):
    return lax.dot_general(a, b, (((1,), (0,)), ((), ())), preferred_element_type=F32)


def mm_nt(a, b):
    return lax.dot_general(a, b, (((1,), (1,)), ((), ())), preferred_element_type=F32)


def mm_tn(a, b):
    return lax.dot_general(a, b, (((0,), (0,)), ((), ())), preferred_element_type=F32)


def heads_of(block, count):
    return jnp.concatenate([block[:, i * LANES : (i + 1) * LANES] for i in range(count)], 0)


def project_kernel(n_query, n_key, x, w, cos_t, sin_t, out):
    cos_v, sin_v = cos_t[...], sin_t[...]
    xv = x[...]
    step = 2 * LANES
    for first in range(0, out.shape[1], step):
        raw = mm(xv, w[:, first : first + step])
        for lane in range(first, first + step, LANES):
            block = raw[:, lane - first : lane - first + LANES]
            if lane < (n_query + n_key) * LANES:
                block = rot(block, cos_v, sin_v)
            out[:, lane : lane + LANES] = block.astype(BF16)


def project(normed, qkv_w, cos_t, sin_t, n_query, n_key):
    rows = normed.shape[0]
    if (n_query + 2 * n_key) % 2:
        qkv_w = jnp.pad(qkv_w, ((0, 0), (0, LANES)))
    out = pl.pallas_call(
        lambda *refs: project_kernel(n_query, n_key, *refs),
        out_shape=jax.ShapeDtypeStruct((rows, qkv_w.shape[1]), BF16),
        compiler_params=VMEM_LIMIT,
        cost_estimate=pl.CostEstimate(
            flops=2 * rows * qkv_w.shape[0] * qkv_w.shape[1],
            bytes_accessed=2 * qkv_w.shape[0] * qkv_w.shape[1],
            transcendentals=0,
        ),
        name="project",
    )(normed, qkv_w, cos_t, sin_t)
    return out[:, : (n_query + 2 * n_key) * LANES]


def lanes_of(index, count=1):
    return slice(index * LANES, (index + count) * LANES)


def attend_kernel(n_query, n_key, own, sib, pos_q, pos_k, out_own, out_sib, lse_out):
    scale = HEAD_DIM ** (-0.5)
    per_key = n_query // n_key
    half = own.shape[0]
    rows = 2 * half
    mask = pos_q[...] >= pos_k[...]
    mask = jnp.concatenate([mask] * per_key, 0)
    for kv_head in range(n_key):
        both = lambda index: jnp.concatenate([own[:, lanes_of(index)], sib[:, lanes_of(index)]], 0)
        key, value = both(n_query + kv_head), both(n_query + n_key + kv_head)
        q_first = kv_head * per_key
        query = jnp.concatenate([both(q_first + i) for i in range(per_key)], 0)
        scores = jnp.where(mask, mm_nt(query, key) * scale, MASK_FILL)
        row_max = jnp.max(scores, -1, keepdims=True)
        weights = jnp.exp(scores - row_max)
        total = jnp.sum(weights, -1, keepdims=True)
        probs = (weights * (1.0 / total)).astype(BF16)
        out = mm(probs, value).astype(BF16)
        for i in range(per_key):
            out_own[:, lanes_of(q_first + i)] = out[i * rows : i * rows + half]
            out_sib[:, lanes_of(q_first + i)] = out[i * rows + half : (i + 1) * rows]
        lse_out[kv_head] = row_max + jnp.log(total)


def attend(own, sib, pos_q, pos_k, n_query, n_key):
    half = own.shape[0]
    return pl.pallas_call(
        lambda *refs: attend_kernel(n_query, n_key, *refs),
        out_shape=[
            jax.ShapeDtypeStruct((half, n_query * LANES), BF16),
            jax.ShapeDtypeStruct((half, n_query * LANES), BF16),
            jax.ShapeDtypeStruct((n_key, n_query // n_key * 2 * half, 1), F32),
        ],
        compiler_params=VMEM_LIMIT,
        cost_estimate=pl.CostEstimate(
            flops=16 * n_query * half * half * LANES,
            bytes_accessed=half * n_query * LANES * 8,
            transcendentals=4 * n_query * half * half,
        ),
        name="attend",
    )(own, sib, pos_q, pos_k)


def attend_back_kernel(
    n_query, n_key, own, sib, do_own, do_sib, lse, cos_t, sin_t, pos_q, pos_k, low_own, low_sib
):
    scale = HEAD_DIM ** (-0.5)
    per_key = n_query // n_key
    half = own.shape[0]
    rows = 2 * half
    cos_v, sin_v = cos_t[...], sin_t[...]
    mask = pos_q[...] >= pos_k[...]
    mask = jnp.concatenate([mask] * per_key, 0)

    def put(index, block):
        low_own[:, lanes_of(index)] = block[:half].astype(BF16)
        low_sib[:, lanes_of(index)] = block[half:].astype(BF16)

    def both(a, b, index):
        return jnp.concatenate([a[:, lanes_of(index)], b[:, lanes_of(index)]], 0)

    for kv_head in range(n_key):
        key, value = both(own, sib, n_query + kv_head), both(own, sib, n_query + n_key + kv_head)
        q_first = kv_head * per_key
        query = jnp.concatenate([both(own, sib, q_first + i) for i in range(per_key)], 0)
        grad = jnp.concatenate([both(do_own, do_sib, q_first + i) for i in range(per_key)], 0)
        scores = jnp.where(mask, mm_nt(query, key) * scale, MASK_FILL)
        probs = jnp.exp(scores - lse[kv_head])
        prob_grad = mm_nt(grad, value)
        delta = jnp.sum(probs * prob_grad, -1, keepdims=True)
        score_grad = (probs * (prob_grad - delta)).astype(BF16)
        dq = mm(score_grad, key) * scale
        for i in range(per_key):
            put(q_first + i, rot_back(dq[i * rows : (i + 1) * rows], cos_v, sin_v))
        put(n_query + kv_head, rot_back(mm_tn(score_grad, query) * scale, cos_v, sin_v))
        put(n_query + n_key + kv_head, mm_tn(probs.astype(BF16), grad))


def attend_back(kept, out_grads, tables, n_query, n_key):
    own, sib, lse = kept
    half, lanes = own.shape
    return pl.pallas_call(
        lambda *refs: attend_back_kernel(n_query, n_key, *refs),
        out_shape=[
            jax.ShapeDtypeStruct((half, lanes), BF16),
            jax.ShapeDtypeStruct((half, lanes), BF16),
        ],
        compiler_params=VMEM_LIMIT,
        cost_estimate=pl.CostEstimate(
            flops=40 * n_query * half * half * LANES,
            bytes_accessed=half * lanes * 16,
            transcendentals=4 * n_query * half * half,
        ),
        name="attend_back",
    )(own, sib, *out_grads, lse, *tables)


def no_round(first):
    return ()


def gather_rows(block, lay, meanwhile=no_round):
    others = [lay.to_member(block, step) for step in range(1, lay.group)]
    own = after(jnp.concatenate([block] + others, 0), *meanwhile(others))
    return own, lay.to_core(own)


def scatter_rows(own, sib, lay, meanwhile=no_round):
    own = own + lay.to_core(sib.astype(BF16)).astype(F32)
    rows = own.shape[0] // lay.group
    parts = own.reshape(lay.group, rows, -1)
    others = [lay.to_member(parts[step].astype(BF16), step) for step in range(1, lay.group)]
    total = parts[0]
    for block in others:
        total = total + block.astype(F32)
    return after(total, *meanwhile(others))


def norm_forward(inputs, gain_vec):
    inverse_rms = lax.rsqrt(jnp.mean(inputs * inputs, -1, keepdims=True) + NORM_EPS)
    return (inputs * inverse_rms * gain_vec).astype(BF16), inverse_rms


def norm_backward(inputs, inverse_rms, gain_vec, upstream):
    scaled = upstream * gain_vec
    input_grad = inverse_rms * scaled - inputs * inverse_rms**3 * jnp.mean(
        scaled * inputs, -1, keepdims=True
    )
    gain_grad = jnp.sum(upstream * inputs * inverse_rms, 0)
    return input_grad, gain_grad


def out_order(block, lay, n_query):
    if head_copies(lay) > 1:
        share = (lay.core * lay.group + lay.member) % head_copies(lay) == 0
        return jnp.where(share, block, jnp.zeros_like(block))
    if n_query != 2 or lay.cores * lay.group != KV_HEADS:
        return block
    swapped = jnp.concatenate([block[:, LANES:], block[:, :LANES]], 1)
    return jnp.where(lay.shard == 0, block, swapped)


class Layer:
    def __init__(self, lay, tables, n_query, n_key, gain_one, gain_two, qkv_w, out_w):
        self.lay, self.tables, self.n_query, self.n_key = lay, tables, n_query, n_key
        self.gain_one, self.gain_two = gain_one, gain_two
        self.qkv_w, self.out_w = qkv_w, out_w

    def start(self, inputs, meanwhile=no_round):
        self.inputs = inputs
        normed, self.inverse_first = norm_forward(inputs, self.gain_one)
        self.normed = gather_rows(relative(normed, self.lay), self.lay, meanwhile)

    def attention(self, during_out=no_round, during_rows=no_round):
        lay = self.lay
        cos_own, sin_own, cos_sib, sin_sib, pos_q, pos_k = self.tables
        heads = self.n_query, self.n_key
        own = project(self.normed[0], self.qkv_w, cos_own, sin_own, *heads)
        sib = project(self.normed[1], self.qkv_w, cos_sib, sin_sib, *heads)
        out_own, out_sib, lse = attend(own, sib, pos_q, pos_k, *heads)
        self.attn_kept = own, sib, lse
        self.attn_out = [out_order(block, lay, self.n_query) for block in (out_own, out_sib)]
        partial = [mm(block, self.out_w) for block in self.attn_out]
        self.mid_stream = self.inputs + scatter_rows(*partial, lay, during_out)
        normed, self.inverse_second = norm_forward(self.mid_stream, self.gain_two)
        self.normed_mid = gather_rows(relative(normed, lay), lay, during_rows)

    def hide(self):
        lay = self.lay
        self.gate_up, self.hidden = [], []
        for block in self.normed_mid:
            pre = mm(block, self.gate_up_w)
            ff = pre.shape[1] // 2
            gate_pre, up_pre = pre[:, :ff], pre[:, ff:]
            self.gate_up.append((gate_pre, up_pre))
            self.hidden.append(relative((jax.nn.silu(gate_pre) * up_pre).astype(BF16), lay))

    def feed_forward(self, meanwhile=no_round):
        lay = self.lay
        partial = [mm(block, self.down_w) for block in self.hidden]
        return self.mid_stream + scatter_rows(*partial, lay, meanwhile)

    def start_back(self, out_grad, meanwhile=no_round):
        self.out_grad = out_grad
        self.down_in = gather_rows(out_grad.astype(BF16), self.lay, meanwhile)

    def feed_forward_back(self):
        self.gate_up_grad, partial = [], []
        for block, (gate_pre, up_pre) in zip(self.down_in, self.gate_up):
            hidden_grad = relative(mm_nt(block, self.down_w), self.lay)
            sigmoid_gate = jax.nn.sigmoid(gate_pre)
            gate_grad_in = (
                hidden_grad * up_pre * sigmoid_gate * (1.0 + gate_pre * (1.0 - sigmoid_gate))
            ).astype(BF16)
            up_grad_in = (hidden_grad * gate_pre * sigmoid_gate).astype(BF16)
            both = jnp.concatenate([gate_grad_in, up_grad_in], 1)
            self.gate_up_grad.append(both)
            partial.append(mm_nt(both, self.gate_up_w))
        return partial

    def middle_back(self, partial, during_sum=no_round, during_rows=no_round):
        lay = self.lay
        normed_mid_grad = relative(scatter_rows(*partial, lay, during_sum), lay)
        mid_part, self.gain_two_grad = norm_backward(
            self.mid_stream, self.inverse_second, self.gain_two, normed_mid_grad
        )
        self.mid_grad = self.out_grad + mid_part
        self.mid_low = gather_rows(self.mid_grad.astype(BF16), lay, during_rows)

    def attention_back(self):
        cos_own, sin_own, cos_sib, sin_sib, pos_q, pos_k = self.tables
        grads = [
            out_order(mm_nt(block, self.out_w).astype(BF16), self.lay, self.n_query)
            for block in self.mid_low
        ]
        cos_t, sin_t = jnp.concatenate([cos_own, cos_sib]), jnp.concatenate([sin_own, sin_sib])
        tables = cos_t, sin_t, pos_q, pos_k
        self.lows = attend_back(self.attn_kept, grads, tables, self.n_query, self.n_key)
        return [mm_nt(block, self.qkv_w) for block in self.lows]

    def finish_back(self, partial, meanwhile=no_round):
        lay = self.lay
        normed_grad = relative(scatter_rows(*partial, lay, meanwhile), lay)
        input_part, gain_one_grad = norm_backward(
            self.inputs, self.inverse_first, self.gain_one, normed_grad
        )
        self.gain_grads = jnp.stack([gain_one_grad, self.gain_two_grad])
        return self.mid_grad + input_part


def joined(pair):
    return jnp.concatenate(pair, 0)


def gain_sums(gains, lay):
    own = pick(gains, lay.core) + lay.to_core(pick(gains, 1 - lay.core))
    parts = own.reshape(2, lay.shards, lay.halves, lay.group, -1).transpose(1, 2, 3, 0, 4)
    parts = pick(parts, lay.shard) + lay.to_shard(pick(parts, 1 - lay.shard))
    parts = pick(parts, lay.half) + lay.to_half(pick(parts, 1 - lay.half))
    total = pick(parts, lay.member)
    for step in range(1, lay.group):
        total = total + lay.to_member(pick(parts, lay.member ^ step), step)
    return total


def row_tables(pair_table, block_rows, lay):
    cores = []
    for core in (lay.core, 1 - lay.core):
        ctx_ids = jnp.stack([core * lay.group + (lay.member ^ step) for step in range(lay.group)])
        owned = jnp.sum(
            jnp.where(ctx_ids[:, None] == jnp.arange(lay.ctx)[None, :], pair_table[None, :], 0), 1
        )
        blocks = jnp.stack([owned, 2 * lay.ctx - 1 - owned], 1)
        rows = blocks[:, :, None] * block_rows + jnp.arange(block_rows)[None, None, :]
        cores.append(rows.reshape(-1))
    positions = jnp.concatenate(cores)
    freq_idx = jnp.arange(HALF, dtype=F32)
    inverse = ROPE_BASE ** (-2.0 * freq_idx / HEAD_DIM)
    angles = positions.astype(F32)[:, None] * inverse[None, :]
    pad = ((0, 0), (0, HALF_LANES - HALF))
    cos_h, sin_h = jnp.pad(jnp.cos(angles), pad), jnp.pad(jnp.sin(angles), pad)
    cos_t = jnp.concatenate([cos_h, cos_h], 1)
    sin_t = jnp.concatenate([-sin_h, sin_h], 1)
    count = cores[0].shape[0]
    return (
        cos_t[:count],
        sin_t[:count],
        cos_t[count:],
        sin_t[count:],
        positions[:, None],
        positions[None, :],
    )


def deal_rows(local, lay):
    turn = lay.half ^ lay.core
    straight = lay.move(
        pick(local, turn), lambda core, half, member, shard: (half, half ^ core, member, shard)
    )
    crossed = lay.move(
        pick(local, 1 - turn),
        lambda core, half, member, shard: (half, 1 - (half ^ core), member, shard),
    )
    return jnp.where(turn == 0, straight, crossed), jnp.where(turn == 0, crossed, straight)


def return_rows(input_grad, outputs, lay):
    turn = lay.half ^ lay.core
    straight = lay.move(
        jnp.where(turn == 0, input_grad, outputs),
        lambda core, half, member, shard: (core ^ half, core, member, shard),
    )
    crossed = lay.move(
        jnp.where(turn == 0, outputs, input_grad),
        lambda core, half, member, shard: (1 - (core ^ half), core, member, shard),
    )
    return two_way(turn, straight, crossed, 0)


def body(
    ends_in, pair_table, norm_attn, w_query, w_key, w_value, w_out, norm_mlp, w_gate, w_up, w_down
):
    lay = Layout()
    rows = ends_in.shape[3]
    width = ends_in.shape[4]
    row_block = w_query.shape[1]
    pairs = lay.cores * lay.group
    n_query = max(1, HEADS // pairs)
    n_key = max(1, KV_HEADS // pairs)
    ff_unit = w_down.shape[1] // lay.cores
    q_cols, k_cols = n_query * HEAD_DIM, n_key * HEAD_DIM
    spread_lanes = lane_matrix(n_query + 2 * n_key)
    spread_out = lane_matrix(n_query)
    over_half, over_shard = Wire(lay.to_half), Wire(lay.to_shard)
    cols = q_cols + 2 * k_cols
    ff = ff_unit * 4

    gains = jnp.stack([norm_attn[0], norm_mlp[0]])
    gain_parts = [lay.to_member(gains, step) for step in range(1, lay.group)]
    heads = pack_heads(w_query[0], w_key[0], w_value[0], lay)
    qkv_layers = split_cores(heads, lay)
    qkv_first, begun = swap_columns(qkv_layers[0], lay, gain_parts)
    gains = place(gains, gain_parts, lay.member)
    gains = two_way(lay.half, gains, lay.to_half(after(gains, begun)), 0)
    qkv_0 = Spread(qkv_first)
    sent = qkv_0.over_half(over_half, (gains,))
    gains = two_way(lay.shard, gains, lay.to_shard(after(gains, sent)), 0)
    local = to_inner(after(ends_in, begun)[0, :, 0], lay)
    own_in, own_cot = deal_rows(after(local, sent), lay)
    gains = two_way(lay.core, gains, lay.to_core(gains), 0)
    gains = gains.transpose(0, 4, 1, 2, 3, 5).reshape(2, 2, -1).astype(F32)
    w_gate, w_up, w_out, w_down = (after(block, begun) for block in (w_gate, w_up, w_out, w_down))
    gate_up_layers = split_cores(pack_ff(w_gate[0], w_up[0], lay, ff_unit), lay, (sent,))
    rest = jnp.concatenate([gate_up_layers[0], qkv_layers[1], gate_up_layers[1]], -1)
    rest, rest_sent = swap_columns(rest, lay, (own_in, own_cot))
    out = SpreadOut(to_inner(w_out[0], lay), lay, (rest_sent,))
    down_layers = split_cores(
        to_inner(w_down[0], lay).reshape(lay.cores, ff_unit, width), lay, (rest_sent,)
    )
    tables = row_tables(after(pair_table, begun), rows // 2, lay)
    gate_0, up_0 = Spread(rest[:, :ff]), Spread(rest[:, ff : 2 * ff])
    qkv_1 = Spread(rest[:, 2 * ff : 2 * ff + cols])
    gate_1 = Spread(rest[:, 2 * ff + cols : 3 * ff + cols])
    up_1 = Spread(rest[:, 3 * ff + cols :])
    down_0, down_1 = Spread(down_layers[0]), Spread(down_layers[1])
    out.over_half(over_half)
    qkv_0.over_shard(over_shard)
    gate_0.over_half(over_half)
    out.over_shard(over_shard)

    def round_of(halves, shards):
        def run(arrived):
            sent = [item.over_half(over_half, arrived) for item in halves]
            return sent + [item.over_shard(over_shard, arrived) for item in shards]

        return run

    def layer(index, qkv, out_w):
        return Layer(
            lay,
            tables,
            n_query,
            n_key,
            gains[index, 0],
            gains[index, 1],
            mm(qkv.full(), spread_lanes).astype(BF16),
            mm_tn(spread_out, out_w).astype(BF16),
        )

    out_w = out.full()
    first = layer(0, qkv_0, out_w[0])
    first.start(own_in.astype(F32))
    first.attention(round_of([up_0], [gate_0]), round_of([down_0], [up_0]))
    first.gate_up_w = jnp.concatenate([gate_0.full(), up_0.full()], 1)
    down_0.over_shard(over_shard)
    qkv_1.over_half(over_half, (up_0.got,))
    first.down_w = down_0.full()
    first.hide()
    first_out = first.feed_forward(round_of([gate_1], [qkv_1]))
    second = layer(1, qkv_1, out_w[1])
    second.start(first_out.astype(BF16).astype(F32), round_of([up_1], [gate_1]))
    second.start_back(own_cot.astype(F32))
    second.attention(round_of([down_1], [up_1]), round_of([], [down_1]))
    second.gate_up_w = jnp.concatenate([gate_1.full(), up_1.full()], 1)
    second.down_w = down_1.full()

    def gate_up_collects(which):
        left, right = joined(which.normed_mid), joined(which.gate_up_grad)
        return Collect(left, right[:, :ff]), Collect(left, right[:, ff:])

    def out_collect(which):
        left = mm_nt(joined(which.attn_out), spread_out).astype(BF16)
        return CollectOut(left, joined(which.mid_low), lay, row_block)

    def qkv_collect(which):
        low = mm_nt(joined(which.lows), spread_lanes).astype(BF16)
        return Collect(joined(which.normed), low)

    second.hide()
    down_1 = Collect(joined(second.hidden), joined(second.down_in))
    second_out = second.feed_forward(round_of([], [down_1]))
    partial = second.feed_forward_back()
    partial[0] = after(partial[0], second_out)
    gate_1, up_1 = gate_up_collects(second)
    second.middle_back(partial, round_of([down_1], [gate_1]), round_of([gate_1], [up_1]))
    out_1 = out_collect(second)
    partial = second.attention_back()
    qkv_1 = qkv_collect(second)

    def last_of_second(arrived):
        sent = [qkv_1.over_shard(over_shard, arrived)]
        sent.append(out_1.over_shard(over_shard, arrived, beside=True))
        return sent + [up_1.over_half(over_half, arrived)]

    second_grad = second.finish_back(partial, last_of_second)

    first.start_back(second_grad.astype(BF16).astype(F32), round_of([qkv_1], []))
    down_0 = Collect(joined(first.hidden), joined(first.down_in))
    partial = first.feed_forward_back()
    partial[0] = after(partial[0], down_0.over_shard(over_shard))
    gate_0, up_0 = gate_up_collects(first)
    first.middle_back(partial, round_of([out_1, down_0], [gate_0]), round_of([gate_0], [up_0]))
    out_0 = out_collect(first)
    parts = [gate_1.total(), up_1.total(), qkv_1.total()]
    parts = jnp.concatenate(parts, 1).reshape(lay.group, row_block, -1)
    back_1, sent = return_columns(parts, lay, (first.mid_low[1],))
    partial = first.attention_back()
    qkv_0 = qkv_collect(first)
    partial[1] = after(partial[1], qkv_0.over_shard(over_shard), *sent)
    first_grad = first.finish_back(partial, round_of([up_0], [out_0]))
    last = qkv_0.over_half(over_half)
    out_0.over_half(over_half, beside=True)

    def member_parts(blocks, deps):
        parts = jnp.concatenate([block.total(deps) for block in blocks], 1)
        return parts.reshape(lay.group, row_block, -1)

    back_0, sent = return_columns(member_parts([gate_0, up_0], sent), lay, ())
    back_q, sent = return_columns(member_parts([qkv_0], sent), lay, ())
    first_w = back_q, out_0.total(sent), back_0, down_0.total(sent)
    second_w = back_1[..., 2 * ff :], out_1.total(sent), back_1[..., : 2 * ff], down_1.total(sent)
    first_gains, second_gains = first.gain_grads, second.gain_grads
    gain_g = gain_sums(jnp.stack([first_gains, second_gains]), lay)
    ends = to_outer(return_rows(first_grad.astype(BF16), second_out.astype(BF16), lay), lay)

    qkv_g = unpack_heads(join_cores(first_w[0], second_w[0], lay), lay)
    out_g = to_outer(join_out(first_w[1], second_w[1], lay, row_block), lay)
    gate_up_g = unpack_ff(join_cores(first_w[2], second_w[2], lay), lay, ff_unit)
    down_g = to_outer(join_cores(first_w[3], second_w[3], lay).reshape(-1, width), lay)
    return (
        ends[None, :, None],
        gain_g[0][None],
        qkv_g[0][None],
        qkv_g[1][None],
        qkv_g[2][None],
        out_g[None],
        gain_g[1][None],
        gate_up_g[0][None],
        gate_up_g[1][None],
        down_g[None],
    )


def solution(mesh):
    rows = P("section", None, "shard", "ctx", None)
    vector = P("section", ("ctx", "shard"))
    matrix = P("section", ("ctx", "shard"), None)
    return jax.shard_map(
        body,
        mesh=mesh,
        in_specs=(rows, P(), vector, matrix, matrix, matrix, matrix, vector, matrix, matrix, matrix),
        out_specs=(rows, vector, matrix, matrix, matrix, matrix, vector, matrix, matrix, matrix),
        check_vma=False,
    )
```

```python
import jax
import jax.numpy as jnp
from jax import lax
from jax.experimental import pallas as pl
from jax.experimental.pallas import tpu as pltpu
from jax.sharding import PartitionSpec as P

HEADS = 16
KV_HEADS = 8
HEAD_DIM = 96
HALF = HEAD_DIM // 2
LANES = 128
HALF_LANES = LANES // 2

NORM_EPS = 1e-05
ROPE_BASE = 100000.0
MASK_FILL = -1e30

MESH_AXES = ("section", "ctx", "shard")
F32 = jnp.float32
BF16 = jnp.bfloat16
VMEM_LIMIT = pltpu.CompilerParams(vmem_limit_bytes=56 * 1024 * 1024)


class Layout:
    def __init__(self):
        self.cores = lax.axis_size("section")
        self.ctx = lax.axis_size("ctx")
        self.shards = lax.axis_size("shard")
        self.halves = 2
        self.group = self.ctx // self.halves
        ctx_index = lax.axis_index("ctx")
        self.core = lax.axis_index("section")
        self.half = ctx_index // self.group
        self.member = ctx_index % self.group
        self.shard = lax.axis_index("shard")

    def move(self, block, target):
        pairs = []
        for core in range(self.cores):
            for half in range(self.halves):
                for member in range(self.group):
                    for shard in range(self.shards):
                        to = target(core, half, member, shard)
                        pairs.append((self.flat(core, half, member, shard), self.flat(*to)))
        return lax.ppermute(block, MESH_AXES, pairs)

    def move_some(self, block, sends, target):
        pairs = []
        for core in range(self.cores):
            for half in range(self.halves):
                for member in range(self.group):
                    for shard in range(self.shards):
                        if sends(core, half, member, shard):
                            to = target(core, half, member, shard)
                            pairs.append((self.flat(core, half, member, shard), self.flat(*to)))
        return lax.ppermute(block, MESH_AXES, pairs)

    def flat(self, core, half, member, shard):
        return (core * self.ctx + half * self.group + member) * self.shards + shard

    def to_member(self, block, step):
        return self.move(block, lambda core, half, member, shard: (core, half, member ^ step, shard))

    def to_half(self, block):
        return self.move(block, lambda core, half, member, shard: (core, 1 - half, member, shard))

    def to_shard(self, block):
        return self.move(block, lambda core, half, member, shard: (core, half, member, 1 - shard))

    def to_core(self, block):
        return self.move(block, lambda core, half, member, shard: (1 - core, half, member, shard))


def pick(parts, index):
    return lax.dynamic_index_in_dim(parts, index, 0, False)


def after(block, *earlier):
    return lax.optimization_barrier((block,) + earlier)[0] if earlier else block


class Order:
    def __init__(self):
        self.last = ()

    def __call__(self, *blocks):
        if self.last:
            blocks = lax.optimization_barrier(tuple(blocks) + self.last)[: len(blocks)]
        self.last = (blocks[0],)
        return blocks[0] if len(blocks) == 1 else blocks

    def sent(self, transfer, wire):
        self.last = (transfer(wire, self.last),)


class Wire:
    def __init__(self, move):
        self.move = move
        self.last = ()

    def send(self, block, deps=(), move=None, beside=False):
        block = after(block, *(() if beside else self.last), *deps)
        got = (move or self.move)(block)
        self.last = self.last + (got,) if beside else (got,)
        return got, block


def two_way(index, own, other, axis):
    first = jnp.where(index == 0, own, other)
    second = jnp.where(index == 0, other, own)
    return jnp.stack([first, second], axis)


def rearrange_kernel(plans, count, *refs):
    sources, outs = refs[:count], refs[count:]
    for out, plan in zip(outs, plans):
        for index, pieces in plan:
            blocks = [
                sources[source][place + (slice(None), slice(column, column + width))]
                for source, place, column, width in pieces
            ]
            out[index] = jnp.concatenate(blocks, 1) if len(blocks) > 1 else blocks[0]


def rearrange(sources, shapes, plans):
    dtype = sources[0].dtype
    moved = sum(source.size for source in sources) * dtype.itemsize
    return pl.pallas_call(
        lambda *refs: rearrange_kernel(plans, len(sources), *refs),
        out_shape=[jax.ShapeDtypeStruct(shape, dtype) for shape in shapes],
        compiler_params=VMEM_LIMIT,
        cost_estimate=pl.CostEstimate(flops=0, bytes_accessed=2 * moved, transcendentals=0),
        name="rearrange",
    )(*sources)


def kernel_width(width):
    return width % HEAD_DIM == 0 or width % LANES == 0


def to_inner(block, lay, inner=True):
    blocks = lay.shards * lay.halves * lay.group
    width = block.shape[-1] // blocks
    outer_order = [
        ((half * lay.group + member) * lay.shards + shard) * width
        for shard in range(lay.shards)
        for half in range(lay.halves)
        for member in range(lay.group)
    ]
    if kernel_width(width):
        columns = outer_order
        if not inner:
            columns = [outer_order.index(i * width) * width for i in range(blocks)]
        flat = block.reshape(-1, block.shape[-1])
        plan = [((slice(None), slice(None)), [(0, (), column, width) for column in columns])]
        return rearrange([flat], [flat.shape], [plan])[0].reshape(block.shape)
    if inner:
        parts = block.reshape(block.shape[:-1] + (lay.halves, lay.group, lay.shards, -1))
        return jnp.moveaxis(parts, -2, -4).reshape(block.shape)
    parts = block.reshape(block.shape[:-1] + (lay.shards, lay.halves, lay.group, -1))
    return jnp.moveaxis(parts, -4, -2).reshape(block.shape)


def to_outer(block, lay):
    return to_inner(block, lay, False)


def relative(block, lay):
    width = block.shape[-1] // 4
    parts = [block[..., i * width : (i + 1) * width] for i in range(4)]
    parts = [jnp.where(lay.half == 0, parts[i], parts[i ^ 1]) for i in range(4)]
    parts = [jnp.where(lay.shard == 0, parts[i], parts[i ^ 2]) for i in range(4)]
    return jnp.concatenate(parts, -1)


def head_copies(lay):
    return max(1, lay.cores * lay.group // HEADS)


def split_heads(weight, lay, heads):
    rows = weight.shape[0]
    pairs = lay.cores * lay.group
    distinct = min(pairs, heads)
    parts = weight.reshape(rows, distinct, -1).transpose(1, 0, 2)
    parts = jnp.repeat(parts, pairs // distinct, axis=0) if pairs > distinct else parts
    return parts.reshape((lay.cores, lay.group) + parts.shape[1:])


def merge_heads(parts, lay, heads):
    pairs = lay.cores * lay.group
    distinct = min(pairs, heads)
    rows = parts.shape[2]
    parts = parts.reshape(distinct, pairs // distinct, rows, -1)
    parts = jnp.sum(parts, 1) if pairs > distinct else parts[:, 0]
    return parts.transpose(1, 0, 2).reshape(rows, -1)


def split_ff(weight, lay, unit):
    rows = weight.shape[0]
    parts = weight.reshape(rows, lay.halves, lay.group, lay.shards, lay.cores, unit)
    return parts.transpose(4, 2, 0, 3, 1, 5).reshape(lay.cores, lay.group, rows, -1)


def merge_ff(parts, lay, unit):
    rows = parts.shape[2]
    parts = parts.reshape(lay.cores, lay.group, rows, lay.shards, lay.halves, unit)
    return parts.transpose(2, 4, 1, 3, 0, 5).reshape(rows, -1)


def pack_heads(query, key, value, lay):
    pairs = lay.cores * lay.group
    if pairs != KV_HEADS or query.shape[0] % 16:
        sides = [(query, HEADS), (key, KV_HEADS), (value, KV_HEADS)]
        return jnp.concatenate([split_heads(block, lay, heads) for block, heads in sides], -1)
    wide, slim = query.shape[1] // pairs, key.shape[1] // pairs
    plan = []
    for pair in range(pairs):
        pieces = [(0, (), pair * wide, wide), (1, (), pair * slim, slim), (2, (), pair * slim, slim)]
        plan.append(((pair // lay.group, pair % lay.group), pieces))
    shape = (lay.cores, lay.group, query.shape[0], wide + 2 * slim)
    return rearrange([query, key, value], [shape], [plan])[0]


def unpack_heads(parts, lay):
    pairs = lay.cores * lay.group
    q_cols = max(1, HEADS // pairs) * HEAD_DIM
    k_cols = max(1, KV_HEADS // pairs) * HEAD_DIM
    if pairs != KV_HEADS:
        sides = [(0, q_cols, HEADS), (q_cols, k_cols, KV_HEADS), (q_cols + k_cols, k_cols, KV_HEADS)]
        return [merge_heads(parts[..., at : at + cols], lay, heads) for at, cols, heads in sides]
    rows = parts.shape[2]
    plans, shapes = [], []
    for first, cols in ((0, q_cols), (q_cols, k_cols), (q_cols + k_cols, k_cols)):
        pieces = [(0, (pair // lay.group, pair % lay.group), first, cols) for pair in range(pairs)]
        plans.append([((slice(None), slice(None)), pieces)])
        shapes.append((rows, pairs * cols))
    return rearrange([parts], shapes, plans)


def ff_columns(lay, core, member, unit):
    for shard in range(lay.shards):
        for half in range(lay.halves):
            block = (half * lay.group + member) * lay.shards + shard
            yield (block * lay.cores + core) * unit, shard * lay.halves + half


def pack_ff(gate, up, lay, unit):
    if not kernel_width(unit):
        return jnp.concatenate([split_ff(gate, lay, unit), split_ff(up, lay, unit)], -1)
    plan = []
    for core in range(lay.cores):
        for member in range(lay.group):
            columns = [column for column, _ in ff_columns(lay, core, member, unit)]
            pieces = [(side, (), column, unit) for side in (0, 1) for column in columns]
            plan.append(((core, member), pieces))
    shape = (lay.cores, lay.group, gate.shape[0], 8 * unit)
    return rearrange([gate, up], [shape], [plan])[0]


def unpack_ff(parts, lay, unit):
    ff = 4 * unit
    if not kernel_width(unit):
        return [merge_ff(parts[..., :ff], lay, unit), merge_ff(parts[..., ff:], lay, unit)]
    rows = parts.shape[2]
    plans = []
    for side in (0, 1):
        found = {}
        for core in range(lay.cores):
            for member in range(lay.group):
                for column, place in ff_columns(lay, core, member, unit):
                    found[column] = (0, (core, member), side * ff + place * unit, unit)
        pieces = [found[column] for column in sorted(found)]
        plans.append([((slice(None), slice(None)), pieces)])
    return rearrange([parts], [(rows, len(found) * unit)] * 2, plans)


def place(own, others, member):
    group = 1 + len(others)
    stacked = jnp.zeros((group,) + own.shape, own.dtype)
    for step, block in enumerate((own,) + tuple(others)):
        stacked = lax.dynamic_update_index_in_dim(stacked, block, member ^ step, 0)
    return stacked


def split_cores(parts, lay, order):
    return lay.to_core(order(pick(parts, 1 - lay.core)))


def core_layers(parts, other, lay):
    kept = pick(parts, lay.core)
    return jnp.where(lay.core == 0, kept, other), jnp.where(lay.core == 0, other, kept)


def to_members(parts, lay, order):
    sent = order(*[pick(parts, lay.member ^ step) for step in range(1, lay.group)])
    sent = sent if isinstance(sent, (tuple, list)) else (sent,)
    return [lay.to_member(block, step) for step, block in enumerate(sent, 1)]


def listed(blocks):
    return list(blocks) if isinstance(blocks, (tuple, list)) else [blocks]


def member_rows(parts, others, lay):
    return place(pick(parts, lay.member), others, lay.member).reshape(-1, parts.shape[-1])


class Spread:
    def __init__(self, block):
        self.block = block

    def over_half(self, wire, deps=(), **how):
        self.got, sent = wire.send(self.block, deps, **how)
        return sent

    def over_shard(self, wire, deps=(), **how):
        self.pair = jnp.concatenate([self.block, after(self.got, *deps)], 0)
        self.got, sent = wire.send(self.pair, **how)
        return sent

    def full(self):
        return jnp.concatenate([self.pair, self.got], 0)


class Collect:
    def __init__(self, left, right):
        self.left, self.right = left, right
        self.rows = left.shape[1] // 4

    def over_shard(self, wire, deps=(), **how):
        block = mm_tn(self.left[:, 2 * self.rows :], self.right).astype(BF16)
        self.got, sent = wire.send(block, deps, **how)
        return sent

    def over_half(self, wire, deps=(), **how):
        rows = self.rows
        kept = mm_tn(self.left[:, : 2 * rows], self.right)
        got = after(self.got, *deps).astype(F32)
        self.kept = kept[:rows] + got[:rows]
        self.arrived, sent = wire.send((kept[rows:] + got[rows:]).astype(BF16), **how)
        return sent

    def total(self, deps=()):
        return self.kept + after(self.arrived, *deps).astype(F32)


def join_cores(first, second, lay, order):
    sent = order(jnp.where(lay.core == 0, second, first).astype(BF16))
    return jnp.where(lay.core == 0, first, second), lay.to_core(sent)


def joined_cores(pair, lay, order):
    return two_way(lay.core, pair[0], order(pair[1]).astype(F32), 0)


def out_aligned(lay, block_rows):
    return block_rows == HEAD_DIM and lay.cores * lay.group == KV_HEADS and lay.cores == lay.halves


class SpreadOut:
    def __init__(self, w_out, lay, order):
        self.lay, self.width = lay, w_out.shape[-1]
        self.aligned = out_aligned(lay, w_out.shape[0])
        if not self.aligned:
            w_out = lax.all_gather(w_out, ("ctx", "shard"), axis=0, tiled=True)
        self.own = w_out
        self.got = lay.to_core(order(w_out))

    def stack(self, order):
        lay, other = self.lay, order(self.got)
        self.block = jnp.stack(
            [jnp.where(lay.core == 0, self.own, other), jnp.where(lay.core == 0, other, self.own)]
        )

    def over_half(self, wire, deps=()):
        lay = self.lay
        if not self.aligned:
            return self.block
        move = lambda block: lay.move_some(
            block,
            lambda core, half, member, shard: half == core,
            lambda core, half, member, shard: (core, 1 - half, member, shard),
        )
        self.got, sent = wire.send(self.block, deps, move)
        return sent

    def over_shard(self, wire, deps=()):
        lay = self.lay
        if not self.aligned:
            return self.block
        self.block = jnp.where(lay.half == lay.core, self.block, after(self.got, *deps))
        self.got, sent = wire.send(self.block)
        return sent

    def full(self):
        if self.aligned:
            return jnp.concatenate([self.block, self.got], 1)
        head = (self.lay.core * self.lay.group + self.lay.member) // head_copies(self.lay)
        count = max(1, HEADS // (self.lay.cores * self.lay.group)) * HEAD_DIM
        return lax.dynamic_slice_in_dim(self.block, head * count, count, 1)


def out_pair(which, spread_out):
    return mm_nt(joined(which.attn_out), spread_out).astype(BF16), joined(which.mid_low)


class CollectOut:
    def __init__(self, pairs, lay, block_rows):
        self.pairs, self.lay = pairs, lay
        self.aligned = out_aligned(lay, block_rows)
        self.rows = pairs[0][0].shape[1] // 2

    def over_shard(self, wire, deps=(), **how):
        if not self.aligned:
            self.kept = jnp.stack([mm_tn(left, right) for left, right in self.pairs])
            return self.kept
        blocks = [mm_tn(left[:, self.rows :], right).astype(BF16) for left, right in self.pairs]
        self.got, sent = wire.send(jnp.concatenate(blocks, 0), deps, **how)
        return sent

    def over_half(self, wire, deps=(), **how):
        lay = self.lay
        if not self.aligned:
            return self.kept
        blocks = [mm_tn(left[:, : self.rows], right) for left, right in self.pairs]
        self.kept = jnp.concatenate(blocks, 0) + after(self.got, *deps).astype(F32)
        move = lambda block: lay.move_some(
            block,
            lambda core, half, member, shard: half != core,
            lambda core, half, member, shard: (core, 1 - half, member, shard),
        )
        self.arrived, sent = wire.send(self.kept.astype(BF16), (), move, **how)
        return sent

    def total(self, deps=()):
        if not self.aligned:
            return self.kept[0], self.kept[1]
        total = self.kept + after(self.arrived, *deps).astype(F32)
        return total[: self.rows], total[self.rows :]


def join_out(first, second, lay, block_rows):
    if not out_aligned(lay, block_rows):
        width = first.shape[1]
        head = (lay.core * lay.group + lay.member) // head_copies(lay)
        full = jnp.zeros((2, HEADS * HEAD_DIM, width), F32)
        full = lax.dynamic_update_slice_in_dim(
            full, jnp.stack([first, second]), head * first.shape[0], 1
        )
        full = pick(lax.psum(full, MESH_AXES), lay.core)
        block = (lay.half * lay.group + lay.member) * lay.shards + lay.shard
        return lax.dynamic_slice_in_dim(full, block * block_rows, block_rows, 0)
    kept = jnp.where(lay.core == 0, first, second)
    sent = jnp.where(lay.core == 0, second, first).astype(BF16)
    other = lay.to_core(sent).astype(F32)
    return jnp.where(lay.half == lay.core, kept, other)


def lane_matrix(heads):
    source = jnp.arange(heads * HEAD_DIM)
    head, offset = source // HEAD_DIM, source % HEAD_DIM
    target = head * LANES + (offset // HALF) * HALF_LANES + offset % HALF
    return (target[:, None] == jnp.arange(heads * LANES)[None, :]).astype(BF16)


def rot(vec, cos_t, sin_t):
    return vec * cos_t + pltpu.roll(vec, HALF_LANES, 1) * sin_t


def rot_back(vec, cos_t, sin_t):
    return vec * cos_t - pltpu.roll(vec, HALF_LANES, 1) * sin_t


def mm(a, b):
    return lax.dot_general(a, b, (((1,), (0,)), ((), ())), preferred_element_type=F32)


def mm_nt(a, b):
    return lax.dot_general(a, b, (((1,), (1,)), ((), ())), preferred_element_type=F32)


def mm_tn(a, b):
    return lax.dot_general(a, b, (((0,), (0,)), ((), ())), preferred_element_type=F32)


def heads_of(block, count):
    return jnp.concatenate([block[:, i * LANES : (i + 1) * LANES] for i in range(count)], 0)


def lanes_of(index, count=1):
    return slice(index * LANES, (index + count) * LANES)


def attend_kernel(
    n_query, n_key, raw_own, raw_sib, cos_t, sin_t, pos_q, pos_k, out_own, out_sib, lse_out, own, sib
):
    scale = HEAD_DIM ** (-0.5)
    per_key = n_query // n_key
    half = raw_own.shape[0]
    rows = 2 * half
    cos_v, sin_v = cos_t[...], sin_t[...]
    mask = pos_q[...] >= pos_k[...]
    mask = jnp.concatenate([mask] * per_key, 0)

    def both(index, turned):
        block = jnp.concatenate([raw_own[:, lanes_of(index)], raw_sib[:, lanes_of(index)]], 0)
        block = (rot(block, cos_v, sin_v) if turned else block).astype(BF16)
        own[:, lanes_of(index)] = block[:half]
        sib[:, lanes_of(index)] = block[half:]
        return block

    for kv_head in range(n_key):
        key, value = both(n_query + kv_head, True), both(n_query + n_key + kv_head, False)
        q_first = kv_head * per_key
        query = jnp.concatenate([both(q_first + i, True) for i in range(per_key)], 0)
        scores = jnp.where(mask, mm_nt(query, key) * scale, MASK_FILL)
        row_max = jnp.max(scores, -1, keepdims=True)
        weights = jnp.exp(scores - row_max)
        total = jnp.sum(weights, -1, keepdims=True)
        probs = (weights * (1.0 / total)).astype(BF16)
        out = mm(probs, value).astype(BF16)
        for i in range(per_key):
            out_own[:, lanes_of(q_first + i)] = out[i * rows : i * rows + half]
            out_sib[:, lanes_of(q_first + i)] = out[i * rows + half : (i + 1) * rows]
        lse_out[kv_head] = row_max + jnp.log(total)


def attend(raw_own, raw_sib, tables, n_query, n_key):
    half, lanes = raw_own.shape
    return pl.pallas_call(
        lambda *refs: attend_kernel(n_query, n_key, *refs),
        out_shape=[
            jax.ShapeDtypeStruct((half, n_query * LANES), BF16),
            jax.ShapeDtypeStruct((half, n_query * LANES), BF16),
            jax.ShapeDtypeStruct((n_key, n_query // n_key * 2 * half, 1), F32),
            jax.ShapeDtypeStruct((half, lanes), BF16),
            jax.ShapeDtypeStruct((half, lanes), BF16),
        ],
        compiler_params=VMEM_LIMIT,
        cost_estimate=pl.CostEstimate(
            flops=16 * n_query * half * half * LANES,
            bytes_accessed=half * n_query * LANES * 24,
            transcendentals=4 * n_query * half * half,
        ),
        name="attend",
    )(raw_own, raw_sib, *tables)


def attend_back_kernel(
    n_query, n_key, own, sib, do_own, do_sib, lse, cos_t, sin_t, pos_q, pos_k, low_own, low_sib
):
    scale = HEAD_DIM ** (-0.5)
    per_key = n_query // n_key
    half = own.shape[0]
    rows = 2 * half
    cos_v, sin_v = cos_t[...], sin_t[...]
    mask = pos_q[...] >= pos_k[...]
    mask = jnp.concatenate([mask] * per_key, 0)

    def put(index, block):
        low_own[:, lanes_of(index)] = block[:half].astype(BF16)
        low_sib[:, lanes_of(index)] = block[half:].astype(BF16)

    def both(a, b, index):
        return jnp.concatenate([a[:, lanes_of(index)], b[:, lanes_of(index)]], 0)

    for kv_head in range(n_key):
        key, value = both(own, sib, n_query + kv_head), both(own, sib, n_query + n_key + kv_head)
        q_first = kv_head * per_key
        query = jnp.concatenate([both(own, sib, q_first + i) for i in range(per_key)], 0)
        grad = jnp.concatenate([both(do_own, do_sib, q_first + i) for i in range(per_key)], 0)
        scores = jnp.where(mask, mm_nt(query, key) * scale, MASK_FILL)
        probs = jnp.exp(scores - lse[kv_head])
        prob_grad = mm_nt(grad, value)
        delta = jnp.sum(probs * prob_grad, -1, keepdims=True)
        score_grad = (probs * (prob_grad - delta)).astype(BF16)
        dq = mm(score_grad, key) * scale
        for i in range(per_key):
            put(q_first + i, rot_back(dq[i * rows : (i + 1) * rows], cos_v, sin_v))
        put(n_query + kv_head, rot_back(mm_tn(score_grad, query) * scale, cos_v, sin_v))
        put(n_query + n_key + kv_head, mm_tn(probs.astype(BF16), grad))


def attend_back(kept, out_grads, tables, n_query, n_key):
    own, sib, lse = kept
    half, lanes = own.shape
    return pl.pallas_call(
        lambda *refs: attend_back_kernel(n_query, n_key, *refs),
        out_shape=[
            jax.ShapeDtypeStruct((half, lanes), BF16),
            jax.ShapeDtypeStruct((half, lanes), BF16),
        ],
        compiler_params=VMEM_LIMIT,
        cost_estimate=pl.CostEstimate(
            flops=40 * n_query * half * half * LANES,
            bytes_accessed=half * lanes * 16,
            transcendentals=4 * n_query * half * half,
        ),
        name="attend_back",
    )(own, sib, *out_grads, lse, *tables)


def no_round(first):
    return ()


def gather_rows(block, lay, meanwhile=no_round):
    others = [lay.to_member(block, step) for step in range(1, lay.group)]
    own = after(jnp.concatenate([block] + others, 0), *meanwhile(others))
    return own, lay.to_core(own)


def scatter_rows(own, sib, lay, meanwhile=no_round):
    own = own + lay.to_core(sib.astype(BF16)).astype(F32)
    rows = own.shape[0] // lay.group
    parts = own.reshape(lay.group, rows, -1)
    others = [lay.to_member(parts[step].astype(BF16), step) for step in range(1, lay.group)]
    total = parts[0]
    for block in others:
        total = total + block.astype(F32)
    return after(total, *meanwhile(others))


def norm_forward(inputs, gain_vec):
    inverse_rms = lax.rsqrt(jnp.mean(inputs * inputs, -1, keepdims=True) + NORM_EPS)
    return (inputs * inverse_rms * gain_vec).astype(BF16), inverse_rms


def norm_backward(inputs, inverse_rms, gain_vec, upstream):
    scaled = upstream * gain_vec
    input_grad = inverse_rms * scaled - inputs * inverse_rms**3 * jnp.mean(
        scaled * inputs, -1, keepdims=True
    )
    gain_grad = jnp.sum(upstream * inputs * inverse_rms, 0)
    return input_grad, gain_grad


def out_order(block, lay, n_query):
    if head_copies(lay) > 1:
        share = (lay.core * lay.group + lay.member) % head_copies(lay) == 0
        return jnp.where(share, block, jnp.zeros_like(block))
    if n_query != 2 or lay.cores * lay.group != KV_HEADS:
        return block
    swapped = jnp.concatenate([block[:, LANES:], block[:, :LANES]], 1)
    return jnp.where(lay.shard == 0, block, swapped)


class Layer:
    def __init__(self, lay, tables, n_query, n_key, gain_one, gain_two, order):
        self.order = order
        self.lay, self.tables, self.n_query, self.n_key = lay, tables, n_query, n_key
        self.gain_one, self.gain_two = gain_one, gain_two

    def normed_rows(self, inputs):
        self.inputs = inputs
        normed, self.inverse_first = norm_forward(inputs, self.gain_one)
        return self.order(normed, self.lay)

    def start(self, inputs, meanwhile=no_round):
        self.normed = gather_rows(self.normed_rows(inputs), self.lay, meanwhile)

    def attend(self):
        lay = self.lay
        raw = [mm(block, self.qkv_w) for block in self.normed]
        out_own, out_sib, lse, own, sib = attend(*raw, self.tables, self.n_query, self.n_key)
        self.attn_kept = own, sib, lse
        self.attn_out = [out_order(block, lay, self.n_query) for block in (out_own, out_sib)]

    def attention(self, during_out=no_round, during_rows=no_round):
        lay = self.lay
        partial = [mm(block, self.out_w) for block in self.attn_out]
        self.mid_stream = self.inputs + scatter_rows(*partial, lay, during_out)
        normed, self.inverse_second = norm_forward(self.mid_stream, self.gain_two)
        self.normed_mid = gather_rows(self.order(normed, lay), lay, during_rows)

    def hide(self):
        lay = self.lay
        self.gate_up, self.hidden = [], []
        for block in self.normed_mid:
            gate_pre, up_pre = mm(block, self.gate_w), mm(block, self.up_w)
            self.gate_up.append((gate_pre, up_pre))
            self.hidden.append(relative((jax.nn.silu(gate_pre) * up_pre).astype(BF16), lay))

    def feed_forward(self, meanwhile=no_round):
        lay = self.lay
        partial = [mm(block, self.down_w) for block in self.hidden]
        return self.mid_stream + scatter_rows(*partial, lay, meanwhile)

    def start_back(self, out_grad, meanwhile=no_round):
        self.out_grad = out_grad
        self.down_in = gather_rows(out_grad.astype(BF16), self.lay, meanwhile)

    def feed_forward_back(self):
        self.gate_grad, self.up_grad, partial = [], [], []
        for block, (gate_pre, up_pre) in zip(self.down_in, self.gate_up):
            hidden_grad = relative(mm_nt(block, self.down_w), self.lay)
            sigmoid_gate = jax.nn.sigmoid(gate_pre)
            gate_grad_in = (
                hidden_grad * up_pre * sigmoid_gate * (1.0 + gate_pre * (1.0 - sigmoid_gate))
            ).astype(BF16)
            up_grad_in = (hidden_grad * gate_pre * sigmoid_gate).astype(BF16)
            self.gate_grad.append(gate_grad_in)
            self.up_grad.append(up_grad_in)
            partial.append(mm_nt(gate_grad_in, self.gate_w) + mm_nt(up_grad_in, self.up_w))
        return partial

    def middle_back(self, partial, during_sum=no_round, during_rows=no_round):
        lay = self.lay
        normed_mid_grad = relative(scatter_rows(*partial, lay, during_sum), lay)
        mid_part, self.gain_two_grad = norm_backward(
            self.mid_stream, self.inverse_second, self.gain_two, normed_mid_grad
        )
        self.mid_grad = self.out_grad + mid_part
        self.mid_low = gather_rows(self.mid_grad.astype(BF16), lay, during_rows)

    def attention_back(self):
        grads = [
            out_order(mm_nt(block, self.out_w).astype(BF16), self.lay, self.n_query)
            for block in self.mid_low
        ]
        self.lows = attend_back(self.attn_kept, grads, self.tables, self.n_query, self.n_key)
        return [mm_nt(block, self.qkv_w) for block in self.lows]

    def finish_back(self, partial, meanwhile=no_round):
        lay = self.lay
        normed_grad = relative(scatter_rows(*partial, lay, meanwhile), lay)
        input_part, gain_one_grad = norm_backward(
            self.inputs, self.inverse_first, self.gain_one, normed_grad
        )
        self.gain_grads = jnp.stack([gain_one_grad, self.gain_two_grad])
        return self.mid_grad + input_part


def joined(pair):
    return jnp.concatenate(pair, 0)


def row_tables(pair_table, block_rows, lay):
    cores = []
    for core in (lay.core, 1 - lay.core):
        ctx_ids = jnp.stack([core * lay.group + (lay.member ^ step) for step in range(lay.group)])
        owned = jnp.sum(
            jnp.where(ctx_ids[:, None] == jnp.arange(lay.ctx)[None, :], pair_table[None, :], 0), 1
        )
        blocks = jnp.stack([owned, 2 * lay.ctx - 1 - owned], 1)
        rows = blocks[:, :, None] * block_rows + jnp.arange(block_rows)[None, None, :]
        cores.append(rows.reshape(-1))
    positions = jnp.concatenate(cores)
    freq_idx = jnp.arange(HALF, dtype=F32)
    inverse = ROPE_BASE ** (-2.0 * freq_idx / HEAD_DIM)
    angles = positions.astype(F32)[:, None] * inverse[None, :]
    pad = ((0, 0), (0, HALF_LANES - HALF))
    cos_h, sin_h = jnp.pad(jnp.cos(angles), pad), jnp.pad(jnp.sin(angles), pad)
    cos_t = jnp.concatenate([cos_h, cos_h], 1)
    sin_t = jnp.concatenate([-sin_h, sin_h], 1)
    return cos_t, sin_t, positions[:, None], positions[None, :]


def deal_rows(local, lay, order):
    turn = lay.half ^ lay.core
    sent = order(pick(local, turn), pick(local, 1 - turn))
    straight = lay.move(
        sent[0], lambda core, half, member, shard: (half, half ^ core, member, shard)
    )
    crossed = lay.move(
        sent[1], lambda core, half, member, shard: (half, 1 - (half ^ core), member, shard)
    )
    return straight, crossed


def dealt(straight, crossed, lay):
    turn = lay.half ^ lay.core
    return jnp.where(turn == 0, straight, crossed), jnp.where(turn == 0, crossed, straight)


def return_rows(input_grad, outputs, lay, order):
    turn = lay.half ^ lay.core
    sent = order(
        jnp.where(turn == 0, input_grad, outputs), jnp.where(turn == 0, outputs, input_grad)
    )
    straight = lay.move(
        sent[0], lambda core, half, member, shard: (core ^ half, core, member, shard)
    )
    crossed = lay.move(
        sent[1], lambda core, half, member, shard: (1 - (core ^ half), core, member, shard)
    )
    return straight, crossed


def body(
    ends_in, pair_table, norm_attn, w_query, w_key, w_value, w_out, norm_mlp, w_gate, w_up, w_down
):
    lay = Layout()
    rows = ends_in.shape[3]
    width = ends_in.shape[4]
    row_block = w_query.shape[1]
    pairs = lay.cores * lay.group
    n_query = max(1, HEADS // pairs)
    n_key = max(1, KV_HEADS // pairs)
    ff_unit = w_down.shape[1] // lay.cores
    q_cols, k_cols = n_query * HEAD_DIM, n_key * HEAD_DIM
    spread_lanes = lane_matrix(n_query + 2 * n_key)
    spread_out = lane_matrix(n_query)
    over_half, over_shard = Wire(lay.to_half), Wire(lay.to_shard)
    cols = q_cols + 2 * k_cols
    ff = ff_unit * 4

    order = Order()
    gains = jnp.stack([norm_attn[0], norm_mlp[0]])
    gain_parts = [lay.to_member(gains, step) for step in range(1, lay.group)]
    heads = pack_heads(w_query[0], w_key[0], w_value[0], lay)
    heads_other = split_cores(heads, lay, order)
    heads_other, *gain_parts = order(heads_other, *gain_parts)
    qkv_layers = core_layers(heads, heads_other, lay)
    qkv_others = to_members(qkv_layers[0], lay, order)
    gains = order(place(gains, gain_parts, lay.member))
    gains_other = lay.to_half(gains)
    w_gate, w_up = order(w_gate, w_up)
    gate_up_own = pack_ff(w_gate[0], w_up[0], lay, ff_unit)
    gate_up_other = split_cores(gate_up_own, lay, order)
    qkv_0 = Spread(member_rows(qkv_layers[0], listed(order(*qkv_others)), lay))
    order.sent(qkv_0.over_half, over_half)
    gains = order(two_way(lay.half, gains, order(gains_other), 0))
    gains_other = lay.to_shard(gains)
    arrived = deal_rows(to_inner(order(ends_in)[0, :, 0], lay), lay, order)
    gains = order(two_way(lay.shard, gains, order(gains_other), 0))
    gains_other = lay.to_core(gains)
    out = SpreadOut(to_inner(order(w_out)[0], lay), lay, order)
    tables = row_tables(order(pair_table), rows // 2, lay)
    gains = two_way(lay.core, gains, order(gains_other), 0)
    gains = gains.transpose(0, 4, 1, 2, 3, 5).reshape(2, 2, -1).astype(F32)

    def layer(index, which):
        heads = n_query, n_key, gains[index, 0], gains[index, 1]
        return Layer(lay, tables, *heads, which)

    first, second = layer(0, relative), layer(1, relative)
    out.stack(order)
    own_in, own_cot = dealt(*order(*arrived), lay)
    block = order(first.normed_rows(own_in.astype(F32)))
    others = [lay.to_member(block, step) for step in range(1, lay.group)]
    qkv_0.got = order(qkv_0.got)
    order.sent(qkv_0.over_shard, over_shard)
    order.sent(out.over_half, over_half)
    down_own = to_inner(order(w_down)[0], lay).reshape(lay.cores, ff_unit, width)
    down_other = split_cores(down_own, lay, order)
    own = order(jnp.concatenate([block] + listed(order(*others)), 0))
    first.normed = own, lay.to_core(own)
    gate_up_layers = core_layers(gate_up_own, order(gate_up_other), lay)
    gate_up_others = to_members(gate_up_layers[0], lay, order)
    if out.aligned:
        out.got = order(out.got)
    order.sent(out.over_shard, over_shard)
    qkv_0.got = order(qkv_0.got)

    def round_of(halves, shards):
        def run(arrived):
            sent = []
            for order, item in enumerate(halves):
                sent.append(item.over_half(over_half, arrived, beside=order > 0))
            for order, item in enumerate(shards):
                sent.append(item.over_shard(over_shard, arrived, beside=order > 0))
            return sent

        return run

    def attention_weights(which, qkv, out_w):
        which.qkv_w = mm(qkv.full(), spread_lanes).astype(BF16)
        which.out_w = mm_tn(spread_out, out_w).astype(BF16)

    first.qkv_w = mm(qkv_0.full(), spread_lanes).astype(BF16)
    first.attend()
    gate_up_others = listed(order(*gate_up_others))
    gate_up = member_rows(gate_up_layers[0], gate_up_others, lay)
    gate_0, up_0 = Spread(gate_up[:, :ff]), Spread(gate_up[:, ff:])
    order.sent(gate_0.over_half, over_half)
    down_layers = core_layers(down_own, order(down_other), lay)
    down_0, down_1 = Spread(down_layers[0]), Spread(down_layers[1])
    order.last = (first.attn_out[0],)
    rest = jnp.concatenate([qkv_layers[1], gate_up_layers[1]], -1)
    rest_others = to_members(rest, lay, order)
    if out.aligned:
        out.got = order(out.got)
    out_w = out.full()
    first.out_w = mm_tn(spread_out, out_w[0]).astype(BF16)
    rest = member_rows(rest, listed(order(*rest_others)), lay)
    qkv_1, gate_up_1 = Spread(rest[:, :cols]), Spread(rest[:, cols:])
    first.attn_out = [after(block, *order.last) for block in first.attn_out]
    first.attention(round_of([up_0], [gate_0]), round_of([down_0], [up_0]))
    first.gate_w, first.up_w = gate_0.full(), up_0.full()
    down_0.over_shard(over_shard)
    qkv_1.over_half(over_half, (up_0.got,))
    gate_up_1.over_half(over_half, (up_0.got,), beside=True)
    first.down_w = down_0.full()
    first.hide()
    first_out = first.feed_forward(round_of([], [qkv_1]))
    second.start(first_out.astype(BF16).astype(F32), round_of([down_1], [gate_up_1]))
    second.start_back(after(own_cot, second.normed[0]).astype(F32))
    attention_weights(second, qkv_1, out_w[1])
    second.attend()
    second.attention(round_of([], [down_1]))
    both = gate_up_1.full()
    second.gate_w, second.up_w = both[:, :ff], both[:, ff:]
    second.down_w = down_1.full()

    def gate_up_collects(which):
        left = joined(which.normed_mid)
        return Collect(left, joined(which.gate_grad)), Collect(left, joined(which.up_grad))

    def qkv_collect(which):
        low = mm_nt(joined(which.lows), spread_lanes).astype(BF16)
        return Collect(joined(which.normed), low)

    second.hide()
    down_1 = Collect(joined(second.hidden), joined(second.down_in))
    second_out = second.feed_forward(round_of([], [down_1]))
    partial = second.feed_forward_back()
    partial[0] = after(partial[0], second_out)
    grads = [jnp.concatenate(pair, 1) for pair in zip(second.gate_grad, second.up_grad)]
    gate_up_1 = Collect(joined(second.normed_mid), joined(grads))
    second.middle_back(partial, round_of([down_1], [gate_up_1]))
    partial = second.attention_back()
    qkv_1 = qkv_collect(second)
    second_grad = second.finish_back(partial, round_of([gate_up_1], [qkv_1]))

    first.start_back(second_grad.astype(BF16).astype(F32))
    down_0 = Collect(joined(first.hidden), joined(first.down_in))
    partial = first.feed_forward_back()
    partial[0] = after(partial[0], down_0.over_shard(over_shard))
    gate_0, up_0 = gate_up_collects(first)
    first.middle_back(partial, round_of([qkv_1], [gate_0]), round_of([down_0], [up_0]))
    partial = first.attention_back()
    qkv_0 = qkv_collect(first)
    last = [gate_0.over_half(over_half, (first.lows[0],))]
    last.append(up_0.over_half(over_half, (first.lows[0],), beside=True))
    partial[1] = after(partial[1], *last)
    first_grad = first.finish_back(partial)

    def by_member(*blocks):
        return jnp.concatenate(blocks, 1).reshape(lay.group, row_block, -1)

    out_both = CollectOut([out_pair(which, spread_out) for which in (first, second)], lay, row_block)
    order = Order()
    order.last = (first_grad,)
    gains, gains_other = jnp.stack([first.gain_grads, second.gain_grads]), None
    gains_other = lay.to_core(order(pick(gains, 1 - lay.core)))
    arrived = return_rows(first_grad.astype(BF16), second_out.astype(BF16), lay, order)
    gains = pick(gains, lay.core) + order(gains_other)
    gains = gains.reshape(2, lay.shards, lay.halves, lay.group, -1).transpose(1, 2, 3, 0, 4)
    gains_other = lay.to_shard(order(pick(gains, 1 - lay.shard)))
    order.sent(qkv_0.over_shard, over_shard)
    down_join = join_cores(down_0.total(order.last), down_1.total(order.last), lay, order)
    straight, crossed = order(*arrived)
    ends = two_way(lay.half ^ lay.core, straight, crossed, 0)
    mlp = [block.total(order.last) for block in (gate_up_1, qkv_1, gate_0, up_0)]
    mlp = by_member(*mlp)
    others = to_members(mlp.astype(BF16), lay, order)
    gains = pick(gains, lay.shard) + order(gains_other)
    gains_other = lay.to_half(order(pick(gains, 1 - lay.half)))
    qkv_0.got = order(qkv_0.got)
    order.sent(qkv_0.over_half, over_half)
    order.sent(out_both.over_shard, over_shard)
    down_join = joined_cores(down_join, lay, order)
    others = listed(order(*others))
    back = place(pick(mlp, lay.member), [block.astype(F32) for block in others], lay.member)
    ff_join = join_cores(back[..., cols + 2 * ff :], back[..., : 2 * ff], lay, order)
    gains = pick(gains, lay.half) + order(gains_other)
    mlp = by_member(qkv_0.total(order.last))
    others = to_members(mlp.astype(BF16), lay, order)
    gain_g = pick(gains, lay.member)
    gain_others = to_members(gains, lay, order)
    if out_both.aligned:
        out_both.got = order(out_both.got)
    order.sent(out_both.over_half, over_half)
    gate_up_g = unpack_ff(joined_cores(ff_join, lay, order), lay, ff_unit)
    others = listed(order(*others))
    back_0 = place(pick(mlp, lay.member), [block.astype(F32) for block in others], lay.member)
    qkv_join = join_cores(back_0, back[..., 2 * ff : 2 * ff + cols], lay, order)
    for block in listed(order(*gain_others)):
        gain_g = gain_g + block
    qkv_g = unpack_heads(joined_cores(qkv_join, lay, order), lay)
    out_g = to_outer(join_out(*out_both.total(order.last), lay, row_block), lay)
    down_g = to_outer(down_join.reshape(-1, width), lay)
    ends = to_outer(ends, lay)
    return (
        ends[None, :, None],
        gain_g[0][None],
        qkv_g[0][None],
        qkv_g[1][None],
        qkv_g[2][None],
        out_g[None],
        gain_g[1][None],
        gate_up_g[0][None],
        gate_up_g[1][None],
        down_g[None],
    )


def solution(mesh):
    rows = P("section", None, "shard", "ctx", None)
    vector = P("section", ("ctx", "shard"))
    matrix = P("section", ("ctx", "shard"), None)
    return jax.shard_map(
        body,
        mesh=mesh,
        in_specs=(rows, P(), vector, matrix, matrix, matrix, matrix, vector, matrix, matrix, matrix),
        out_specs=(rows, vector, matrix, matrix, matrix, matrix, vector, matrix, matrix, matrix),
        check_vma=False,
    )
```

```python
import jax
import jax.numpy as jnp
from jax import lax
from jax.experimental import pallas as pl
from jax.experimental.pallas import tpu as pltpu
from jax.sharding import PartitionSpec as P

HEADS = 16
KV_HEADS = 8
HEAD_DIM = 96
HALF = HEAD_DIM // 2
LANES = 128
HALF_LANES = LANES // 2

NORM_EPS = 1e-05
ROPE_BASE = 100000.0
MASK_FILL = -1e30

MESH_AXES = ("section", "ctx", "shard")
F32 = jnp.float32
BF16 = jnp.bfloat16
VMEM_LIMIT = pltpu.CompilerParams(vmem_limit_bytes=56 * 1024 * 1024)


class Layout:
    def __init__(self):
        self.cores = lax.axis_size("section")
        self.ctx = lax.axis_size("ctx")
        self.shards = lax.axis_size("shard")
        self.halves = 2
        self.group = self.ctx // self.halves
        ctx_index = lax.axis_index("ctx")
        self.core = lax.axis_index("section")
        self.half = ctx_index // self.group
        self.member = ctx_index % self.group
        self.shard = lax.axis_index("shard")

    def move(self, block, target):
        pairs = []
        for core in range(self.cores):
            for half in range(self.halves):
                for member in range(self.group):
                    for shard in range(self.shards):
                        to = target(core, half, member, shard)
                        pairs.append((self.flat(core, half, member, shard), self.flat(*to)))
        return lax.ppermute(block, MESH_AXES, pairs)

    def move_some(self, block, sends, target):
        pairs = []
        for core in range(self.cores):
            for half in range(self.halves):
                for member in range(self.group):
                    for shard in range(self.shards):
                        if sends(core, half, member, shard):
                            to = target(core, half, member, shard)
                            pairs.append((self.flat(core, half, member, shard), self.flat(*to)))
        return lax.ppermute(block, MESH_AXES, pairs)

    def flat(self, core, half, member, shard):
        return (core * self.ctx + half * self.group + member) * self.shards + shard

    def to_member(self, block, step):
        return self.move(block, lambda core, half, member, shard: (core, half, member ^ step, shard))

    def to_half(self, block):
        return self.move(block, lambda core, half, member, shard: (core, 1 - half, member, shard))

    def to_shard(self, block):
        return self.move(block, lambda core, half, member, shard: (core, half, member, 1 - shard))

    def to_core(self, block):
        return self.move(block, lambda core, half, member, shard: (1 - core, half, member, shard))


def pick(parts, index):
    return lax.dynamic_index_in_dim(parts, index, 0, False)


class Order:
    def __init__(self):
        self.last = ()

    def __call__(self, *blocks):
        if self.last:
            blocks = lax.optimization_barrier(tuple(blocks) + self.last)[: len(blocks)]
        self.last = (blocks[0],)
        return blocks[0] if len(blocks) == 1 else blocks

    def each(self, blocks):
        blocks = self(*blocks)
        return list(blocks) if isinstance(blocks, (tuple, list)) else [blocks]


def two_way(index, own, other, axis):
    first = jnp.where(index == 0, own, other)
    second = jnp.where(index == 0, other, own)
    return jnp.stack([first, second], axis)


def rearrange_kernel(plans, count, *refs):
    sources, outs = refs[:count], refs[count:]
    for out, plan in zip(outs, plans):
        for index, pieces in plan:
            blocks = [
                sources[source][place + (slice(None), slice(column, column + width))]
                for source, place, column, width in pieces
            ]
            out[index] = jnp.concatenate(blocks, 1) if len(blocks) > 1 else blocks[0]


def rearrange(sources, shapes, plans):
    dtype = sources[0].dtype
    moved = sum(source.size for source in sources) * dtype.itemsize
    return pl.pallas_call(
        lambda *refs: rearrange_kernel(plans, len(sources), *refs),
        out_shape=[jax.ShapeDtypeStruct(shape, dtype) for shape in shapes],
        compiler_params=VMEM_LIMIT,
        cost_estimate=pl.CostEstimate(flops=0, bytes_accessed=0, transcendentals=0),
        name="rearrange",
    )(*sources)


def kernel_width(width):
    return width % HEAD_DIM == 0 or width % LANES == 0


def to_inner(block, lay, inner=True):
    blocks = lay.shards * lay.halves * lay.group
    width = block.shape[-1] // blocks
    outer_order = [
        ((half * lay.group + member) * lay.shards + shard) * width
        for shard in range(lay.shards)
        for half in range(lay.halves)
        for member in range(lay.group)
    ]
    if kernel_width(width):
        columns = outer_order
        if not inner:
            columns = [outer_order.index(i * width) * width for i in range(blocks)]
        flat = block.reshape(-1, block.shape[-1])
        plan = [((slice(None), slice(None)), [(0, (), column, width) for column in columns])]
        return rearrange([flat], [flat.shape], [plan])[0].reshape(block.shape)
    if inner:
        parts = block.reshape(block.shape[:-1] + (lay.halves, lay.group, lay.shards, -1))
        return jnp.moveaxis(parts, -2, -4).reshape(block.shape)
    parts = block.reshape(block.shape[:-1] + (lay.shards, lay.halves, lay.group, -1))
    return jnp.moveaxis(parts, -4, -2).reshape(block.shape)


def to_outer(block, lay):
    return to_inner(block, lay, False)


def relative(block, lay):
    width = block.shape[-1] // 4
    parts = [block[..., i * width : (i + 1) * width] for i in range(4)]
    parts = [jnp.where(lay.half == 0, parts[i], parts[i ^ 1]) for i in range(4)]
    parts = [jnp.where(lay.shard == 0, parts[i], parts[i ^ 2]) for i in range(4)]
    return jnp.concatenate(parts, -1)


def head_copies(lay):
    return max(1, lay.cores * lay.group // HEADS)


def split_heads(weight, lay, heads):
    rows = weight.shape[0]
    pairs = lay.cores * lay.group
    distinct = min(pairs, heads)
    parts = weight.reshape(rows, distinct, -1).transpose(1, 0, 2)
    parts = jnp.repeat(parts, pairs // distinct, axis=0) if pairs > distinct else parts
    return parts.reshape((lay.cores, lay.group) + parts.shape[1:])


def merge_heads(parts, lay, heads):
    pairs = lay.cores * lay.group
    distinct = min(pairs, heads)
    rows = parts.shape[2]
    parts = parts.reshape(distinct, pairs // distinct, rows, -1)
    parts = jnp.sum(parts, 1) if pairs > distinct else parts[:, 0]
    return parts.transpose(1, 0, 2).reshape(rows, -1)


def split_ff(weight, lay, unit):
    rows = weight.shape[0]
    parts = weight.reshape(rows, lay.halves, lay.group, lay.shards, lay.cores, unit)
    return parts.transpose(4, 2, 0, 3, 1, 5).reshape(lay.cores, lay.group, rows, -1)


def merge_ff(parts, lay, unit):
    rows = parts.shape[2]
    parts = parts.reshape(lay.cores, lay.group, rows, lay.shards, lay.halves, unit)
    return parts.transpose(2, 4, 1, 3, 0, 5).reshape(rows, -1)


def pack_heads(query, key, value, lay):
    pairs = lay.cores * lay.group
    if pairs != KV_HEADS or query.shape[0] % 16:
        sides = [(query, HEADS), (key, KV_HEADS), (value, KV_HEADS)]
        return jnp.concatenate([split_heads(block, lay, heads) for block, heads in sides], -1)
    wide, slim = query.shape[1] // pairs, key.shape[1] // pairs
    plan = []
    for pair in range(pairs):
        pieces = [(0, (), pair * wide, wide), (1, (), pair * slim, slim), (2, (), pair * slim, slim)]
        plan.append(((pair // lay.group, pair % lay.group), pieces))
    shape = (lay.cores, lay.group, query.shape[0], wide + 2 * slim)
    return rearrange([query, key, value], [shape], [plan])[0]


def unpack_heads(parts, lay):
    pairs = lay.cores * lay.group
    q_cols = max(1, HEADS // pairs) * HEAD_DIM
    k_cols = max(1, KV_HEADS // pairs) * HEAD_DIM
    if pairs != KV_HEADS:
        sides = [(0, q_cols, HEADS), (q_cols, k_cols, KV_HEADS), (q_cols + k_cols, k_cols, KV_HEADS)]
        return [merge_heads(parts[..., at : at + cols], lay, heads) for at, cols, heads in sides]
    rows = parts.shape[2]
    plans, shapes = [], []
    for first, cols in ((0, q_cols), (q_cols, k_cols), (q_cols + k_cols, k_cols)):
        pieces = [(0, (pair // lay.group, pair % lay.group), first, cols) for pair in range(pairs)]
        plans.append([((slice(None), slice(None)), pieces)])
        shapes.append((rows, pairs * cols))
    return rearrange([parts], shapes, plans)


def ff_columns(lay, core, member, unit):
    for shard in range(lay.shards):
        for half in range(lay.halves):
            block = (half * lay.group + member) * lay.shards + shard
            yield (block * lay.cores + core) * unit, shard * lay.halves + half


def pack_ff(gate, up, lay, unit):
    if not kernel_width(unit):
        return jnp.concatenate([split_ff(gate, lay, unit), split_ff(up, lay, unit)], -1)
    plan = []
    for core in range(lay.cores):
        for member in range(lay.group):
            columns = [column for column, _ in ff_columns(lay, core, member, unit)]
            pieces = [(side, (), column, unit) for side in (0, 1) for column in columns]
            plan.append(((core, member), pieces))
    shape = (lay.cores, lay.group, gate.shape[0], 8 * unit)
    return rearrange([gate, up], [shape], [plan])[0]


def unpack_ff(parts, lay, unit):
    ff = 4 * unit
    if not kernel_width(unit):
        return [merge_ff(parts[..., :ff], lay, unit), merge_ff(parts[..., ff:], lay, unit)]
    rows = parts.shape[2]
    plans = []
    for side in (0, 1):
        found = {}
        for core in range(lay.cores):
            for member in range(lay.group):
                for column, place in ff_columns(lay, core, member, unit):
                    found[column] = (0, (core, member), side * ff + place * unit, unit)
        pieces = [found[column] for column in sorted(found)]
        plans.append([((slice(None), slice(None)), pieces)])
    return rearrange([parts], [(rows, len(found) * unit)] * 2, plans)


def place(own, others, member):
    group = 1 + len(others)
    stacked = jnp.zeros((group,) + own.shape, own.dtype)
    for step, block in enumerate((own,) + tuple(others)):
        stacked = lax.dynamic_update_index_in_dim(stacked, block, member ^ step, 0)
    return stacked


def split_cores(parts, lay, order):
    return lay.to_core(order(pick(parts, 1 - lay.core)))


def core_layers(parts, other, lay):
    kept = pick(parts, lay.core)
    return jnp.where(lay.core == 0, kept, other), jnp.where(lay.core == 0, other, kept)


def to_members(parts, lay, order):
    sent = order.each([pick(parts, lay.member ^ step) for step in range(1, lay.group)])
    return [lay.to_member(block, step) for step, block in enumerate(sent, 1)]


def member_rows(parts, others, lay):
    return place(pick(parts, lay.member), others, lay.member).reshape(-1, parts.shape[-1])


class Spread:
    def __init__(self, block, lay, order):
        self.block, self.lay, self.order = block, lay, order

    def half(self):
        self.got = self.lay.to_half(self.order(self.block))

    def half_done(self):
        self.pair = jnp.concatenate([self.block, self.order(self.got)], 0)

    def shard(self):
        self.got = self.lay.to_shard(self.order(self.pair))

    def shard_done(self):
        self.full = jnp.concatenate([self.pair, self.order(self.got)], 0)


class Collect:
    def __init__(self, left, right, lay, order):
        self.left, self.right, self.lay, self.order = left, right, lay, order
        self.rows = left.shape[1] // 4

    def shard(self):
        block = mm_tn(self.left[:, 2 * self.rows :], self.right).astype(BF16)
        self.got = self.lay.to_shard(self.order(block))

    def shard_done(self):
        self.got, self.left = self.order(self.got, self.left)

    def half(self):
        rows, got = self.rows, self.got.astype(F32)
        kept = mm_tn(self.left[:, : 2 * rows], self.right)
        self.kept = kept[:rows] + got[:rows]
        self.got = self.lay.to_half(self.order((kept[rows:] + got[rows:]).astype(BF16)))

    def half_done(self):
        self.total = self.kept + self.order(self.got).astype(F32)


def join_cores(first, second, lay, order):
    sent = order(jnp.where(lay.core == 0, second, first).astype(BF16))
    return jnp.where(lay.core == 0, first, second), lay.to_core(sent)


def joined_cores(pair, lay, order):
    return two_way(lay.core, pair[0], order(pair[1]).astype(F32), 0)


def out_aligned(lay, block_rows):
    return block_rows == HEAD_DIM and lay.cores * lay.group == KV_HEADS and lay.cores == lay.halves


class SpreadOut:
    def __init__(self, w_out, lay, order):
        self.lay, self.order, self.width = lay, order, w_out.shape[-1]
        self.aligned = out_aligned(lay, w_out.shape[0])
        if not self.aligned:
            w_out = lax.all_gather(w_out, MESH_AXES[1:], axis=0, tiled=True)
        self.own = w_out

    def core(self):
        self.got = self.lay.to_core(self.order(self.own))

    def core_done(self):
        lay, other = self.lay, self.order(self.got)
        self.block = jnp.stack(
            [jnp.where(lay.core == 0, self.own, other), jnp.where(lay.core == 0, other, self.own)]
        )

    def half(self):
        if self.aligned:
            self.got = self.lay.move_some(
                self.order(self.block),
                lambda core, half, member, shard: half == core,
                lambda core, half, member, shard: (core, 1 - half, member, shard),
            )

    def half_done(self):
        if self.aligned:
            lay = self.lay
            self.block = jnp.where(lay.half == lay.core, self.block, self.order(self.got))

    def shard(self):
        if self.aligned:
            self.got = self.lay.to_shard(self.order(self.block))

    def shard_done(self):
        if self.aligned:
            self.full = jnp.concatenate([self.block, self.order(self.got)], 1)
            return
        lay = self.lay
        head = (lay.core * lay.group + lay.member) // head_copies(lay)
        count = max(1, HEADS // (lay.cores * lay.group)) * HEAD_DIM
        self.full = lax.dynamic_slice_in_dim(self.block, head * count, count, 1)


def out_pair(which, spread_out):
    return mm_nt(joined(which.attn_out), spread_out).astype(BF16), joined(which.mid_low)


class CollectOut:
    def __init__(self, pairs, lay, order, block_rows):
        self.pairs, self.lay, self.order = pairs, lay, order
        self.aligned = out_aligned(lay, block_rows)
        self.rows = pairs[0][0].shape[1] // 2

    def shard(self):
        if not self.aligned:
            self.total = [mm_tn(left, right) for left, right in self.pairs]
            return
        blocks = [mm_tn(left[:, self.rows :], right).astype(BF16) for left, right in self.pairs]
        self.got = self.lay.to_shard(self.order(jnp.concatenate(blocks, 0)))

    def shard_done(self):
        if self.aligned:
            self.got = self.order(self.got)

    def half(self):
        if not self.aligned:
            return
        blocks = [mm_tn(left[:, : self.rows], right) for left, right in self.pairs]
        self.kept = jnp.concatenate(blocks, 0) + self.got.astype(F32)
        self.got = self.lay.move_some(
            self.order(self.kept.astype(BF16)),
            lambda core, half, member, shard: half != core,
            lambda core, half, member, shard: (core, 1 - half, member, shard),
        )

    def half_done(self):
        if self.aligned:
            total = self.kept + self.order(self.got).astype(F32)
            self.total = total[: self.rows], total[self.rows :]


def join_out_start(first, second, lay, order, block_rows):
    if not out_aligned(lay, block_rows):
        width = first.shape[1]
        head = (lay.core * lay.group + lay.member) // head_copies(lay)
        full = jnp.zeros((2, HEADS * HEAD_DIM, width), F32)
        full = lax.dynamic_update_slice_in_dim(
            full, jnp.stack([first, second]), head * first.shape[0], 1
        )
        full = pick(lax.psum(full, MESH_AXES), lay.core)
        block = (lay.half * lay.group + lay.member) * lay.shards + lay.shard
        return lax.dynamic_slice_in_dim(full, block * block_rows, block_rows, 0), None
    return join_cores(first, second, lay, order)


def join_out(pair, lay, order):
    kept, other = pair
    if other is None:
        return kept
    return jnp.where(lay.half == lay.core, kept, order(other).astype(F32))


def lane_matrix(heads):
    source = jnp.arange(heads * HEAD_DIM)
    head, offset = source // HEAD_DIM, source % HEAD_DIM
    target = head * LANES + (offset // HALF) * HALF_LANES + offset % HALF
    return (target[:, None] == jnp.arange(heads * LANES)[None, :]).astype(BF16)


def rot(vec, cos_t, sin_t):
    return vec * cos_t + pltpu.roll(vec, HALF_LANES, 1) * sin_t


def rot_back(vec, cos_t, sin_t):
    return vec * cos_t - pltpu.roll(vec, HALF_LANES, 1) * sin_t


def mm(a, b):
    return lax.dot_general(a, b, (((1,), (0,)), ((), ())), preferred_element_type=F32)


def mm_nt(a, b):
    return lax.dot_general(a, b, (((1,), (1,)), ((), ())), preferred_element_type=F32)


def mm_tn(a, b):
    return lax.dot_general(a, b, (((0,), (0,)), ((), ())), preferred_element_type=F32)


def heads_of(block, count):
    return jnp.concatenate([block[:, i * LANES : (i + 1) * LANES] for i in range(count)], 0)


def lanes_of(index, count=1):
    return slice(index * LANES, (index + count) * LANES)


def attend_kernel(
    n_query, n_key, raw_own, raw_sib, cos_t, sin_t, pos_q, pos_k, out_own, out_sib, lse_out, own, sib
):
    scale = HEAD_DIM ** (-0.5)
    per_key = n_query // n_key
    half = raw_own.shape[0]
    rows = 2 * half
    cos_v, sin_v = cos_t[...], sin_t[...]
    mask = pos_q[...] >= pos_k[...]
    mask = jnp.concatenate([mask] * per_key, 0)

    def both(index, turned):
        block = jnp.concatenate([raw_own[:, lanes_of(index)], raw_sib[:, lanes_of(index)]], 0)
        block = (rot(block, cos_v, sin_v) if turned else block).astype(BF16)
        own[:, lanes_of(index)] = block[:half]
        sib[:, lanes_of(index)] = block[half:]
        return block

    for kv_head in range(n_key):
        key, value = both(n_query + kv_head, True), both(n_query + n_key + kv_head, False)
        q_first = kv_head * per_key
        query = jnp.concatenate([both(q_first + i, True) for i in range(per_key)], 0)
        scores = jnp.where(mask, mm_nt(query, key) * scale, MASK_FILL)
        row_max = jnp.max(scores, -1, keepdims=True)
        weights = jnp.exp(scores - row_max)
        total = jnp.sum(weights, -1, keepdims=True)
        probs = (weights * (1.0 / total)).astype(BF16)
        out = mm(probs, value).astype(BF16)
        for i in range(per_key):
            out_own[:, lanes_of(q_first + i)] = out[i * rows : i * rows + half]
            out_sib[:, lanes_of(q_first + i)] = out[i * rows + half : (i + 1) * rows]
        lse_out[kv_head] = row_max + jnp.log(total)


def attend(raw_own, raw_sib, tables, n_query, n_key):
    half, lanes = raw_own.shape
    return pl.pallas_call(
        lambda *refs: attend_kernel(n_query, n_key, *refs),
        out_shape=[
            jax.ShapeDtypeStruct((half, n_query * LANES), BF16),
            jax.ShapeDtypeStruct((half, n_query * LANES), BF16),
            jax.ShapeDtypeStruct((n_key, n_query // n_key * 2 * half, 1), F32),
            jax.ShapeDtypeStruct((half, lanes), BF16),
            jax.ShapeDtypeStruct((half, lanes), BF16),
        ],
        compiler_params=VMEM_LIMIT,
        cost_estimate=pl.CostEstimate(flops=0, bytes_accessed=0, transcendentals=0),
        name="attend",
    )(raw_own, raw_sib, *tables)


def attend_back_kernel(
    n_query, n_key, own, sib, do_own, do_sib, lse, cos_t, sin_t, pos_q, pos_k, low_own, low_sib
):
    scale = HEAD_DIM ** (-0.5)
    per_key = n_query // n_key
    half = own.shape[0]
    rows = 2 * half
    cos_v, sin_v = cos_t[...], sin_t[...]
    mask = pos_q[...] >= pos_k[...]
    mask = jnp.concatenate([mask] * per_key, 0)

    def put(index, block):
        low_own[:, lanes_of(index)] = block[:half].astype(BF16)
        low_sib[:, lanes_of(index)] = block[half:].astype(BF16)

    def both(a, b, index):
        return jnp.concatenate([a[:, lanes_of(index)], b[:, lanes_of(index)]], 0)

    for kv_head in range(n_key):
        key, value = both(own, sib, n_query + kv_head), both(own, sib, n_query + n_key + kv_head)
        q_first = kv_head * per_key
        query = jnp.concatenate([both(own, sib, q_first + i) for i in range(per_key)], 0)
        grad = jnp.concatenate([both(do_own, do_sib, q_first + i) for i in range(per_key)], 0)
        scores = jnp.where(mask, mm_nt(query, key) * scale, MASK_FILL)
        probs = jnp.exp(scores - lse[kv_head])
        prob_grad = mm_nt(grad, value)
        delta = jnp.sum(probs * prob_grad, -1, keepdims=True)
        score_grad = (probs * (prob_grad - delta)).astype(BF16)
        dq = mm(score_grad, key) * scale
        for i in range(per_key):
            put(q_first + i, rot_back(dq[i * rows : (i + 1) * rows], cos_v, sin_v))
        put(n_query + kv_head, rot_back(mm_tn(score_grad, query) * scale, cos_v, sin_v))
        put(n_query + n_key + kv_head, mm_tn(probs.astype(BF16), grad))


def attend_back(kept, out_grads, tables, n_query, n_key):
    own, sib, lse = kept
    half, lanes = own.shape
    return pl.pallas_call(
        lambda *refs: attend_back_kernel(n_query, n_key, *refs),
        out_shape=[
            jax.ShapeDtypeStruct((half, lanes), BF16),
            jax.ShapeDtypeStruct((half, lanes), BF16),
        ],
        compiler_params=VMEM_LIMIT,
        cost_estimate=pl.CostEstimate(flops=0, bytes_accessed=0, transcendentals=0),
        name="attend_back",
    )(own, sib, *out_grads, lse, *tables)


def rows_start(block, lay, order):
    block = order(block)
    return block, [lay.to_member(block, step) for step in range(1, lay.group)]


def rows_middle(begun, lay, order):
    block, others = begun
    own = order(jnp.concatenate([block] + order.each(others), 0))
    return [own, lay.to_core(own)]


def rows_done(rows, order):
    rows[1] = order(rows[1])
    return rows


def sums_start(own, sib, lay, order):
    return own, lay.to_core(order(sib.astype(BF16)))


def sums_middle(begun, lay, order):
    own, got = begun
    own = own + order(got).astype(F32)
    rows = own.shape[0] // lay.group
    parts = own.reshape(lay.group, rows, -1)
    sent = order.each([parts[step].astype(BF16) for step in range(1, lay.group)])
    return parts[0], [lay.to_member(block, step) for step, block in enumerate(sent, 1)]


def sums_done(begun, order):
    total, others = begun
    for block in order.each(others):
        total = total + block.astype(F32)
    return total


def norm_forward(inputs, gain_vec):
    inverse_rms = lax.rsqrt(jnp.mean(inputs * inputs, -1, keepdims=True) + NORM_EPS)
    return (inputs * inverse_rms * gain_vec).astype(BF16), inverse_rms


def norm_backward(inputs, inverse_rms, gain_vec, upstream):
    scaled = upstream * gain_vec
    input_grad = inverse_rms * scaled - inputs * inverse_rms**3 * jnp.mean(
        scaled * inputs, -1, keepdims=True
    )
    gain_grad = jnp.sum(upstream * inputs * inverse_rms, 0)
    return input_grad, gain_grad


def out_order(block, lay, n_query):
    if head_copies(lay) > 1:
        share = (lay.core * lay.group + lay.member) % head_copies(lay) == 0
        return jnp.where(share, block, jnp.zeros_like(block))
    if n_query != 2 or lay.cores * lay.group != KV_HEADS:
        return block
    swapped = jnp.concatenate([block[:, LANES:], block[:, :LANES]], 1)
    return jnp.where(lay.shard == 0, block, swapped)


class Layer:
    def __init__(self, lay, tables, n_query, n_key, gain_one, gain_two):
        self.lay, self.tables, self.n_query, self.n_key = lay, tables, n_query, n_key
        self.gain_one, self.gain_two = gain_one, gain_two

    def first_norm(self, inputs):
        self.inputs = inputs
        normed, self.inverse_first = norm_forward(inputs, self.gain_one)
        return relative(normed, self.lay)

    def attend(self):
        raw = [mm(block, self.qkv_w) for block in self.normed]
        out_own, out_sib, lse, own, sib = attend(*raw, self.tables, self.n_query, self.n_key)
        self.attn_kept = own, sib, lse
        self.attn_out = [out_order(block, self.lay, self.n_query) for block in (out_own, out_sib)]

    def out_partial(self):
        return [mm(block, self.out_w) for block in self.attn_out]

    def second_norm(self, attended):
        self.mid_stream = self.inputs + attended
        normed, self.inverse_second = norm_forward(self.mid_stream, self.gain_two)
        return relative(normed, self.lay)

    def hide(self):
        self.gate_up, self.hidden = [], []
        for block in self.normed_mid:
            gate_pre, up_pre = mm(block, self.gate_w), mm(block, self.up_w)
            self.gate_up.append((gate_pre, up_pre))
            hidden = (jax.nn.silu(gate_pre) * up_pre).astype(BF16)
            self.hidden.append(relative(hidden, self.lay))

    def down_partial(self):
        return [mm(block, self.down_w) for block in self.hidden]

    def feed_forward_back(self):
        self.gate_grad, self.up_grad, partial = [], [], []
        for block, (gate_pre, up_pre) in zip(self.down_in, self.gate_up):
            hidden_grad = relative(mm_nt(block, self.down_w), self.lay)
            sigmoid_gate = jax.nn.sigmoid(gate_pre)
            gate_grad_in = (
                hidden_grad * up_pre * sigmoid_gate * (1.0 + gate_pre * (1.0 - sigmoid_gate))
            ).astype(BF16)
            up_grad_in = (hidden_grad * gate_pre * sigmoid_gate).astype(BF16)
            self.gate_grad.append(gate_grad_in)
            self.up_grad.append(up_grad_in)
            partial.append(mm_nt(gate_grad_in, self.gate_w) + mm_nt(up_grad_in, self.up_w))
        return partial

    def second_norm_back(self, out_grad, upstream):
        part, self.gain_two_grad = norm_backward(
            self.mid_stream, self.inverse_second, self.gain_two, relative(upstream, self.lay)
        )
        self.mid_grad = out_grad + part
        return self.mid_grad.astype(BF16)

    def attention_back(self):
        grads = [
            out_order(mm_nt(block, self.out_w).astype(BF16), self.lay, self.n_query)
            for block in self.mid_low
        ]
        self.lows = attend_back(self.attn_kept, grads, self.tables, self.n_query, self.n_key)
        return [mm_nt(block, self.qkv_w) for block in self.lows]

    def first_norm_back(self, upstream):
        part, gain_one_grad = norm_backward(
            self.inputs, self.inverse_first, self.gain_one, relative(upstream, self.lay)
        )
        self.gain_grads = jnp.stack([gain_one_grad, self.gain_two_grad])
        return self.mid_grad + part


def joined(pair):
    return jnp.concatenate(pair, 0)


def row_tables(pair_table, block_rows, lay):
    cores = []
    for core in (lay.core, 1 - lay.core):
        ctx_ids = jnp.stack([core * lay.group + (lay.member ^ step) for step in range(lay.group)])
        owned = jnp.sum(
            jnp.where(ctx_ids[:, None] == jnp.arange(lay.ctx)[None, :], pair_table[None, :], 0), 1
        )
        blocks = jnp.stack([owned, 2 * lay.ctx - 1 - owned], 1)
        rows = blocks[:, :, None] * block_rows + jnp.arange(block_rows)[None, None, :]
        cores.append(rows.reshape(-1))
    positions = jnp.concatenate(cores)
    freq_idx = jnp.arange(HALF, dtype=F32)
    inverse = ROPE_BASE ** (-2.0 * freq_idx / HEAD_DIM)
    angles = positions.astype(F32)[:, None] * inverse[None, :]
    pad = ((0, 0), (0, HALF_LANES - HALF))
    cos_h, sin_h = jnp.pad(jnp.cos(angles), pad), jnp.pad(jnp.sin(angles), pad)
    cos_t = jnp.concatenate([cos_h, cos_h], 1)
    sin_t = jnp.concatenate([-sin_h, sin_h], 1)
    return cos_t, sin_t, positions[:, None], positions[None, :]


def deal_rows(local, lay, order):
    turn = lay.half ^ lay.core
    sent = order(pick(local, turn), pick(local, 1 - turn))
    straight = lay.move(
        sent[0], lambda core, half, member, shard: (half, half ^ core, member, shard)
    )
    crossed = lay.move(
        sent[1], lambda core, half, member, shard: (half, 1 - (half ^ core), member, shard)
    )
    return straight, crossed


def dealt(straight, crossed, lay):
    turn = lay.half ^ lay.core
    return jnp.where(turn == 0, straight, crossed), jnp.where(turn == 0, crossed, straight)


def return_rows(input_grad, outputs, lay, order):
    turn = lay.half ^ lay.core
    sent = order(
        jnp.where(turn == 0, input_grad, outputs), jnp.where(turn == 0, outputs, input_grad)
    )
    straight = lay.move(
        sent[0], lambda core, half, member, shard: (core ^ half, core, member, shard)
    )
    crossed = lay.move(
        sent[1], lambda core, half, member, shard: (1 - (core ^ half), core, member, shard)
    )
    return straight, crossed


def body(
    ends_in, pair_table, norm_attn, w_query, w_key, w_value, w_out, norm_mlp, w_gate, w_up, w_down
):
    lay = Layout()
    rows = ends_in.shape[3]
    width = ends_in.shape[4]
    row_block = w_query.shape[1]
    pairs = lay.cores * lay.group
    n_query = max(1, HEADS // pairs)
    n_key = max(1, KV_HEADS // pairs)
    ff_unit = w_down.shape[1] // lay.cores
    q_cols, k_cols = n_query * HEAD_DIM, n_key * HEAD_DIM
    spread_lanes = lane_matrix(n_query + 2 * n_key)
    spread_out = lane_matrix(n_query)
    cols = q_cols + 2 * k_cols
    ff = ff_unit * 4
    order = Order()

    def by_member(*blocks):
        return jnp.concatenate(blocks, 1).reshape(lay.group, row_block, -1)

    tables = row_tables(pair_table, rows // 2, lay)
    gains = jnp.stack([norm_attn[0], norm_mlp[0]])
    gain_parts = [lay.to_member(gains, step) for step in range(1, lay.group)]
    heads = pack_heads(w_query[0], w_key[0], w_value[0], lay)
    heads_other = split_cores(heads, lay, order)
    heads_other, *gain_parts = order(heads_other, *gain_parts)
    qkv_layers = core_layers(heads, heads_other, lay)
    qkv_others = to_members(qkv_layers[0], lay, order)
    gains = order(place(gains, gain_parts, lay.member))
    gains_other = lay.to_half(gains)
    w_gate, w_up, ends_in = order(w_gate, w_up, ends_in)
    own_rows = to_inner(ends_in[0, :, 0], lay)
    gate_up_own = pack_ff(w_gate[0], w_up[0], lay, ff_unit)
    gate_up_other = split_cores(gate_up_own, lay, order)
    rows_other = deal_rows(own_rows, lay, order)
    qkv_0 = Spread(member_rows(qkv_layers[0], order.each(qkv_others), lay), lay, order)
    qkv_0.half()
    gains = order(two_way(lay.half, gains, order(gains_other), 0))
    gains_other = lay.to_shard(gains)
    gains = order(two_way(lay.shard, gains, order(gains_other), 0))
    gains_other = lay.to_core(gains)
    out = SpreadOut(to_inner(order(w_out)[0], lay), lay, order)
    out.core()
    gains = two_way(lay.core, gains, order(gains_other), 0)
    gains = gains.transpose(0, 4, 1, 2, 3, 5).reshape(2, 2, -1).astype(F32)
    gate_up_layers = core_layers(gate_up_own, order(gate_up_other), lay)
    out.core_done()
    own_in, own_cot = dealt(*order(*rows_other), lay)
    first = Layer(lay, tables, n_query, n_key, gains[0, 0], gains[0, 1])
    second = Layer(lay, tables, n_query, n_key, gains[1, 0], gains[1, 1])
    normed = rows_start(first.first_norm(own_in.astype(F32)), lay, order)
    qkv_0.half_done()
    qkv_0.shard()
    out.half()
    normed = rows_middle(normed, lay, order)
    gate_up_others = to_members(gate_up_layers[0], lay, order)
    qkv_0.shard_done()
    out.half_done()
    out.shard()
    first.qkv_w = mm(qkv_0.full, spread_lanes).astype(BF16)
    first.normed = rows_done(normed, order)
    first.attend()
    first.attn_out = order.each(first.attn_out)
    gate_up = member_rows(gate_up_layers[0], order.each(gate_up_others), lay)
    gate_0 = Spread(gate_up[:, :ff], lay, order)
    up_0 = Spread(gate_up[:, ff:], lay, order)
    gate_0.half()
    down_own = to_inner(order(w_down)[0], lay).reshape(lay.cores, ff_unit, width)
    down_other = split_cores(down_own, lay, order)
    out.shard_done()
    first.out_w = mm_tn(spread_out, out.full[0]).astype(BF16)
    second.out_w = mm_tn(spread_out, out.full[1]).astype(BF16)
    sums = sums_middle(sums_start(*first.out_partial(), lay, order), lay, order)
    down_layers = core_layers(down_own, order(down_other), lay)
    down_0, down_1 = Spread(down_layers[0], lay, order), Spread(down_layers[1], lay, order)
    attended = sums_done(sums, order)
    gate_0.half_done()
    gate_0.shard()
    up_0.half()
    normed = rows_start(first.second_norm(attended), lay, order)
    normed = rows_middle(normed, lay, order)
    rest = jnp.concatenate([qkv_layers[1], gate_up_layers[1]], -1)
    rest_others = to_members(rest, lay, order)
    up_0.half_done()
    gate_0.shard_done()
    up_0.shard()
    down_0.half()
    first.normed_mid = rows_done(normed, order)
    rest = member_rows(rest, order.each(rest_others), lay)
    qkv_1 = Spread(rest[:, :cols], lay, order)
    gate_up_1 = Spread(rest[:, cols:], lay, order)
    up_0.shard_done()
    down_0.half_done()
    down_0.shard()
    qkv_1.half()
    own_cot = own_cot.astype(F32)
    cot = rows_start(own_cot.astype(BF16), lay, order)
    first.gate_w, first.up_w = gate_0.full, up_0.full
    first.hide()
    second.down_in = rows_middle(cot, lay, order)
    qkv_1.half_done()
    gate_up_1.half()
    down_0.shard_done()
    qkv_1.shard()
    first.down_w = down_0.full
    sums = sums_middle(sums_start(*first.down_partial(), lay, order), lay, order)
    first_out = first.mid_stream + sums_done(sums, order)
    normed = rows_start(second.first_norm(first_out.astype(BF16).astype(F32)), lay, order)
    normed = rows_middle(normed, lay, order)
    gate_up_1.half_done()
    gate_up_1.shard()
    down_1.half()
    qkv_1.shard_done()
    second.qkv_w = mm(qkv_1.full, spread_lanes).astype(BF16)
    second.normed = rows_done(normed, order)
    second.attend()
    sums = sums_start(*second.out_partial(), lay, order)
    sums = sums_middle(sums, lay, order)
    attended = sums_done(sums, order)
    gate_up_1.shard_done()
    down_1.half_done()
    down_1.shard()
    normed = rows_start(second.second_norm(attended), lay, order)
    normed = rows_middle(normed, lay, order)
    second.gate_w, second.up_w = gate_up_1.full[:, :ff], gate_up_1.full[:, ff:]
    second.normed_mid = rows_done(normed, order)
    second.down_in = rows_done(second.down_in, order)
    second.hide()

    down_g1 = Collect(joined(second.hidden), joined(second.down_in), lay, order)
    down_g1.shard()
    down_1.shard_done()
    second.down_w = down_1.full
    partial = second.feed_forward_back()
    sums = sums_start(*partial, lay, order)
    grads = [jnp.concatenate(pair, 1) for pair in zip(second.gate_grad, second.up_grad)]
    gate_up_g1 = Collect(joined(second.normed_mid), joined(grads), lay, order)
    sums = sums_middle(sums, lay, order)
    gate_up_g1.shard()
    upstream = sums_done(sums, order)
    low = second.second_norm_back(own_cot, upstream)
    down_g1.shard_done()
    low = rows_start(low, lay, order)
    low = rows_middle(low, lay, order)
    down_g1.half()
    outputs = sums_start(*second.down_partial(), lay, order)
    second.mid_low = rows_done(low, order)
    outputs = sums_middle(outputs, lay, order)
    partial = second.attention_back()
    sums = sums_start(*partial, lay, order)
    second_out = second.mid_stream + sums_done(outputs, order)
    low = mm_nt(joined(second.lows), spread_lanes).astype(BF16)
    qkv_g1 = Collect(joined(second.normed), low, lay, order)
    gate_up_g1.shard_done()
    qkv_g1.shard()
    sums = sums_middle(sums, lay, order)
    upstream = sums_done(sums, order)
    down_g1.half_done()
    gate_up_g1.half()
    second_grad = second.first_norm_back(upstream)

    first_cot = second_grad.astype(BF16)
    down_in = rows_start(first_cot, lay, order)
    down_in = rows_middle(down_in, lay, order)
    first.down_in = rows_done(down_in, order)
    down_g0 = Collect(joined(first.hidden), joined(first.down_in), lay, order)
    qkv_g1.shard_done()
    down_g0.shard()
    partial = first.feed_forward_back()
    sums = sums_start(*partial, lay, order)
    left = joined(first.normed_mid)
    gate_g0 = Collect(left, joined(first.gate_grad), lay, order)
    up_g0 = Collect(left, joined(first.up_grad), lay, order)
    gate_up_g1.half_done()
    qkv_g1.half()
    sums = sums_middle(sums, lay, order)
    upstream = sums_done(sums, order)
    low = rows_start(first.second_norm_back(first_cot.astype(F32), upstream), lay, order)
    down_g0.shard_done()
    gate_g0.shard()
    qkv_g1.half_done()
    down_g0.half()
    low = rows_middle(low, lay, order)
    first.mid_low = rows_done(low, order)
    mlp_1 = by_member(gate_up_g1.total)
    others_1 = to_members(mlp_1.astype(BF16), lay, order)
    partial = first.attention_back()
    first.lows = order.each(first.lows)
    others_1 = order.each(others_1)
    gate_g0.shard_done()
    up_g0.shard()
    down_g0.half_done()
    gate_g0.half()
    sums = sums_start(*partial, lay, order)
    low = mm_nt(joined(first.lows), spread_lanes).astype(BF16)
    qkv_g0 = Collect(joined(first.normed), low, lay, order)
    sums = sums_middle(sums, lay, order)
    upstream = sums_done(sums, order)
    first_grad = first.first_norm_back(upstream)

    out_both = CollectOut(
        [out_pair(which, spread_out) for which in (first, second)], lay, order, row_block
    )
    up_g0.shard_done()
    up_g0.half()
    qkv_g0.shard()
    out_both.shard()
    gains = jnp.stack([first.gain_grads, second.gain_grads])
    gains_other = lay.to_core(order(pick(gains, 1 - lay.core)))
    gate_g0.half_done()
    down_join = join_cores(down_g0.total, down_g1.total, lay, order)
    gains = pick(gains, lay.core) + order(gains_other)
    gains = gains.reshape(2, lay.shards, lay.halves, lay.group, -1).transpose(1, 2, 3, 0, 4)
    gains_other = lay.to_shard(order(pick(gains, 1 - lay.shard)))
    down_g = to_outer(joined_cores(down_join, lay, order).reshape(-1, width), lay)
    back_1 = place(pick(mlp_1, lay.member), [block.astype(F32) for block in others_1], lay.member)
    qkv_g0.shard_done()
    up_g0.half_done()
    qkv_g0.half()
    mlp_0 = by_member(gate_g0.total, up_g0.total)
    others_0 = to_members(mlp_0.astype(BF16), lay, order)
    rows_other = return_rows(first_grad.astype(BF16), second_out.astype(BF16), lay, order)
    others_0 = order.each(others_0)
    back_0 = place(pick(mlp_0, lay.member), [block.astype(F32) for block in others_0], lay.member)
    ff_join = join_cores(back_0, back_1, lay, order)
    out_both.shard_done()
    out_both.half()
    gains = pick(gains, lay.shard) + order(gains_other)
    gains_other = lay.to_half(order(pick(gains, 1 - lay.half)))
    gate_up_g = order.each(unpack_ff(joined_cores(ff_join, lay, order), lay, ff_unit))
    qkv_g0.half_done()
    attn = by_member(qkv_g0.total, qkv_g1.total)
    others_q = to_members(attn.astype(BF16), lay, order)
    straight, crossed = order(*rows_other)
    ends = two_way(lay.half ^ lay.core, straight, crossed, 0)
    others_q = order.each(others_q)
    back_q = place(pick(attn, lay.member), [block.astype(F32) for block in others_q], lay.member)
    qkv_join = join_cores(back_q[..., :cols], back_q[..., cols:], lay, order)
    gains = pick(gains, lay.half) + order(gains_other)
    gain_g = pick(gains, lay.member)
    gain_others = to_members(gains, lay, order)
    qkv_g = unpack_heads(joined_cores(qkv_join, lay, order), lay)
    out_both.half_done()
    out_join = join_out_start(*out_both.total, lay, order, row_block)
    for block in order.each(gain_others):
        gain_g = gain_g + block
    out_g = to_outer(join_out(out_join, lay, order), lay)
    ends = to_outer(ends, lay)
    return (
        ends[None, :, None],
        gain_g[0][None],
        qkv_g[0][None],
        qkv_g[1][None],
        qkv_g[2][None],
        out_g[None],
        gain_g[1][None],
        gate_up_g[0][None],
        gate_up_g[1][None],
        down_g[None],
    )


def solution(mesh):
    rows = P("section", None, "shard", "ctx", None)
    vector = P("section", ("ctx", "shard"))
    matrix = P("section", ("ctx", "shard"), None)
    return jax.shard_map(
        body,
        mesh=mesh,
        in_specs=(rows, P(), vector, matrix, matrix, matrix, matrix, vector, matrix, matrix, matrix),
        out_specs=(rows, vector, matrix, matrix, matrix, matrix, vector, matrix, matrix, matrix),
        check_vma=False,
    )
```

```python
import jax
import jax.numpy as jnp
from jax import lax
from jax.experimental import pallas as pl
from jax.experimental.pallas import tpu as pltpu
from jax.sharding import PartitionSpec as P

HEADS = 16
KV_HEADS = 8
HEAD_DIM = 96
HALF = HEAD_DIM // 2
LANES = 128
HALF_LANES = LANES // 2

NORM_EPS = 1e-05
ROPE_BASE = 100000.0
MASK_FILL = -1e30

MESH_AXES = ("section", "ctx", "shard")
F32 = jnp.float32
BF16 = jnp.bfloat16
VMEM_LIMIT = pltpu.CompilerParams(vmem_limit_bytes=56 * 1024 * 1024)


class Layout:
    def __init__(self):
        self.cores = lax.axis_size("section")
        self.ctx = lax.axis_size("ctx")
        self.shards = lax.axis_size("shard")
        self.halves = 2
        self.group = self.ctx // self.halves
        ctx_index = lax.axis_index("ctx")
        self.core = lax.axis_index("section")
        self.half = ctx_index // self.group
        self.member = ctx_index % self.group
        self.shard = lax.axis_index("shard")

    def move(self, block, target):
        pairs = []
        for core in range(self.cores):
            for half in range(self.halves):
                for member in range(self.group):
                    for shard in range(self.shards):
                        to = target(core, half, member, shard)
                        pairs.append((self.flat(core, half, member, shard), self.flat(*to)))
        return lax.ppermute(block, MESH_AXES, pairs)

    def move_some(self, block, sends, target):
        pairs = []
        for core in range(self.cores):
            for half in range(self.halves):
                for member in range(self.group):
                    for shard in range(self.shards):
                        if sends(core, half, member, shard):
                            to = target(core, half, member, shard)
                            pairs.append((self.flat(core, half, member, shard), self.flat(*to)))
        return lax.ppermute(block, MESH_AXES, pairs)

    def flat(self, core, half, member, shard):
        return (core * self.ctx + half * self.group + member) * self.shards + shard

    def to_member(self, block, step):
        return self.move(block, lambda core, half, member, shard: (core, half, member ^ step, shard))

    def to_half(self, block):
        return self.move(block, lambda core, half, member, shard: (core, 1 - half, member, shard))

    def to_shard(self, block):
        return self.move(block, lambda core, half, member, shard: (core, half, member, 1 - shard))

    def to_core(self, block):
        return self.move(block, lambda core, half, member, shard: (1 - core, half, member, shard))


def pick(parts, index):
    return lax.dynamic_index_in_dim(parts, index, 0, False)


class Order:
    def __init__(self):
        self.last = ()

    def __call__(self, *blocks):
        if self.last:
            blocks = lax.optimization_barrier(tuple(blocks) + self.last)[: len(blocks)]
        self.last = (blocks[0],)
        return blocks[0] if len(blocks) == 1 else blocks

    def each(self, blocks):
        blocks = self(*blocks)
        return list(blocks) if isinstance(blocks, (tuple, list)) else [blocks]


def two_way(index, own, other, axis):
    first = jnp.where(index == 0, own, other)
    second = jnp.where(index == 0, other, own)
    return jnp.stack([first, second], axis)


def rearrange_kernel(plans, count, *refs):
    sources, outs = refs[:count], refs[count:]
    for out, plan in zip(outs, plans):
        for index, pieces in plan:
            blocks = [
                sources[source][place + (slice(None), slice(column, column + width))]
                for source, place, column, width in pieces
            ]
            out[index] = jnp.concatenate(blocks, 1) if len(blocks) > 1 else blocks[0]


def rearrange(sources, shapes, plans):
    dtype = sources[0].dtype
    moved = sum(source.size for source in sources) * dtype.itemsize
    return pl.pallas_call(
        lambda *refs: rearrange_kernel(plans, len(sources), *refs),
        out_shape=[jax.ShapeDtypeStruct(shape, dtype) for shape in shapes],
        compiler_params=VMEM_LIMIT,
        cost_estimate=pl.CostEstimate(flops=0, bytes_accessed=0, transcendentals=0),
        name="rearrange",
    )(*sources)


def kernel_width(width):
    return width % HEAD_DIM == 0 or width % LANES == 0


def to_inner(block, lay, inner=True):
    blocks = lay.shards * lay.halves * lay.group
    width = block.shape[-1] // blocks
    outer_order = [
        ((half * lay.group + member) * lay.shards + shard) * width
        for shard in range(lay.shards)
        for half in range(lay.halves)
        for member in range(lay.group)
    ]
    if kernel_width(width):
        columns = outer_order
        if not inner:
            columns = [outer_order.index(i * width) * width for i in range(blocks)]
        flat = block.reshape(-1, block.shape[-1])
        plan = [((slice(None), slice(None)), [(0, (), column, width) for column in columns])]
        return rearrange([flat], [flat.shape], [plan])[0].reshape(block.shape)
    if inner:
        parts = block.reshape(block.shape[:-1] + (lay.halves, lay.group, lay.shards, -1))
        return jnp.moveaxis(parts, -2, -4).reshape(block.shape)
    parts = block.reshape(block.shape[:-1] + (lay.shards, lay.halves, lay.group, -1))
    return jnp.moveaxis(parts, -4, -2).reshape(block.shape)


def to_outer(block, lay):
    return to_inner(block, lay, False)


def relative(block, lay):
    width = block.shape[-1] // 4
    parts = [block[..., i * width : (i + 1) * width] for i in range(4)]
    parts = [jnp.where(lay.half == 0, parts[i], parts[i ^ 1]) for i in range(4)]
    parts = [jnp.where(lay.shard == 0, parts[i], parts[i ^ 2]) for i in range(4)]
    return jnp.concatenate(parts, -1)


def head_copies(lay):
    return max(1, lay.cores * lay.group // HEADS)


def split_heads(weight, lay, heads):
    rows = weight.shape[0]
    pairs = lay.cores * lay.group
    distinct = min(pairs, heads)
    parts = weight.reshape(rows, distinct, -1).transpose(1, 0, 2)
    parts = jnp.repeat(parts, pairs // distinct, axis=0) if pairs > distinct else parts
    return parts.reshape((lay.cores, lay.group) + parts.shape[1:])


def merge_heads(parts, lay, heads):
    pairs = lay.cores * lay.group
    distinct = min(pairs, heads)
    rows = parts.shape[2]
    parts = parts.reshape(distinct, pairs // distinct, rows, -1)
    parts = jnp.sum(parts, 1) if pairs > distinct else parts[:, 0]
    return parts.transpose(1, 0, 2).reshape(rows, -1)


def split_ff(weight, lay, unit):
    rows = weight.shape[0]
    parts = weight.reshape(rows, lay.halves, lay.group, lay.shards, lay.cores, unit)
    return parts.transpose(4, 2, 0, 3, 1, 5).reshape(lay.cores, lay.group, rows, -1)


def merge_ff(parts, lay, unit):
    rows = parts.shape[2]
    parts = parts.reshape(lay.cores, lay.group, rows, lay.shards, lay.halves, unit)
    return parts.transpose(2, 4, 1, 3, 0, 5).reshape(rows, -1)


def pack_heads(query, key, value, lay):
    pairs = lay.cores * lay.group
    if pairs != KV_HEADS or query.shape[0] % 16:
        sides = [(query, HEADS), (key, KV_HEADS), (value, KV_HEADS)]
        return jnp.concatenate([split_heads(block, lay, heads) for block, heads in sides], -1)
    wide, slim = query.shape[1] // pairs, key.shape[1] // pairs
    plan = []
    for pair in range(pairs):
        pieces = [(0, (), pair * wide, wide), (1, (), pair * slim, slim), (2, (), pair * slim, slim)]
        plan.append(((pair // lay.group, pair % lay.group), pieces))
    shape = (lay.cores, lay.group, query.shape[0], wide + 2 * slim)
    return rearrange([query, key, value], [shape], [plan])[0]


def unpack_heads(parts, lay):
    pairs = lay.cores * lay.group
    q_cols = max(1, HEADS // pairs) * HEAD_DIM
    k_cols = max(1, KV_HEADS // pairs) * HEAD_DIM
    if pairs != KV_HEADS:
        sides = [(0, q_cols, HEADS), (q_cols, k_cols, KV_HEADS), (q_cols + k_cols, k_cols, KV_HEADS)]
        return [merge_heads(parts[..., at : at + cols], lay, heads) for at, cols, heads in sides]
    rows = parts.shape[2]
    plans, shapes = [], []
    for first, cols in ((0, q_cols), (q_cols, k_cols), (q_cols + k_cols, k_cols)):
        pieces = [(0, (pair // lay.group, pair % lay.group), first, cols) for pair in range(pairs)]
        plans.append([((slice(None), slice(None)), pieces)])
        shapes.append((rows, pairs * cols))
    return rearrange([parts], shapes, plans)


def ff_columns(lay, core, member, unit):
    for shard in range(lay.shards):
        for half in range(lay.halves):
            block = (half * lay.group + member) * lay.shards + shard
            yield (block * lay.cores + core) * unit, shard * lay.halves + half


def pack_ff(gate, up, lay, unit):
    if not kernel_width(unit):
        return jnp.concatenate([split_ff(gate, lay, unit), split_ff(up, lay, unit)], -1)
    plan = []
    for core in range(lay.cores):
        for member in range(lay.group):
            columns = [column for column, _ in ff_columns(lay, core, member, unit)]
            pieces = [(side, (), column, unit) for side in (0, 1) for column in columns]
            plan.append(((core, member), pieces))
    shape = (lay.cores, lay.group, gate.shape[0], 8 * unit)
    return rearrange([gate, up], [shape], [plan])[0]


def unpack_ff(parts, lay, unit):
    ff = 4 * unit
    if not kernel_width(unit):
        return [merge_ff(parts[..., :ff], lay, unit), merge_ff(parts[..., ff:], lay, unit)]
    rows = parts.shape[2]
    plans = []
    for side in (0, 1):
        found = {}
        for core in range(lay.cores):
            for member in range(lay.group):
                for column, place in ff_columns(lay, core, member, unit):
                    found[column] = (0, (core, member), side * ff + place * unit, unit)
        pieces = [found[column] for column in sorted(found)]
        plans.append([((slice(None), slice(None)), pieces)])
    return rearrange([parts], [(rows, len(found) * unit)] * 2, plans)


def place(own, others, member):
    group = 1 + len(others)
    stacked = jnp.zeros((group,) + own.shape, own.dtype)
    for step, block in enumerate((own,) + tuple(others)):
        stacked = lax.dynamic_update_index_in_dim(stacked, block, member ^ step, 0)
    return stacked


def split_cores(parts, lay, order):
    return lay.to_core(order(pick(parts, 1 - lay.core)))


def core_layers(parts, other, lay):
    kept = pick(parts, lay.core)
    return jnp.where(lay.core == 0, kept, other), jnp.where(lay.core == 0, other, kept)


def to_members(parts, lay, order):
    sent = order.each([pick(parts, lay.member ^ step) for step in range(1, lay.group)])
    return [lay.to_member(block, step) for step, block in enumerate(sent, 1)]


def member_rows(parts, others, lay):
    return place(pick(parts, lay.member), others, lay.member).reshape(-1, parts.shape[-1])


class Spread:
    def __init__(self, block, lay, order):
        self.block, self.lay, self.order = block, lay, order

    def half(self):
        self.got = self.lay.to_half(self.order(self.block))

    def half_done(self):
        self.pair = jnp.concatenate([self.block, self.order(self.got)], 0)

    def shard(self):
        self.got = self.lay.to_shard(self.order(self.pair))

    def shard_done(self):
        self.full = jnp.concatenate([self.pair, self.order(self.got)], 0)


class Collect:
    def __init__(self, left, right, lay, order):
        self.left, self.right, self.lay, self.order = left, right, lay, order
        self.rows = left.shape[1] // 4

    def shard(self):
        block = mm_tn(self.left[:, 2 * self.rows :], self.right).astype(BF16)
        self.got = self.lay.to_shard(self.order(block))

    def shard_done(self):
        self.got, self.left = self.order(self.got, self.left)

    def half(self):
        rows, got = self.rows, self.got.astype(F32)
        kept = mm_tn(self.left[:, : 2 * rows], self.right)
        self.kept = kept[:rows] + got[:rows]
        self.got = self.lay.to_half(self.order((kept[rows:] + got[rows:]).astype(BF16)))

    def half_done(self):
        self.total = self.kept + self.order(self.got).astype(F32)


def join_cores(first, second, lay, order):
    sent = order(jnp.where(lay.core == 0, second, first).astype(BF16))
    return jnp.where(lay.core == 0, first, second), lay.to_core(sent)


def joined_cores(pair, lay, order):
    return two_way(lay.core, pair[0], order(pair[1]).astype(F32), 0)


def out_aligned(lay, block_rows):
    return block_rows == HEAD_DIM and lay.cores * lay.group == KV_HEADS and lay.cores == lay.halves


class SpreadOut:
    def __init__(self, w_out, lay, order):
        self.lay, self.order, self.width = lay, order, w_out.shape[-1]
        self.aligned = out_aligned(lay, w_out.shape[0])
        if not self.aligned:
            w_out = lax.all_gather(w_out, MESH_AXES[1:], axis=0, tiled=True)
        self.own = w_out

    def core(self):
        self.got = self.lay.to_core(self.order(self.own))

    def core_done(self):
        lay, other = self.lay, self.order(self.got)
        self.block = jnp.stack(
            [jnp.where(lay.core == 0, self.own, other), jnp.where(lay.core == 0, other, self.own)]
        )

    def half(self):
        if self.aligned:
            self.got = self.lay.move_some(
                self.order(self.block),
                lambda core, half, member, shard: half == core,
                lambda core, half, member, shard: (core, 1 - half, member, shard),
            )

    def half_done(self):
        if self.aligned:
            lay = self.lay
            self.block = jnp.where(lay.half == lay.core, self.block, self.order(self.got))

    def shard(self):
        if self.aligned:
            self.got = self.lay.to_shard(self.order(self.block))

    def shard_done(self):
        if self.aligned:
            self.full = jnp.concatenate([self.block, self.order(self.got)], 1)
            return
        lay = self.lay
        head = (lay.core * lay.group + lay.member) // head_copies(lay)
        count = max(1, HEADS // (lay.cores * lay.group)) * HEAD_DIM
        self.full = lax.dynamic_slice_in_dim(self.block, head * count, count, 1)


def out_pair(which, spread_out):
    return mm_nt(joined(which.attn_out), spread_out).astype(BF16), joined(which.mid_low)


class CollectOut:
    def __init__(self, pairs, lay, order, block_rows):
        self.pairs, self.lay, self.order = pairs, lay, order
        self.aligned = out_aligned(lay, block_rows)
        self.rows = pairs[0][0].shape[1] // 2

    def shard(self):
        if not self.aligned:
            self.total = [mm_tn(left, right) for left, right in self.pairs]
            return
        blocks = [mm_tn(left[:, self.rows :], right).astype(BF16) for left, right in self.pairs]
        self.got = self.lay.to_shard(self.order(jnp.concatenate(blocks, 0)))

    def shard_done(self):
        if self.aligned:
            self.got = self.order(self.got)

    def half(self):
        if not self.aligned:
            return
        blocks = [mm_tn(left[:, : self.rows], right) for left, right in self.pairs]
        self.kept = jnp.concatenate(blocks, 0) + self.got.astype(F32)
        self.got = self.lay.move_some(
            self.order(self.kept.astype(BF16)),
            lambda core, half, member, shard: half != core,
            lambda core, half, member, shard: (core, 1 - half, member, shard),
        )

    def half_done(self):
        if self.aligned:
            total = self.kept + self.order(self.got).astype(F32)
            self.total = total[: self.rows], total[self.rows :]


def join_out_start(first, second, lay, order, block_rows):
    if not out_aligned(lay, block_rows):
        width = first.shape[1]
        head = (lay.core * lay.group + lay.member) // head_copies(lay)
        full = jnp.zeros((2, HEADS * HEAD_DIM, width), F32)
        full = lax.dynamic_update_slice_in_dim(
            full, jnp.stack([first, second]), head * first.shape[0], 1
        )
        full = pick(lax.psum(full, MESH_AXES), lay.core)
        block = (lay.half * lay.group + lay.member) * lay.shards + lay.shard
        return lax.dynamic_slice_in_dim(full, block * block_rows, block_rows, 0), None
    return join_cores(first, second, lay, order)


def join_out(pair, lay, order):
    kept, other = pair
    if other is None:
        return kept
    return jnp.where(lay.half == lay.core, kept, order(other).astype(F32))


def lane_matrix(heads):
    source = jnp.arange(heads * HEAD_DIM)
    head, offset = source // HEAD_DIM, source % HEAD_DIM
    target = head * LANES + (offset // HALF) * HALF_LANES + offset % HALF
    return (target[:, None] == jnp.arange(heads * LANES)[None, :]).astype(BF16)


def rot(vec, cos_t, sin_t):
    return vec * cos_t + pltpu.roll(vec, HALF_LANES, 1) * sin_t


def rot_back(vec, cos_t, sin_t):
    return vec * cos_t - pltpu.roll(vec, HALF_LANES, 1) * sin_t


def mm(a, b):
    return lax.dot_general(a, b, (((1,), (0,)), ((), ())), preferred_element_type=F32)


def mm_nt(a, b):
    return lax.dot_general(a, b, (((1,), (1,)), ((), ())), preferred_element_type=F32)


def mm_tn(a, b):
    return lax.dot_general(a, b, (((0,), (0,)), ((), ())), preferred_element_type=F32)


def heads_of(block, count):
    return jnp.concatenate([block[:, i * LANES : (i + 1) * LANES] for i in range(count)], 0)


def lanes_of(index, count=1):
    return slice(index * LANES, (index + count) * LANES)


def attend_kernel(
    n_query, n_key, raw_own, raw_sib, cos_t, sin_t, pos_q, pos_k, out_own, out_sib, lse_out, own, sib
):
    scale = HEAD_DIM ** (-0.5)
    per_key = n_query // n_key
    half = raw_own.shape[0]
    rows = 2 * half
    cos_v, sin_v = cos_t[...], sin_t[...]
    mask = pos_q[...] >= pos_k[...]
    mask = jnp.concatenate([mask] * per_key, 0)

    def both(index, turned):
        block = jnp.concatenate([raw_own[:, lanes_of(index)], raw_sib[:, lanes_of(index)]], 0)
        block = (rot(block, cos_v, sin_v) if turned else block).astype(BF16)
        own[:, lanes_of(index)] = block[:half]
        sib[:, lanes_of(index)] = block[half:]
        return block

    for kv_head in range(n_key):
        key, value = both(n_query + kv_head, True), both(n_query + n_key + kv_head, False)
        q_first = kv_head * per_key
        query = jnp.concatenate([both(q_first + i, True) for i in range(per_key)], 0)
        scores = jnp.where(mask, mm_nt(query, key) * scale, MASK_FILL)
        row_max = jnp.max(scores, -1, keepdims=True)
        weights = jnp.exp(scores - row_max)
        total = jnp.sum(weights, -1, keepdims=True)
        probs = (weights * (1.0 / total)).astype(BF16)
        out = mm(probs, value).astype(BF16)
        for i in range(per_key):
            out_own[:, lanes_of(q_first + i)] = out[i * rows : i * rows + half]
            out_sib[:, lanes_of(q_first + i)] = out[i * rows + half : (i + 1) * rows]
        lse_out[kv_head] = row_max + jnp.log(total)


def attend(raw_own, raw_sib, tables, n_query, n_key):
    half, lanes = raw_own.shape
    return pl.pallas_call(
        lambda *refs: attend_kernel(n_query, n_key, *refs),
        out_shape=[
            jax.ShapeDtypeStruct((half, n_query * LANES), BF16),
            jax.ShapeDtypeStruct((half, n_query * LANES), BF16),
            jax.ShapeDtypeStruct((n_key, n_query // n_key * 2 * half, 1), F32),
            jax.ShapeDtypeStruct((half, lanes), BF16),
            jax.ShapeDtypeStruct((half, lanes), BF16),
        ],
        compiler_params=VMEM_LIMIT,
        cost_estimate=pl.CostEstimate(flops=0, bytes_accessed=0, transcendentals=0),
        name="attend",
    )(raw_own, raw_sib, *tables)


def attend_back_kernel(
    n_query, n_key, own, sib, do_own, do_sib, lse, cos_t, sin_t, pos_q, pos_k, low_own, low_sib
):
    scale = HEAD_DIM ** (-0.5)
    per_key = n_query // n_key
    half = own.shape[0]
    rows = 2 * half
    cos_v, sin_v = cos_t[...], sin_t[...]
    mask = pos_q[...] >= pos_k[...]
    mask = jnp.concatenate([mask] * per_key, 0)

    def put(index, block):
        low_own[:, lanes_of(index)] = block[:half].astype(BF16)
        low_sib[:, lanes_of(index)] = block[half:].astype(BF16)

    def both(a, b, index):
        return jnp.concatenate([a[:, lanes_of(index)], b[:, lanes_of(index)]], 0)

    for kv_head in range(n_key):
        key, value = both(own, sib, n_query + kv_head), both(own, sib, n_query + n_key + kv_head)
        q_first = kv_head * per_key
        query = jnp.concatenate([both(own, sib, q_first + i) for i in range(per_key)], 0)
        grad = jnp.concatenate([both(do_own, do_sib, q_first + i) for i in range(per_key)], 0)
        scores = jnp.where(mask, mm_nt(query, key) * scale, MASK_FILL)
        probs = jnp.exp(scores - lse[kv_head])
        prob_grad = mm_nt(grad, value)
        delta = jnp.sum(probs * prob_grad, -1, keepdims=True)
        score_grad = (probs * (prob_grad - delta)).astype(BF16)
        dq = mm(score_grad, key) * scale
        for i in range(per_key):
            put(q_first + i, rot_back(dq[i * rows : (i + 1) * rows], cos_v, sin_v))
        put(n_query + kv_head, rot_back(mm_tn(score_grad, query) * scale, cos_v, sin_v))
        put(n_query + n_key + kv_head, mm_tn(probs.astype(BF16), grad))


def attend_back(kept, out_grads, tables, n_query, n_key):
    own, sib, lse = kept
    half, lanes = own.shape
    return pl.pallas_call(
        lambda *refs: attend_back_kernel(n_query, n_key, *refs),
        out_shape=[
            jax.ShapeDtypeStruct((half, lanes), BF16),
            jax.ShapeDtypeStruct((half, lanes), BF16),
        ],
        compiler_params=VMEM_LIMIT,
        cost_estimate=pl.CostEstimate(flops=0, bytes_accessed=0, transcendentals=0),
        name="attend_back",
    )(own, sib, *out_grads, lse, *tables)


def rows_start(block, lay, order):
    block = order(block)
    return block, [lay.to_member(block, step) for step in range(1, lay.group)]


def rows_middle(begun, lay, order):
    block, others = begun
    own = order(jnp.concatenate([block] + order.each(others), 0))
    return [own, lay.to_core(own)]


def rows_done(rows, order):
    rows[1] = order(rows[1])
    return rows


def sums_start(own, sib, lay, order):
    return own, lay.to_core(order(sib.astype(BF16)))


def sums_middle(begun, lay, order):
    own, got = begun
    own = own + order(got).astype(F32)
    rows = own.shape[0] // lay.group
    parts = own.reshape(lay.group, rows, -1)
    sent = order.each([parts[step].astype(BF16) for step in range(1, lay.group)])
    return parts[0], [lay.to_member(block, step) for step, block in enumerate(sent, 1)]


def sums_done(begun, order):
    total, others = begun
    for block in order.each(others):
        total = total + block.astype(F32)
    return total


def norm_forward(inputs, gain_vec):
    inverse_rms = lax.rsqrt(jnp.mean(inputs * inputs, -1, keepdims=True) + NORM_EPS)
    return (inputs * inverse_rms * gain_vec).astype(BF16), inverse_rms


def norm_backward(inputs, inverse_rms, gain_vec, upstream):
    scaled = upstream * gain_vec
    input_grad = inverse_rms * scaled - inputs * inverse_rms**3 * jnp.mean(
        scaled * inputs, -1, keepdims=True
    )
    gain_grad = jnp.sum(upstream * inputs * inverse_rms, 0)
    return input_grad, gain_grad


def out_order(block, lay, n_query):
    if head_copies(lay) > 1:
        share = (lay.core * lay.group + lay.member) % head_copies(lay) == 0
        return jnp.where(share, block, jnp.zeros_like(block))
    if n_query != 2 or lay.cores * lay.group != KV_HEADS:
        return block
    swapped = jnp.concatenate([block[:, LANES:], block[:, :LANES]], 1)
    return jnp.where(lay.shard == 0, block, swapped)


class Layer:
    def __init__(self, lay, tables, n_query, n_key, gain_one, gain_two):
        self.lay, self.tables, self.n_query, self.n_key = lay, tables, n_query, n_key
        self.gain_one, self.gain_two = gain_one, gain_two

    def first_norm(self, inputs):
        self.inputs = inputs
        normed, self.inverse_first = norm_forward(inputs, self.gain_one)
        return relative(normed, self.lay)

    def attend(self):
        raw = [mm(block, self.qkv_w) for block in self.normed]
        out_own, out_sib, lse, own, sib = attend(*raw, self.tables, self.n_query, self.n_key)
        self.attn_kept = own, sib, lse
        self.attn_out = [out_order(block, self.lay, self.n_query) for block in (out_own, out_sib)]

    def out_partial(self):
        return [mm(block, self.out_w) for block in self.attn_out]

    def second_norm(self, attended):
        self.mid_stream = self.inputs + attended
        normed, self.inverse_second = norm_forward(self.mid_stream, self.gain_two)
        return relative(normed, self.lay)

    def hide(self):
        self.gate_up, self.hidden = [], []
        for block in self.normed_mid:
            gate_pre, up_pre = mm(block, self.gate_w), mm(block, self.up_w)
            self.gate_up.append((gate_pre, up_pre))
            hidden = (jax.nn.silu(gate_pre) * up_pre).astype(BF16)
            self.hidden.append(relative(hidden, self.lay))

    def down_partial(self):
        return [mm(block, self.down_w) for block in self.hidden]

    def feed_forward_back(self):
        self.gate_grad, self.up_grad, partial = [], [], []
        for block, (gate_pre, up_pre) in zip(self.down_in, self.gate_up):
            hidden_grad = relative(mm_nt(block, self.down_w), self.lay)
            sigmoid_gate = jax.nn.sigmoid(gate_pre)
            gate_grad_in = (
                hidden_grad * up_pre * sigmoid_gate * (1.0 + gate_pre * (1.0 - sigmoid_gate))
            ).astype(BF16)
            up_grad_in = (hidden_grad * gate_pre * sigmoid_gate).astype(BF16)
            self.gate_grad.append(gate_grad_in)
            self.up_grad.append(up_grad_in)
            partial.append(mm_nt(gate_grad_in, self.gate_w) + mm_nt(up_grad_in, self.up_w))
        return partial

    def second_norm_back(self, out_grad, upstream):
        part, self.gain_two_grad = norm_backward(
            self.mid_stream, self.inverse_second, self.gain_two, relative(upstream, self.lay)
        )
        self.mid_grad = out_grad + part
        return self.mid_grad.astype(BF16)

    def attention_back(self, order):
        grads = [
            out_order(mm_nt(block, self.out_w).astype(BF16), self.lay, self.n_query)
            for block in self.mid_low
        ]
        self.lows = attend_back(self.attn_kept, grads, self.tables, self.n_query, self.n_key)
        self.lows = order.each(self.lows)
        return [mm_nt(block, self.qkv_w) for block in self.lows]

    def first_norm_back(self, upstream):
        part, gain_one_grad = norm_backward(
            self.inputs, self.inverse_first, self.gain_one, relative(upstream, self.lay)
        )
        self.gain_grads = jnp.stack([gain_one_grad, self.gain_two_grad])
        return self.mid_grad + part


def joined(pair):
    return jnp.concatenate(pair, 0)


def row_tables(pair_table, block_rows, lay):
    cores = []
    for core in (lay.core, 1 - lay.core):
        ctx_ids = jnp.stack([core * lay.group + (lay.member ^ step) for step in range(lay.group)])
        owned = jnp.sum(
            jnp.where(ctx_ids[:, None] == jnp.arange(lay.ctx)[None, :], pair_table[None, :], 0), 1
        )
        blocks = jnp.stack([owned, 2 * lay.ctx - 1 - owned], 1)
        rows = blocks[:, :, None] * block_rows + jnp.arange(block_rows)[None, None, :]
        cores.append(rows.reshape(-1))
    positions = jnp.concatenate(cores)
    freq_idx = jnp.arange(HALF, dtype=F32)
    inverse = ROPE_BASE ** (-2.0 * freq_idx / HEAD_DIM)
    angles = positions.astype(F32)[:, None] * inverse[None, :]
    pad = ((0, 0), (0, HALF_LANES - HALF))
    cos_h, sin_h = jnp.pad(jnp.cos(angles), pad), jnp.pad(jnp.sin(angles), pad)
    cos_t = jnp.concatenate([cos_h, cos_h], 1)
    sin_t = jnp.concatenate([-sin_h, sin_h], 1)
    return cos_t, sin_t, positions[:, None], positions[None, :]


def deal_rows(local, lay, order):
    turn = lay.half ^ lay.core
    sent = order(pick(local, turn), pick(local, 1 - turn))
    straight = lay.move(
        sent[0], lambda core, half, member, shard: (half, half ^ core, member, shard)
    )
    crossed = lay.move(
        sent[1], lambda core, half, member, shard: (half, 1 - (half ^ core), member, shard)
    )
    return straight, crossed


def dealt(straight, crossed, lay):
    turn = lay.half ^ lay.core
    return jnp.where(turn == 0, straight, crossed), jnp.where(turn == 0, crossed, straight)


def return_rows(input_grad, outputs, lay, order):
    turn = lay.half ^ lay.core
    sent = order(
        jnp.where(turn == 0, input_grad, outputs), jnp.where(turn == 0, outputs, input_grad)
    )
    straight = lay.move(
        sent[0], lambda core, half, member, shard: (core ^ half, core, member, shard)
    )
    crossed = lay.move(
        sent[1], lambda core, half, member, shard: (1 - (core ^ half), core, member, shard)
    )
    return straight, crossed


def body(
    ends_in, pair_table, norm_attn, w_query, w_key, w_value, w_out, norm_mlp, w_gate, w_up, w_down
):
    lay = Layout()
    rows = ends_in.shape[3]
    width = ends_in.shape[4]
    row_block = w_query.shape[1]
    pairs = lay.cores * lay.group
    n_query = max(1, HEADS // pairs)
    n_key = max(1, KV_HEADS // pairs)
    ff_unit = w_down.shape[1] // lay.cores
    q_cols, k_cols = n_query * HEAD_DIM, n_key * HEAD_DIM
    spread_lanes = lane_matrix(n_query + 2 * n_key)
    spread_out = lane_matrix(n_query)
    cols = q_cols + 2 * k_cols
    ff = ff_unit * 4
    order = Order()

    def by_member(*blocks):
        return jnp.concatenate(blocks, 1).reshape(lay.group, row_block, -1)

    tables = row_tables(pair_table, rows // 2, lay)
    gains = jnp.stack([norm_attn[0], norm_mlp[0]])
    gain_parts = [lay.to_member(gains, step) for step in range(1, lay.group)]
    heads = pack_heads(w_query[0], w_key[0], w_value[0], lay)
    heads_other = split_cores(heads, lay, order)
    heads_other, *gain_parts = order(heads_other, *gain_parts)
    qkv_layers = core_layers(heads, heads_other, lay)
    qkv_others = to_members(qkv_layers[0], lay, order)
    gains = order(place(gains, gain_parts, lay.member))
    gains_other = lay.to_half(gains)
    w_gate, w_up, ends_in = order(w_gate, w_up, ends_in)
    own_rows = to_inner(ends_in[0, :, 0], lay)
    gate_up_own = pack_ff(w_gate[0], w_up[0], lay, ff_unit)
    gate_up_other = split_cores(gate_up_own, lay, order)
    rows_other = deal_rows(own_rows, lay, order)
    qkv_0 = Spread(member_rows(qkv_layers[0], order.each(qkv_others), lay), lay, order)
    qkv_0.half()
    gains = order(two_way(lay.half, gains, order(gains_other), 0))
    gains_other = lay.to_shard(gains)
    gains = order(two_way(lay.shard, gains, order(gains_other), 0))
    gains_other = lay.to_core(gains)
    out = SpreadOut(to_inner(order(w_out)[0], lay), lay, order)
    out.core()
    gains = two_way(lay.core, gains, order(gains_other), 0)
    gains = gains.transpose(0, 4, 1, 2, 3, 5).reshape(2, 2, -1).astype(F32)
    gate_up_layers = core_layers(gate_up_own, order(gate_up_other), lay)
    out.core_done()
    own_in, own_cot = dealt(*order(*rows_other), lay)
    first = Layer(lay, tables, n_query, n_key, gains[0, 0], gains[0, 1])
    second = Layer(lay, tables, n_query, n_key, gains[1, 0], gains[1, 1])
    normed = rows_start(first.first_norm(own_in.astype(F32)), lay, order)
    qkv_0.half_done()
    qkv_0.shard()
    out.half()
    normed = rows_middle(normed, lay, order)
    gate_up_others = to_members(gate_up_layers[0], lay, order)
    qkv_0.shard_done()
    out.half_done()
    out.shard()
    first.qkv_w = mm(qkv_0.full, spread_lanes).astype(BF16)
    first.normed = rows_done(normed, order)
    first.attend()
    first.attn_out = order.each(first.attn_out)
    gate_up = member_rows(gate_up_layers[0], order.each(gate_up_others), lay)
    gate_0 = Spread(gate_up[:, :ff], lay, order)
    up_0 = Spread(gate_up[:, ff:], lay, order)
    gate_0.half()
    down_own = to_inner(order(w_down)[0], lay).reshape(lay.cores, ff_unit, width)
    down_other = split_cores(down_own, lay, order)
    out.shard_done()
    first.out_w = mm_tn(spread_out, out.full[0]).astype(BF16)
    second.out_w = mm_tn(spread_out, out.full[1]).astype(BF16)
    sums = sums_middle(sums_start(*first.out_partial(), lay, order), lay, order)
    down_layers = core_layers(down_own, order(down_other), lay)
    down_0, down_1 = Spread(down_layers[0], lay, order), Spread(down_layers[1], lay, order)
    attended = sums_done(sums, order)
    gate_0.half_done()
    gate_0.shard()
    up_0.half()
    normed = rows_start(first.second_norm(attended), lay, order)
    normed = rows_middle(normed, lay, order)
    rest = jnp.concatenate([qkv_layers[1], gate_up_layers[1]], -1)
    rest_others = to_members(rest, lay, order)
    up_0.half_done()
    gate_0.shard_done()
    up_0.shard()
    down_0.half()
    first.normed_mid = rows_done(normed, order)
    rest = member_rows(rest, order.each(rest_others), lay)
    qkv_1 = Spread(rest[:, :cols], lay, order)
    gate_up_1 = Spread(rest[:, cols:], lay, order)
    up_0.shard_done()
    down_0.half_done()
    down_0.shard()
    qkv_1.half()
    own_cot = own_cot.astype(F32)
    cot = rows_start(own_cot.astype(BF16), lay, order)
    first.gate_w, first.up_w = gate_0.full, up_0.full
    first.hide()
    second.down_in = rows_middle(cot, lay, order)
    qkv_1.half_done()
    gate_up_1.half()
    down_0.shard_done()
    qkv_1.shard()
    first.down_w = down_0.full
    sums = sums_middle(sums_start(*first.down_partial(), lay, order), lay, order)
    first_out = first.mid_stream + sums_done(sums, order)
    normed = rows_start(second.first_norm(first_out.astype(BF16).astype(F32)), lay, order)
    normed = rows_middle(normed, lay, order)
    gate_up_1.half_done()
    gate_up_1.shard()
    down_1.half()
    qkv_1.shard_done()
    second.qkv_w = mm(qkv_1.full, spread_lanes).astype(BF16)
    second.normed = rows_done(normed, order)
    second.attend()
    sums = sums_start(*second.out_partial(), lay, order)
    sums = sums_middle(sums, lay, order)
    attended = sums_done(sums, order)
    gate_up_1.shard_done()
    down_1.half_done()
    down_1.shard()
    normed = rows_start(second.second_norm(attended), lay, order)
    normed = rows_middle(normed, lay, order)
    second.gate_w, second.up_w = gate_up_1.full[:, :ff], gate_up_1.full[:, ff:]
    second.normed_mid = rows_done(normed, order)
    second.down_in = rows_done(second.down_in, order)
    second.hide()

    down_g1 = Collect(joined(second.hidden), joined(second.down_in), lay, order)
    down_g1.shard()
    down_1.shard_done()
    second.down_w = down_1.full
    partial = second.feed_forward_back()
    sums = sums_start(*partial, lay, order)
    grads = [jnp.concatenate(pair, 1) for pair in zip(second.gate_grad, second.up_grad)]
    gate_up_g1 = Collect(joined(second.normed_mid), joined(grads), lay, order)
    sums = sums_middle(sums, lay, order)
    gate_up_g1.shard()
    upstream = sums_done(sums, order)
    low = second.second_norm_back(own_cot, upstream)
    down_g1.shard_done()
    low = rows_start(low, lay, order)
    low = rows_middle(low, lay, order)
    down_g1.half()
    second.mid_low = rows_done(low, order)
    partial = second.attention_back(order)
    sums = sums_start(*partial, lay, order)
    low = mm_nt(joined(second.lows), spread_lanes).astype(BF16)
    qkv_g1 = Collect(joined(second.normed), low, lay, order)
    gate_up_g1.shard_done()
    qkv_g1.shard()
    sums = sums_middle(sums, lay, order)
    upstream = sums_done(sums, order)
    down_g1.half_done()
    gate_up_g1.half()
    second_grad = second.first_norm_back(upstream)

    first_cot = second_grad.astype(BF16)
    down_in = rows_start(first_cot, lay, order)
    down_in = rows_middle(down_in, lay, order)
    first.down_in = rows_done(down_in, order)
    down_g0 = Collect(joined(first.hidden), joined(first.down_in), lay, order)
    qkv_g1.shard_done()
    down_g0.shard()
    partial = first.feed_forward_back()
    sums = sums_start(*partial, lay, order)
    left = joined(first.normed_mid)
    gate_g0 = Collect(left, joined(first.gate_grad), lay, order)
    up_g0 = Collect(left, joined(first.up_grad), lay, order)
    sums = sums_middle(sums, lay, order)
    upstream = sums_done(sums, order)
    gate_up_g1.half_done()
    qkv_g1.half()
    low = rows_start(first.second_norm_back(first_cot.astype(F32), upstream), lay, order)
    down_g0.shard_done()
    gate_g0.shard()
    low = rows_middle(low, lay, order)
    qkv_g1.half_done()
    down_g0.half()
    first.mid_low = rows_done(low, order)
    partial = first.attention_back(order)
    gate_g0.shard_done()
    up_g0.shard()
    down_g0.half_done()
    gate_g0.half()
    sums = sums_start(*partial, lay, order)
    low = mm_nt(joined(first.lows), spread_lanes).astype(BF16)
    qkv_g0 = Collect(joined(first.normed), low, lay, order)
    sums = sums_middle(sums, lay, order)
    upstream = sums_done(sums, order)
    first_grad = first.first_norm_back(upstream)

    out_both = CollectOut(
        [out_pair(which, spread_out) for which in (first, second)], lay, order, row_block
    )
    up_g0.shard_done()
    up_g0.half()
    qkv_g0.shard()
    mlp_1 = by_member(gate_up_g1.total)
    others_1 = to_members(mlp_1.astype(BF16), lay, order)
    gate_g0.half_done()
    up_g0.half_done()
    others_1 = order.each(others_1)
    gains = jnp.stack([first.gain_grads, second.gain_grads])
    gains_other = lay.to_core(order(pick(gains, 1 - lay.core)))
    mlp_0 = by_member(gate_g0.total, up_g0.total)
    others_0 = to_members(mlp_0.astype(BF16), lay, order)
    qkv_g0.shard_done()
    qkv_g0.half()
    out_both.shard()
    outputs = sums_start(*second.down_partial(), lay, order)
    down_join = join_cores(down_g0.total, down_g1.total, lay, order)
    back_1 = place(pick(mlp_1, lay.member), [block.astype(F32) for block in others_1], lay.member)
    others_0 = order.each(others_0)
    gains = pick(gains, lay.core) + order(gains_other)
    gains = gains.reshape(2, lay.shards, lay.halves, lay.group, -1).transpose(1, 2, 3, 0, 4)
    outputs = sums_middle(outputs, lay, order)
    back_0 = place(pick(mlp_0, lay.member), [block.astype(F32) for block in others_0], lay.member)
    ff_join = join_cores(back_0, back_1, lay, order)
    out_both.shard_done()
    out_both.half()
    gains_other = lay.to_shard(order(pick(gains, 1 - lay.shard)))
    qkv_g0.half_done()
    second_out = second.mid_stream + sums_done(outputs, order)
    attn = by_member(qkv_g0.total, qkv_g1.total)
    others_q = to_members(attn.astype(BF16), lay, order)
    rows_other = return_rows(first_grad.astype(BF16), second_out.astype(BF16), lay, order)
    gains = pick(gains, lay.shard) + order(gains_other)
    gains_other = lay.to_half(order(pick(gains, 1 - lay.half)))
    gate_up_g = order.each(unpack_ff(joined_cores(ff_join, lay, order), lay, ff_unit))
    others_q = order.each(others_q)
    back_q = place(pick(attn, lay.member), [block.astype(F32) for block in others_q], lay.member)
    qkv_join = join_cores(back_q[..., :cols], back_q[..., cols:], lay, order)
    out_both.half_done()
    out_join = join_out_start(*out_both.total, lay, order, row_block)
    gains = pick(gains, lay.half) + order(gains_other)
    gain_g = pick(gains, lay.member)
    gain_others = to_members(gains, lay, order)
    down_g = to_outer(joined_cores(down_join, lay, order).reshape(-1, width), lay)
    qkv_g = unpack_heads(joined_cores(qkv_join, lay, order), lay)
    straight, crossed = order(*rows_other)
    ends = two_way(lay.half ^ lay.core, straight, crossed, 0)
    out_g = to_outer(join_out(out_join, lay, order), lay)
    for block in order.each(gain_others):
        gain_g = gain_g + block
    ends = to_outer(ends, lay)
    return (
        ends[None, :, None],
        gain_g[0][None],
        qkv_g[0][None],
        qkv_g[1][None],
        qkv_g[2][None],
        out_g[None],
        gain_g[1][None],
        gate_up_g[0][None],
        gate_up_g[1][None],
        down_g[None],
    )


def solution(mesh):
    rows = P("section", None, "shard", "ctx", None)
    vector = P("section", ("ctx", "shard"))
    matrix = P("section", ("ctx", "shard"), None)
    return jax.shard_map(
        body,
        mesh=mesh,
        in_specs=(rows, P(), vector, matrix, matrix, matrix, matrix, vector, matrix, matrix, matrix),
        out_specs=(rows, vector, matrix, matrix, matrix, matrix, vector, matrix, matrix, matrix),
        check_vma=False,
    )
```

```python
import jax
import jax.numpy as jnp
from jax import lax
from jax.experimental import pallas as pl
from jax.experimental.pallas import tpu as pltpu
from jax.sharding import PartitionSpec as P

HEADS = 16
KV_HEADS = 8
HEAD_DIM = 96
HALF = HEAD_DIM // 2
LANES = 128
HALF_LANES = LANES // 2

NORM_EPS = 1e-05
ROPE_BASE = 100000.0
MASK_FILL = -1e30

MESH_AXES = ("section", "ctx", "shard")
F32 = jnp.float32
BF16 = jnp.bfloat16
VMEM_LIMIT = pltpu.CompilerParams(vmem_limit_bytes=56 * 1024 * 1024)


class Layout:
    def __init__(self):
        self.cores = lax.axis_size("section")
        self.ctx = lax.axis_size("ctx")
        self.shards = lax.axis_size("shard")
        self.halves = 2
        self.group = self.ctx // self.halves
        ctx_index = lax.axis_index("ctx")
        self.core = lax.axis_index("section")
        self.half = ctx_index // self.group
        self.member = ctx_index % self.group
        self.shard = lax.axis_index("shard")

    def move(self, block, target):
        pairs = []
        for core in range(self.cores):
            for half in range(self.halves):
                for member in range(self.group):
                    for shard in range(self.shards):
                        to = target(core, half, member, shard)
                        pairs.append((self.flat(core, half, member, shard), self.flat(*to)))
        return lax.ppermute(block, MESH_AXES, pairs)

    def move_some(self, block, sends, target):
        pairs = []
        for core in range(self.cores):
            for half in range(self.halves):
                for member in range(self.group):
                    for shard in range(self.shards):
                        if sends(core, half, member, shard):
                            to = target(core, half, member, shard)
                            pairs.append((self.flat(core, half, member, shard), self.flat(*to)))
        return lax.ppermute(block, MESH_AXES, pairs)

    def flat(self, core, half, member, shard):
        return (core * self.ctx + half * self.group + member) * self.shards + shard

    def to_member(self, block, step):
        return self.move(block, lambda core, half, member, shard: (core, half, member ^ step, shard))

    def to_half(self, block):
        return self.move(block, lambda core, half, member, shard: (core, 1 - half, member, shard))

    def to_shard(self, block):
        return self.move(block, lambda core, half, member, shard: (core, half, member, 1 - shard))

    def to_core(self, block):
        return self.move(block, lambda core, half, member, shard: (1 - core, half, member, shard))


def pick(parts, index):
    return lax.dynamic_index_in_dim(parts, index, 0, False)


class Order:
    def __init__(self):
        self.last = ()

    def __call__(self, *blocks):
        if self.last:
            blocks = lax.optimization_barrier(tuple(blocks) + self.last)[: len(blocks)]
        self.last = (blocks[0],)
        return blocks[0] if len(blocks) == 1 else blocks

    def each(self, blocks):
        blocks = self(*blocks)
        return list(blocks) if isinstance(blocks, (tuple, list)) else [blocks]


def two_way(index, own, other, axis):
    first = jnp.where(index == 0, own, other)
    second = jnp.where(index == 0, other, own)
    return jnp.stack([first, second], axis)


def rearrange_kernel(plans, count, *refs):
    sources, outs = refs[:count], refs[count:]
    for out, plan in zip(outs, plans):
        for index, pieces in plan:
            blocks = [
                sources[source][place + (slice(None), slice(column, column + width))]
                for source, place, column, width in pieces
            ]
            out[index] = jnp.concatenate(blocks, 1) if len(blocks) > 1 else blocks[0]


def rearrange(sources, shapes, plans):
    dtype = sources[0].dtype
    moved = sum(source.size for source in sources) * dtype.itemsize
    return pl.pallas_call(
        lambda *refs: rearrange_kernel(plans, len(sources), *refs),
        out_shape=[jax.ShapeDtypeStruct(shape, dtype) for shape in shapes],
        compiler_params=VMEM_LIMIT,
        cost_estimate=pl.CostEstimate(flops=0, bytes_accessed=0, transcendentals=0),
        name="rearrange",
    )(*sources)


def kernel_width(width):
    return width % HEAD_DIM == 0 or width % LANES == 0


def to_inner(block, lay, inner=True):
    blocks = lay.shards * lay.halves * lay.group
    width = block.shape[-1] // blocks
    outer_order = [
        ((half * lay.group + member) * lay.shards + shard) * width
        for shard in range(lay.shards)
        for half in range(lay.halves)
        for member in range(lay.group)
    ]
    if kernel_width(width):
        columns = outer_order
        if not inner:
            columns = [outer_order.index(i * width) * width for i in range(blocks)]
        flat = block.reshape(-1, block.shape[-1])
        plan = [((slice(None), slice(None)), [(0, (), column, width) for column in columns])]
        return rearrange([flat], [flat.shape], [plan])[0].reshape(block.shape)
    if inner:
        parts = block.reshape(block.shape[:-1] + (lay.halves, lay.group, lay.shards, -1))
        return jnp.moveaxis(parts, -2, -4).reshape(block.shape)
    parts = block.reshape(block.shape[:-1] + (lay.shards, lay.halves, lay.group, -1))
    return jnp.moveaxis(parts, -4, -2).reshape(block.shape)


def to_outer(block, lay):
    return to_inner(block, lay, False)


def relative(block, lay):
    width = block.shape[-1] // 4
    parts = [block[..., i * width : (i + 1) * width] for i in range(4)]
    parts = [jnp.where(lay.half == 0, parts[i], parts[i ^ 1]) for i in range(4)]
    parts = [jnp.where(lay.shard == 0, parts[i], parts[i ^ 2]) for i in range(4)]
    return jnp.concatenate(parts, -1)


def head_copies(lay):
    return max(1, lay.cores * lay.group // HEADS)


def split_heads(weight, lay, heads):
    rows = weight.shape[0]
    pairs = lay.cores * lay.group
    distinct = min(pairs, heads)
    parts = weight.reshape(rows, distinct, -1).transpose(1, 0, 2)
    parts = jnp.repeat(parts, pairs // distinct, axis=0) if pairs > distinct else parts
    return parts.reshape((lay.cores, lay.group) + parts.shape[1:])


def merge_heads(parts, lay, heads):
    pairs = lay.cores * lay.group
    distinct = min(pairs, heads)
    rows = parts.shape[2]
    parts = parts.reshape(distinct, pairs // distinct, rows, -1)
    parts = jnp.sum(parts, 1) if pairs > distinct else parts[:, 0]
    return parts.transpose(1, 0, 2).reshape(rows, -1)


def split_ff(weight, lay, unit):
    rows = weight.shape[0]
    parts = weight.reshape(rows, lay.halves, lay.group, lay.shards, lay.cores, unit)
    return parts.transpose(4, 2, 0, 3, 1, 5).reshape(lay.cores, lay.group, rows, -1)


def merge_ff(parts, lay, unit):
    rows = parts.shape[2]
    parts = parts.reshape(lay.cores, lay.group, rows, lay.shards, lay.halves, unit)
    return parts.transpose(2, 4, 1, 3, 0, 5).reshape(rows, -1)


def pack_heads(query, key, value, lay):
    pairs = lay.cores * lay.group
    if pairs != KV_HEADS or query.shape[0] % 16:
        sides = [(query, HEADS), (key, KV_HEADS), (value, KV_HEADS)]
        return jnp.concatenate([split_heads(block, lay, heads) for block, heads in sides], -1)
    wide, slim = query.shape[1] // pairs, key.shape[1] // pairs
    plan = []
    for pair in range(pairs):
        pieces = [(0, (), pair * wide, wide), (1, (), pair * slim, slim), (2, (), pair * slim, slim)]
        plan.append(((pair // lay.group, pair % lay.group), pieces))
    shape = (lay.cores, lay.group, query.shape[0], wide + 2 * slim)
    return rearrange([query, key, value], [shape], [plan])[0]


def unpack_heads(parts, lay):
    pairs = lay.cores * lay.group
    q_cols = max(1, HEADS // pairs) * HEAD_DIM
    k_cols = max(1, KV_HEADS // pairs) * HEAD_DIM
    if pairs != KV_HEADS:
        sides = [(0, q_cols, HEADS), (q_cols, k_cols, KV_HEADS), (q_cols + k_cols, k_cols, KV_HEADS)]
        return [merge_heads(parts[..., at : at + cols], lay, heads) for at, cols, heads in sides]
    rows = parts.shape[2]
    plans, shapes = [], []
    for first, cols in ((0, q_cols), (q_cols, k_cols), (q_cols + k_cols, k_cols)):
        pieces = [(0, (pair // lay.group, pair % lay.group), first, cols) for pair in range(pairs)]
        plans.append([((slice(None), slice(None)), pieces)])
        shapes.append((rows, pairs * cols))
    return rearrange([parts], shapes, plans)


def ff_columns(lay, core, member, unit):
    for shard in range(lay.shards):
        for half in range(lay.halves):
            block = (half * lay.group + member) * lay.shards + shard
            yield (block * lay.cores + core) * unit, shard * lay.halves + half


def pack_ff(gate, up, lay, unit):
    if not kernel_width(unit):
        return jnp.concatenate([split_ff(gate, lay, unit), split_ff(up, lay, unit)], -1)
    plan = []
    for core in range(lay.cores):
        for member in range(lay.group):
            columns = [column for column, _ in ff_columns(lay, core, member, unit)]
            pieces = [(side, (), column, unit) for side in (0, 1) for column in columns]
            plan.append(((core, member), pieces))
    shape = (lay.cores, lay.group, gate.shape[0], 8 * unit)
    return rearrange([gate, up], [shape], [plan])[0]


def unpack_ff(parts, lay, unit):
    ff = 4 * unit
    if not kernel_width(unit):
        return [merge_ff(parts[..., :ff], lay, unit), merge_ff(parts[..., ff:], lay, unit)]
    rows = parts.shape[2]
    plans = []
    for side in (0, 1):
        found = {}
        for core in range(lay.cores):
            for member in range(lay.group):
                for column, place in ff_columns(lay, core, member, unit):
                    found[column] = (0, (core, member), side * ff + place * unit, unit)
        pieces = [found[column] for column in sorted(found)]
        plans.append([((slice(None), slice(None)), pieces)])
    return rearrange([parts], [(rows, len(found) * unit)] * 2, plans)


def place(own, others, member):
    group = 1 + len(others)
    stacked = jnp.zeros((group,) + own.shape, own.dtype)
    for step, block in enumerate((own,) + tuple(others)):
        stacked = lax.dynamic_update_index_in_dim(stacked, block, member ^ step, 0)
    return stacked


def split_cores(parts, lay, order):
    return lay.to_core(order(pick(parts, 1 - lay.core)))


def core_layers(parts, other, lay):
    kept = pick(parts, lay.core)
    return jnp.where(lay.core == 0, kept, other), jnp.where(lay.core == 0, other, kept)


def to_members(parts, lay, order):
    sent = order.each([pick(parts, lay.member ^ step) for step in range(1, lay.group)])
    return [lay.to_member(block, step) for step, block in enumerate(sent, 1)]


def member_rows(parts, others, lay):
    return place(pick(parts, lay.member), others, lay.member).reshape(-1, parts.shape[-1])


class Spread:
    def __init__(self, block, lay, order):
        self.block, self.lay, self.order = block, lay, order

    def half(self):
        self.got = self.lay.to_half(self.order(self.block))

    def half_done(self):
        self.pair = jnp.concatenate([self.block, self.order(self.got)], 0)

    def shard(self):
        self.got = self.lay.to_shard(self.order(self.pair))

    def shard_done(self):
        self.full = jnp.concatenate([self.pair, self.order(self.got)], 0)


class Collect:
    def __init__(self, left, right, lay, order):
        self.left, self.right, self.lay, self.order = left, right, lay, order
        self.rows = left.shape[1] // 4

    def shard(self):
        block = mm_tn(self.left[:, 2 * self.rows :], self.right).astype(BF16)
        self.got = self.lay.to_shard(self.order(block))

    def shard_done(self):
        self.got, self.left = self.order(self.got, self.left)

    def half(self):
        rows, got = self.rows, self.got.astype(F32)
        kept = mm_tn(self.left[:, : 2 * rows], self.right)
        self.kept = kept[:rows] + got[:rows]
        self.got = self.lay.to_half(self.order((kept[rows:] + got[rows:]).astype(BF16)))

    def half_done(self):
        self.total = self.kept + self.order(self.got).astype(F32)


def join_cores(first, second, lay, order):
    sent = order(jnp.where(lay.core == 0, second, first).astype(BF16))
    return jnp.where(lay.core == 0, first, second), lay.to_core(sent)


def joined_cores(pair, lay, order):
    return two_way(lay.core, pair[0], order(pair[1]).astype(F32), 0)


def out_aligned(lay, block_rows):
    return block_rows == HEAD_DIM and lay.cores * lay.group == KV_HEADS and lay.cores == lay.halves


class SpreadOut:
    def __init__(self, w_out, lay, order):
        self.lay, self.order, self.width = lay, order, w_out.shape[-1]
        self.aligned = out_aligned(lay, w_out.shape[0])
        if not self.aligned:
            w_out = lax.all_gather(w_out, MESH_AXES[1:], axis=0, tiled=True)
        self.own = w_out

    def core(self):
        self.got = self.lay.to_core(self.order(self.own))

    def core_done(self):
        lay, other = self.lay, self.order(self.got)
        self.block = jnp.stack(
            [jnp.where(lay.core == 0, self.own, other), jnp.where(lay.core == 0, other, self.own)]
        )

    def half(self):
        if self.aligned:
            self.got = self.lay.move_some(
                self.order(self.block),
                lambda core, half, member, shard: half == core,
                lambda core, half, member, shard: (core, 1 - half, member, shard),
            )

    def half_done(self):
        if self.aligned:
            lay = self.lay
            self.block = jnp.where(lay.half == lay.core, self.block, self.order(self.got))

    def shard(self):
        if self.aligned:
            self.got = self.lay.to_shard(self.order(self.block))

    def shard_done(self):
        if self.aligned:
            self.full = jnp.concatenate([self.block, self.order(self.got)], 1)
            return
        lay = self.lay
        head = (lay.core * lay.group + lay.member) // head_copies(lay)
        count = max(1, HEADS // (lay.cores * lay.group)) * HEAD_DIM
        self.full = lax.dynamic_slice_in_dim(self.block, head * count, count, 1)


def out_pair(which, spread_out):
    return mm_nt(joined(which.attn_out), spread_out).astype(BF16), joined(which.mid_low)


class CollectOut:
    def __init__(self, pairs, lay, order, block_rows):
        self.pairs, self.lay, self.order = pairs, lay, order
        self.aligned = out_aligned(lay, block_rows)
        self.rows = pairs[0][0].shape[1] // 2

    def shard(self):
        if not self.aligned:
            self.total = [mm_tn(left, right) for left, right in self.pairs]
            return
        blocks = [mm_tn(left[:, self.rows :], right).astype(BF16) for left, right in self.pairs]
        self.got = self.lay.to_shard(self.order(jnp.concatenate(blocks, 0)))

    def shard_done(self):
        if self.aligned:
            self.got = self.order(self.got)

    def half(self):
        if not self.aligned:
            return
        blocks = [mm_tn(left[:, : self.rows], right) for left, right in self.pairs]
        self.kept = jnp.concatenate(blocks, 0) + self.got.astype(F32)
        self.got = self.lay.move_some(
            self.order(self.kept.astype(BF16)),
            lambda core, half, member, shard: half != core,
            lambda core, half, member, shard: (core, 1 - half, member, shard),
        )

    def half_done(self):
        if self.aligned:
            total = self.kept + self.order(self.got).astype(F32)
            self.total = total[: self.rows], total[self.rows :]


def join_out_start(first, second, lay, order, block_rows):
    if not out_aligned(lay, block_rows):
        width = first.shape[1]
        head = (lay.core * lay.group + lay.member) // head_copies(lay)
        full = jnp.zeros((2, HEADS * HEAD_DIM, width), F32)
        full = lax.dynamic_update_slice_in_dim(
            full, jnp.stack([first, second]), head * first.shape[0], 1
        )
        full = pick(lax.psum(full, MESH_AXES), lay.core)
        block = (lay.half * lay.group + lay.member) * lay.shards + lay.shard
        return lax.dynamic_slice_in_dim(full, block * block_rows, block_rows, 0), None
    return join_cores(first, second, lay, order)


def join_out(pair, lay, order):
    kept, other = pair
    if other is None:
        return kept
    return jnp.where(lay.half == lay.core, kept, order(other).astype(F32))


def lane_matrix(heads):
    source = jnp.arange(heads * HEAD_DIM)
    head, offset = source // HEAD_DIM, source % HEAD_DIM
    target = head * LANES + (offset // HALF) * HALF_LANES + offset % HALF
    return (target[:, None] == jnp.arange(heads * LANES)[None, :]).astype(BF16)


def rot(vec, cos_t, sin_t):
    return vec * cos_t + pltpu.roll(vec, HALF_LANES, 1) * sin_t


def rot_back(vec, cos_t, sin_t):
    return vec * cos_t - pltpu.roll(vec, HALF_LANES, 1) * sin_t


def mm(a, b):
    return lax.dot_general(a, b, (((1,), (0,)), ((), ())), preferred_element_type=F32)


def mm_nt(a, b):
    return lax.dot_general(a, b, (((1,), (1,)), ((), ())), preferred_element_type=F32)


def mm_tn(a, b):
    return lax.dot_general(a, b, (((0,), (0,)), ((), ())), preferred_element_type=F32)


def heads_of(block, count):
    return jnp.concatenate([block[:, i * LANES : (i + 1) * LANES] for i in range(count)], 0)


def lanes_of(index, count=1):
    return slice(index * LANES, (index + count) * LANES)


def attend_kernel(
    n_query, n_key, raw_own, raw_sib, cos_t, sin_t, pos_q, pos_k, out_own, out_sib, lse_out, own, sib
):
    scale = HEAD_DIM ** (-0.5)
    per_key = n_query // n_key
    half = raw_own.shape[0]
    rows = 2 * half
    cos_v, sin_v = cos_t[...], sin_t[...]
    mask = pos_q[...] >= pos_k[...]
    mask = jnp.concatenate([mask] * per_key, 0)

    def both(index, turned):
        block = jnp.concatenate([raw_own[:, lanes_of(index)], raw_sib[:, lanes_of(index)]], 0)
        block = (rot(block, cos_v, sin_v) if turned else block).astype(BF16)
        own[:, lanes_of(index)] = block[:half]
        sib[:, lanes_of(index)] = block[half:]
        return block

    for kv_head in range(n_key):
        key, value = both(n_query + kv_head, True), both(n_query + n_key + kv_head, False)
        q_first = kv_head * per_key
        query = jnp.concatenate([both(q_first + i, True) for i in range(per_key)], 0)
        scores = jnp.where(mask, mm_nt(query, key) * scale, MASK_FILL)
        row_max = jnp.max(scores, -1, keepdims=True)
        weights = jnp.exp(scores - row_max)
        total = jnp.sum(weights, -1, keepdims=True)
        probs = (weights * (1.0 / total)).astype(BF16)
        out = mm(probs, value).astype(BF16)
        for i in range(per_key):
            out_own[:, lanes_of(q_first + i)] = out[i * rows : i * rows + half]
            out_sib[:, lanes_of(q_first + i)] = out[i * rows + half : (i + 1) * rows]
        lse_out[kv_head] = row_max + jnp.log(total)


def attend(raw_own, raw_sib, tables, n_query, n_key):
    half, lanes = raw_own.shape
    return pl.pallas_call(
        lambda *refs: attend_kernel(n_query, n_key, *refs),
        out_shape=[
            jax.ShapeDtypeStruct((half, n_query * LANES), BF16),
            jax.ShapeDtypeStruct((half, n_query * LANES), BF16),
            jax.ShapeDtypeStruct((n_key, n_query // n_key * 2 * half, 1), F32),
            jax.ShapeDtypeStruct((half, lanes), BF16),
            jax.ShapeDtypeStruct((half, lanes), BF16),
        ],
        compiler_params=VMEM_LIMIT,
        cost_estimate=pl.CostEstimate(flops=0, bytes_accessed=0, transcendentals=0),
        name="attend",
    )(raw_own, raw_sib, *tables)


def attend_back_kernel(
    n_query, n_key, own, sib, do_own, do_sib, lse, cos_t, sin_t, pos_q, pos_k, low_own, low_sib
):
    scale = HEAD_DIM ** (-0.5)
    per_key = n_query // n_key
    half = own.shape[0]
    rows = 2 * half
    cos_v, sin_v = cos_t[...], sin_t[...]
    mask = pos_q[...] >= pos_k[...]
    mask = jnp.concatenate([mask] * per_key, 0)

    def put(index, block):
        low_own[:, lanes_of(index)] = block[:half].astype(BF16)
        low_sib[:, lanes_of(index)] = block[half:].astype(BF16)

    def both(a, b, index):
        return jnp.concatenate([a[:, lanes_of(index)], b[:, lanes_of(index)]], 0)

    for kv_head in range(n_key):
        key, value = both(own, sib, n_query + kv_head), both(own, sib, n_query + n_key + kv_head)
        q_first = kv_head * per_key
        query = jnp.concatenate([both(own, sib, q_first + i) for i in range(per_key)], 0)
        grad = jnp.concatenate([both(do_own, do_sib, q_first + i) for i in range(per_key)], 0)
        scores = jnp.where(mask, mm_nt(query, key) * scale, MASK_FILL)
        probs = jnp.exp(scores - lse[kv_head])
        prob_grad = mm_nt(grad, value)
        delta = jnp.sum(probs * prob_grad, -1, keepdims=True)
        score_grad = (probs * (prob_grad - delta)).astype(BF16)
        dq = mm(score_grad, key) * scale
        for i in range(per_key):
            put(q_first + i, rot_back(dq[i * rows : (i + 1) * rows], cos_v, sin_v))
        put(n_query + kv_head, rot_back(mm_tn(score_grad, query) * scale, cos_v, sin_v))
        put(n_query + n_key + kv_head, mm_tn(probs.astype(BF16), grad))


def attend_back(kept, out_grads, tables, n_query, n_key):
    own, sib, lse = kept
    half, lanes = own.shape
    return pl.pallas_call(
        lambda *refs: attend_back_kernel(n_query, n_key, *refs),
        out_shape=[
            jax.ShapeDtypeStruct((half, lanes), BF16),
            jax.ShapeDtypeStruct((half, lanes), BF16),
        ],
        compiler_params=VMEM_LIMIT,
        cost_estimate=pl.CostEstimate(flops=0, bytes_accessed=0, transcendentals=0),
        name="attend_back",
    )(own, sib, *out_grads, lse, *tables)


def rows_start(block, lay, order):
    block = order(block)
    return block, [lay.to_member(block, step) for step in range(1, lay.group)]


def rows_middle(begun, lay, order):
    block, others = begun
    own = order(jnp.concatenate([block] + order.each(others), 0))
    return [own, lay.to_core(own)]


def rows_done(rows, order):
    rows[1] = order(rows[1])
    return rows


def sums_start(own, sib, lay, order):
    return own, lay.to_core(order(sib.astype(BF16)))


def sums_middle(begun, lay, order):
    own, got = begun
    own = own + order(got).astype(F32)
    rows = own.shape[0] // lay.group
    parts = own.reshape(lay.group, rows, -1)
    sent = order.each([parts[step].astype(BF16) for step in range(1, lay.group)])
    return parts[0], [lay.to_member(block, step) for step, block in enumerate(sent, 1)]


def sums_done(begun, order):
    total, others = begun
    for block in order.each(others):
        total = total + block.astype(F32)
    return total


def norm_forward(inputs, gain_vec):
    inverse_rms = lax.rsqrt(jnp.mean(inputs * inputs, -1, keepdims=True) + NORM_EPS)
    return (inputs * inverse_rms * gain_vec).astype(BF16), inverse_rms


def norm_backward(inputs, inverse_rms, gain_vec, upstream):
    scaled = upstream * gain_vec
    input_grad = inverse_rms * scaled - inputs * inverse_rms**3 * jnp.mean(
        scaled * inputs, -1, keepdims=True
    )
    gain_grad = jnp.sum(upstream * inputs * inverse_rms, 0)
    return input_grad, gain_grad


def out_order(block, lay, n_query):
    if head_copies(lay) > 1:
        share = (lay.core * lay.group + lay.member) % head_copies(lay) == 0
        return jnp.where(share, block, jnp.zeros_like(block))
    if n_query != 2 or lay.cores * lay.group != KV_HEADS:
        return block
    swapped = jnp.concatenate([block[:, LANES:], block[:, :LANES]], 1)
    return jnp.where(lay.shard == 0, block, swapped)


class Layer:
    def __init__(self, lay, tables, n_query, n_key, gain_one, gain_two):
        self.lay, self.tables, self.n_query, self.n_key = lay, tables, n_query, n_key
        self.gain_one, self.gain_two = gain_one, gain_two

    def first_norm(self, inputs):
        self.inputs = inputs
        normed, self.inverse_first = norm_forward(inputs, self.gain_one)
        return relative(normed, self.lay)

    def attend(self):
        raw = [mm(block, self.qkv_w) for block in self.normed]
        out_own, out_sib, lse, own, sib = attend(*raw, self.tables, self.n_query, self.n_key)
        self.attn_kept = own, sib, lse
        self.attn_out = [out_order(block, self.lay, self.n_query) for block in (out_own, out_sib)]

    def out_partial(self):
        return [mm(block, self.out_w) for block in self.attn_out]

    def second_norm(self, attended):
        self.mid_stream = self.inputs + attended
        normed, self.inverse_second = norm_forward(self.mid_stream, self.gain_two)
        return relative(normed, self.lay)

    def hide(self):
        self.gate_up, self.hidden = [], []
        for block in self.normed_mid:
            gate_pre, up_pre = mm(block, self.gate_w), mm(block, self.up_w)
            self.gate_up.append((gate_pre, up_pre))
            hidden = (jax.nn.silu(gate_pre) * up_pre).astype(BF16)
            self.hidden.append(relative(hidden, self.lay))

    def down_partial(self):
        return [mm(block, self.down_w) for block in self.hidden]

    def feed_forward_back(self):
        self.gate_grad, self.up_grad, partial = [], [], []
        for block, (gate_pre, up_pre) in zip(self.down_in, self.gate_up):
            hidden_grad = relative(mm_nt(block, self.down_w), self.lay)
            sigmoid_gate = jax.nn.sigmoid(gate_pre)
            gate_grad_in = (
                hidden_grad * up_pre * sigmoid_gate * (1.0 + gate_pre * (1.0 - sigmoid_gate))
            ).astype(BF16)
            up_grad_in = (hidden_grad * gate_pre * sigmoid_gate).astype(BF16)
            self.gate_grad.append(gate_grad_in)
            self.up_grad.append(up_grad_in)
            partial.append(mm_nt(gate_grad_in, self.gate_w) + mm_nt(up_grad_in, self.up_w))
        return partial

    def second_norm_back(self, out_grad, upstream):
        part, self.gain_two_grad = norm_backward(
            self.mid_stream, self.inverse_second, self.gain_two, relative(upstream, self.lay)
        )
        self.mid_grad = out_grad + part
        return self.mid_grad.astype(BF16)

    def attention_back(self, order):
        grads = [
            out_order(mm_nt(block, self.out_w).astype(BF16), self.lay, self.n_query)
            for block in self.mid_low
        ]
        self.lows = attend_back(self.attn_kept, grads, self.tables, self.n_query, self.n_key)
        self.lows = order.each(self.lows)
        return [mm_nt(block, self.qkv_w) for block in self.lows]

    def first_norm_back(self, upstream):
        part, gain_one_grad = norm_backward(
            self.inputs, self.inverse_first, self.gain_one, relative(upstream, self.lay)
        )
        self.gain_grads = jnp.stack([gain_one_grad, self.gain_two_grad])
        return self.mid_grad + part


def joined(pair):
    return jnp.concatenate(pair, 0)


def row_tables(pair_table, block_rows, lay):
    cores = []
    for core in (lay.core, 1 - lay.core):
        ctx_ids = jnp.stack([core * lay.group + (lay.member ^ step) for step in range(lay.group)])
        owned = jnp.sum(
            jnp.where(ctx_ids[:, None] == jnp.arange(lay.ctx)[None, :], pair_table[None, :], 0), 1
        )
        blocks = jnp.stack([owned, 2 * lay.ctx - 1 - owned], 1)
        rows = blocks[:, :, None] * block_rows + jnp.arange(block_rows)[None, None, :]
        cores.append(rows.reshape(-1))
    positions = jnp.concatenate(cores)
    freq_idx = jnp.arange(HALF, dtype=F32)
    inverse = ROPE_BASE ** (-2.0 * freq_idx / HEAD_DIM)
    angles = positions.astype(F32)[:, None] * inverse[None, :]
    pad = ((0, 0), (0, HALF_LANES - HALF))
    cos_h, sin_h = jnp.pad(jnp.cos(angles), pad), jnp.pad(jnp.sin(angles), pad)
    cos_t = jnp.concatenate([cos_h, cos_h], 1)
    sin_t = jnp.concatenate([-sin_h, sin_h], 1)
    return cos_t, sin_t, positions[:, None], positions[None, :]


def deal_rows(local, lay, order):
    turn = lay.half ^ lay.core
    sent = order(pick(local, turn), pick(local, 1 - turn))
    straight = lay.move(
        sent[0], lambda core, half, member, shard: (half, half ^ core, member, shard)
    )
    crossed = lay.move(
        sent[1], lambda core, half, member, shard: (half, 1 - (half ^ core), member, shard)
    )
    return straight, crossed


def dealt(straight, crossed, lay):
    turn = lay.half ^ lay.core
    return jnp.where(turn == 0, straight, crossed), jnp.where(turn == 0, crossed, straight)


def return_rows(input_grad, outputs, lay, order):
    turn = lay.half ^ lay.core
    sent = order(
        jnp.where(turn == 0, input_grad, outputs), jnp.where(turn == 0, outputs, input_grad)
    )
    straight = lay.move(
        sent[0], lambda core, half, member, shard: (core ^ half, core, member, shard)
    )
    crossed = lay.move(
        sent[1], lambda core, half, member, shard: (1 - (core ^ half), core, member, shard)
    )
    return straight, crossed


def body(
    ends_in, pair_table, norm_attn, w_query, w_key, w_value, w_out, norm_mlp, w_gate, w_up, w_down
):
    lay = Layout()
    rows = ends_in.shape[3]
    width = ends_in.shape[4]
    row_block = w_query.shape[1]
    pairs = lay.cores * lay.group
    n_query = max(1, HEADS // pairs)
    n_key = max(1, KV_HEADS // pairs)
    ff_unit = w_down.shape[1] // lay.cores
    q_cols, k_cols = n_query * HEAD_DIM, n_key * HEAD_DIM
    spread_lanes = lane_matrix(n_query + 2 * n_key)
    spread_out = lane_matrix(n_query)
    cols = q_cols + 2 * k_cols
    ff = ff_unit * 4
    order = Order()

    def by_member(*blocks):
        return jnp.concatenate(blocks, 1).reshape(lay.group, row_block, -1)

    tables = row_tables(pair_table, rows // 2, lay)
    gains = jnp.stack([norm_attn[0], norm_mlp[0]])
    gain_parts = [lay.to_member(gains, step) for step in range(1, lay.group)]
    heads = pack_heads(w_query[0], w_key[0], w_value[0], lay)
    heads_other = split_cores(heads, lay, order)
    heads_other, *gain_parts = order(heads_other, *gain_parts)
    qkv_layers = core_layers(heads, heads_other, lay)
    qkv_others = to_members(qkv_layers[0], lay, order)
    gains = order(place(gains, gain_parts, lay.member))
    gains_other = lay.to_half(gains)
    w_gate, w_up, ends_in = order(w_gate, w_up, ends_in)
    own_rows = to_inner(ends_in[0, :, 0], lay)
    gate_up_own = pack_ff(w_gate[0], w_up[0], lay, ff_unit)
    gate_up_other = split_cores(gate_up_own, lay, order)
    rows_other = deal_rows(own_rows, lay, order)
    qkv_0 = Spread(member_rows(qkv_layers[0], order.each(qkv_others), lay), lay, order)
    qkv_0.half()
    gains = order(two_way(lay.half, gains, order(gains_other), 0))
    gains_other = lay.to_shard(gains)
    gains = order(two_way(lay.shard, gains, order(gains_other), 0))
    gains_other = lay.to_core(gains)
    out = SpreadOut(to_inner(order(w_out)[0], lay), lay, order)
    out.core()
    gains = two_way(lay.core, gains, order(gains_other), 0)
    gains = gains.transpose(0, 4, 1, 2, 3, 5).reshape(2, 2, -1).astype(F32)
    gate_up_layers = core_layers(gate_up_own, order(gate_up_other), lay)
    out.core_done()
    own_in, own_cot = dealt(*order(*rows_other), lay)
    first = Layer(lay, tables, n_query, n_key, gains[0, 0], gains[0, 1])
    second = Layer(lay, tables, n_query, n_key, gains[1, 0], gains[1, 1])
    normed = rows_start(first.first_norm(own_in.astype(F32)), lay, order)
    qkv_0.half_done()
    qkv_0.shard()
    out.half()
    normed = rows_middle(normed, lay, order)
    gate_up_others = to_members(gate_up_layers[0], lay, order)
    qkv_0.shard_done()
    out.half_done()
    out.shard()
    first.qkv_w = mm(qkv_0.full, spread_lanes).astype(BF16)
    first.normed = rows_done(normed, order)
    first.attend()
    first.attn_out = order.each(first.attn_out)
    gate_up = member_rows(gate_up_layers[0], order.each(gate_up_others), lay)
    gate_0 = Spread(gate_up[:, :ff], lay, order)
    up_0 = Spread(gate_up[:, ff:], lay, order)
    gate_0.half()
    down_own = to_inner(order(w_down)[0], lay).reshape(lay.cores, ff_unit, width)
    down_other = split_cores(down_own, lay, order)
    out.shard_done()
    first.out_w = mm_tn(spread_out, out.full[0]).astype(BF16)
    second.out_w = mm_tn(spread_out, out.full[1]).astype(BF16)
    sums = sums_middle(sums_start(*first.out_partial(), lay, order), lay, order)
    down_layers = core_layers(down_own, order(down_other), lay)
    down_0, down_1 = Spread(down_layers[0], lay, order), Spread(down_layers[1], lay, order)
    attended = sums_done(sums, order)
    gate_0.half_done()
    gate_0.shard()
    up_0.half()
    normed = rows_start(first.second_norm(attended), lay, order)
    normed = rows_middle(normed, lay, order)
    rest = jnp.concatenate([qkv_layers[1], gate_up_layers[1]], -1)
    rest_others = to_members(rest, lay, order)
    up_0.half_done()
    gate_0.shard_done()
    up_0.shard()
    down_0.half()
    first.normed_mid = rows_done(normed, order)
    rest = member_rows(rest, order.each(rest_others), lay)
    qkv_1 = Spread(rest[:, :cols], lay, order)
    gate_up_1 = Spread(rest[:, cols:], lay, order)
    up_0.shard_done()
    down_0.half_done()
    down_0.shard()
    own_cot = own_cot.astype(F32)
    cot = rows_start(own_cot.astype(BF16), lay, order)
    qkv_1.half()
    first.gate_w, first.up_w = gate_0.full, up_0.full
    first.hide()
    second.down_in = rows_middle(cot, lay, order)
    qkv_1.half_done()
    gate_up_1.half()
    down_0.shard_done()
    qkv_1.shard()
    first.down_w = down_0.full
    sums = sums_middle(sums_start(*first.down_partial(), lay, order), lay, order)
    first_out = first.mid_stream + sums_done(sums, order)
    normed = rows_start(second.first_norm(first_out.astype(BF16).astype(F32)), lay, order)
    normed = rows_middle(normed, lay, order)
    gate_up_1.half_done()
    gate_up_1.shard()
    down_1.half()
    qkv_1.shard_done()
    second.qkv_w = mm(qkv_1.full, spread_lanes).astype(BF16)
    second.normed = rows_done(normed, order)
    second.attend()
    sums = sums_start(*second.out_partial(), lay, order)
    sums = sums_middle(sums, lay, order)
    attended = sums_done(sums, order)
    gate_up_1.shard_done()
    down_1.half_done()
    down_1.shard()
    normed = rows_start(second.second_norm(attended), lay, order)
    normed = rows_middle(normed, lay, order)
    second.gate_w, second.up_w = gate_up_1.full[:, :ff], gate_up_1.full[:, ff:]
    second.normed_mid = rows_done(normed, order)
    second.down_in = rows_done(second.down_in, order)
    second.hide()

    down_g1 = Collect(joined(second.hidden), joined(second.down_in), lay, order)
    down_g1.shard()
    down_1.shard_done()
    second.down_w = down_1.full
    partial = second.feed_forward_back()
    sums = sums_start(*partial, lay, order)
    grads = [jnp.concatenate(pair, 1) for pair in zip(second.gate_grad, second.up_grad)]
    gate_up_g1 = Collect(joined(second.normed_mid), joined(grads), lay, order)
    sums = sums_middle(sums, lay, order)
    gate_up_g1.shard()
    upstream = sums_done(sums, order)
    low = second.second_norm_back(own_cot, upstream)
    down_g1.shard_done()
    low = rows_start(low, lay, order)
    low = rows_middle(low, lay, order)
    down_g1.half()
    second.mid_low = rows_done(low, order)
    partial = second.attention_back(order)
    sums = sums_start(*partial, lay, order)
    low = mm_nt(joined(second.lows), spread_lanes).astype(BF16)
    qkv_g1 = Collect(joined(second.normed), low, lay, order)
    gate_up_g1.shard_done()
    qkv_g1.shard()
    sums = sums_middle(sums, lay, order)
    upstream = sums_done(sums, order)
    down_g1.half_done()
    gate_up_g1.half()
    second_grad = second.first_norm_back(upstream)

    first_cot = second_grad.astype(BF16)
    down_in = rows_start(first_cot, lay, order)
    down_in = rows_middle(down_in, lay, order)
    first.down_in = rows_done(down_in, order)
    down_g0 = Collect(joined(first.hidden), joined(first.down_in), lay, order)
    qkv_g1.shard_done()
    down_g0.shard()
    partial = first.feed_forward_back()
    sums = sums_start(*partial, lay, order)
    left = joined(first.normed_mid)
    gate_g0 = Collect(left, joined(first.gate_grad), lay, order)
    up_g0 = Collect(left, joined(first.up_grad), lay, order)
    sums = sums_middle(sums, lay, order)
    upstream = sums_done(sums, order)
    gate_up_g1.half_done()
    qkv_g1.half()
    low = rows_start(first.second_norm_back(first_cot.astype(F32), upstream), lay, order)
    down_g0.shard_done()
    gate_g0.shard()
    low = rows_middle(low, lay, order)
    qkv_g1.half_done()
    down_g0.half()
    first.mid_low = rows_done(low, order)
    partial = first.attention_back(order)
    gate_g0.shard_done()
    up_g0.shard()
    down_g0.half_done()
    gate_g0.half()
    sums = sums_start(*partial, lay, order)
    low = mm_nt(joined(first.lows), spread_lanes).astype(BF16)
    qkv_g0 = Collect(joined(first.normed), low, lay, order)
    sums = sums_middle(sums, lay, order)
    upstream = sums_done(sums, order)
    first_grad = first.first_norm_back(upstream)

    out_both = CollectOut(
        [out_pair(which, spread_out) for which in (first, second)], lay, order, row_block
    )
    up_g0.shard_done()
    up_g0.half()
    qkv_g0.shard()
    mlp_1 = by_member(gate_up_g1.total)
    others_1 = to_members(mlp_1.astype(BF16), lay, order)
    gate_g0.half_done()
    up_g0.half_done()
    others_1 = order.each(others_1)
    gains = jnp.stack([first.gain_grads, second.gain_grads])
    gains_other = lay.to_core(order(pick(gains, 1 - lay.core)))
    mlp_0 = by_member(gate_g0.total, up_g0.total)
    others_0 = to_members(mlp_0.astype(BF16), lay, order)
    qkv_g0.shard_done()
    qkv_g0.half()
    out_both.shard()
    outputs = sums_start(*second.down_partial(), lay, order)
    down_join = join_cores(down_g0.total, down_g1.total, lay, order)
    back_1 = place(pick(mlp_1, lay.member), [block.astype(F32) for block in others_1], lay.member)
    others_0 = order.each(others_0)
    gains = pick(gains, lay.core) + order(gains_other)
    gains = gains.reshape(2, lay.shards, lay.halves, lay.group, -1).transpose(1, 2, 3, 0, 4)
    outputs = sums_middle(outputs, lay, order)
    back_0 = place(pick(mlp_0, lay.member), [block.astype(F32) for block in others_0], lay.member)
    ff_join = join_cores(back_0, back_1, lay, order)
    out_both.shard_done()
    out_both.half()
    gains_other = lay.to_shard(order(pick(gains, 1 - lay.shard)))
    second_out = second.mid_stream + sums_done(outputs, order)
    qkv_g0.half_done()
    attn = by_member(qkv_g0.total, qkv_g1.total)
    others_q = to_members(attn.astype(BF16), lay, order)
    rows_other = return_rows(first_grad.astype(BF16), second_out.astype(BF16), lay, order)
    gains = pick(gains, lay.shard) + order(gains_other)
    gains_other = lay.to_half(order(pick(gains, 1 - lay.half)))
    gate_up_g = order.each(unpack_ff(joined_cores(ff_join, lay, order), lay, ff_unit))
    others_q = order.each(others_q)
    back_q = place(pick(attn, lay.member), [block.astype(F32) for block in others_q], lay.member)
    qkv_join = join_cores(back_q[..., :cols], back_q[..., cols:], lay, order)
    out_both.half_done()
    out_join = join_out_start(*out_both.total, lay, order, row_block)
    gains = pick(gains, lay.half) + order(gains_other)
    gain_g = pick(gains, lay.member)
    gain_others = to_members(gains, lay, order)
    down_g = to_outer(joined_cores(down_join, lay, order).reshape(-1, width), lay)
    qkv_g = unpack_heads(joined_cores(qkv_join, lay, order), lay)
    straight, crossed = order(*rows_other)
    ends = two_way(lay.half ^ lay.core, straight, crossed, 0)
    out_g = to_outer(join_out(out_join, lay, order), lay)
    for block in order.each(gain_others):
        gain_g = gain_g + block
    ends = to_outer(ends, lay)
    return (
        ends[None, :, None],
        gain_g[0][None],
        qkv_g[0][None],
        qkv_g[1][None],
        qkv_g[2][None],
        out_g[None],
        gain_g[1][None],
        gate_up_g[0][None],
        gate_up_g[1][None],
        down_g[None],
    )


def solution(mesh):
    rows = P("section", None, "shard", "ctx", None)
    vector = P("section", ("ctx", "shard"))
    matrix = P("section", ("ctx", "shard"), None)
    return jax.shard_map(
        body,
        mesh=mesh,
        in_specs=(rows, P(), vector, matrix, matrix, matrix, matrix, vector, matrix, matrix, matrix),
        out_specs=(rows, vector, matrix, matrix, matrix, matrix, vector, matrix, matrix, matrix),
        check_vma=False,
    )
```

```python
import jax
import jax.numpy as jnp
from jax import lax
from jax.experimental import pallas as pl
from jax.experimental.pallas import tpu as pltpu
from jax.sharding import PartitionSpec as P

HEADS = 16
KV_HEADS = 8
HEAD_DIM = 96
HALF = HEAD_DIM // 2
LANES = 128
HALF_LANES = LANES // 2

NORM_EPS = 1e-05
ROPE_BASE = 100000.0
MASK_FILL = -1e30

MESH_AXES = ("section", "ctx", "shard")
F32 = jnp.float32
BF16 = jnp.bfloat16
VMEM_LIMIT = pltpu.CompilerParams(vmem_limit_bytes=56 * 1024 * 1024)


class Layout:
    def __init__(self):
        self.cores = lax.axis_size("section")
        self.ctx = lax.axis_size("ctx")
        self.shards = lax.axis_size("shard")
        self.halves = 2
        self.group = self.ctx // self.halves
        ctx_index = lax.axis_index("ctx")
        self.core = lax.axis_index("section")
        self.half = ctx_index // self.group
        self.member = ctx_index % self.group
        self.shard = lax.axis_index("shard")

    def move(self, block, target):
        pairs = []
        for core in range(self.cores):
            for half in range(self.halves):
                for member in range(self.group):
                    for shard in range(self.shards):
                        to = target(core, half, member, shard)
                        pairs.append((self.flat(core, half, member, shard), self.flat(*to)))
        return lax.ppermute(block, MESH_AXES, pairs)

    def move_some(self, block, sends, target):
        pairs = []
        for core in range(self.cores):
            for half in range(self.halves):
                for member in range(self.group):
                    for shard in range(self.shards):
                        if sends(core, half, member, shard):
                            to = target(core, half, member, shard)
                            pairs.append((self.flat(core, half, member, shard), self.flat(*to)))
        return lax.ppermute(block, MESH_AXES, pairs)

    def flat(self, core, half, member, shard):
        return (core * self.ctx + half * self.group + member) * self.shards + shard

    def to_member(self, block, step):
        return self.move(block, lambda core, half, member, shard: (core, half, member ^ step, shard))

    def to_half(self, block):
        return self.move(block, lambda core, half, member, shard: (core, 1 - half, member, shard))

    def to_shard(self, block):
        return self.move(block, lambda core, half, member, shard: (core, half, member, 1 - shard))

    def to_core(self, block):
        return self.move(block, lambda core, half, member, shard: (1 - core, half, member, shard))


def pick(parts, index):
    return lax.dynamic_index_in_dim(parts, index, 0, False)


class Order:
    def __init__(self):
        self.last = ()

    def __call__(self, *blocks):
        if self.last:
            blocks = lax.optimization_barrier(tuple(blocks) + self.last)[: len(blocks)]
        self.last = (blocks[0],)
        return blocks[0] if len(blocks) == 1 else blocks

    def each(self, blocks):
        blocks = self(*blocks)
        return list(blocks) if isinstance(blocks, (tuple, list)) else [blocks]


def two_way(index, own, other, axis):
    first = jnp.where(index == 0, own, other)
    second = jnp.where(index == 0, other, own)
    return jnp.stack([first, second], axis)


def rearrange_kernel(plans, count, *refs):
    sources, outs = refs[:count], refs[count:]
    for out, plan in zip(outs, plans):
        for index, pieces in plan:
            blocks = [
                sources[source][place + (slice(None), slice(column, column + width))]
                for source, place, column, width in pieces
            ]
            out[index] = jnp.concatenate(blocks, 1) if len(blocks) > 1 else blocks[0]


def rearrange(sources, shapes, plans):
    dtype = sources[0].dtype
    moved = sum(source.size for source in sources) * dtype.itemsize
    return pl.pallas_call(
        lambda *refs: rearrange_kernel(plans, len(sources), *refs),
        out_shape=[jax.ShapeDtypeStruct(shape, dtype) for shape in shapes],
        compiler_params=VMEM_LIMIT,
        cost_estimate=pl.CostEstimate(flops=0, bytes_accessed=0, transcendentals=0),
        name="rearrange",
    )(*sources)


def kernel_width(width):
    return width % HEAD_DIM == 0 or width % LANES == 0


def to_inner(block, lay, inner=True):
    blocks = lay.shards * lay.halves * lay.group
    width = block.shape[-1] // blocks
    outer_order = [
        ((half * lay.group + member) * lay.shards + shard) * width
        for shard in range(lay.shards)
        for half in range(lay.halves)
        for member in range(lay.group)
    ]
    if kernel_width(width):
        columns = outer_order
        if not inner:
            columns = [outer_order.index(i * width) * width for i in range(blocks)]
        flat = block.reshape(-1, block.shape[-1])
        plan = [((slice(None), slice(None)), [(0, (), column, width) for column in columns])]
        return rearrange([flat], [flat.shape], [plan])[0].reshape(block.shape)
    if inner:
        parts = block.reshape(block.shape[:-1] + (lay.halves, lay.group, lay.shards, -1))
        return jnp.moveaxis(parts, -2, -4).reshape(block.shape)
    parts = block.reshape(block.shape[:-1] + (lay.shards, lay.halves, lay.group, -1))
    return jnp.moveaxis(parts, -4, -2).reshape(block.shape)


def to_outer(block, lay):
    return to_inner(block, lay, False)


def relative(block, lay):
    width = block.shape[-1] // 4
    parts = [block[..., i * width : (i + 1) * width] for i in range(4)]
    parts = [jnp.where(lay.half == 0, parts[i], parts[i ^ 1]) for i in range(4)]
    parts = [jnp.where(lay.shard == 0, parts[i], parts[i ^ 2]) for i in range(4)]
    return jnp.concatenate(parts, -1)


def head_copies(lay):
    return max(1, lay.cores * lay.group // HEADS)


def split_heads(weight, lay, heads):
    rows = weight.shape[0]
    pairs = lay.cores * lay.group
    distinct = min(pairs, heads)
    parts = weight.reshape(rows, distinct, -1).transpose(1, 0, 2)
    parts = jnp.repeat(parts, pairs // distinct, axis=0) if pairs > distinct else parts
    return parts.reshape((lay.cores, lay.group) + parts.shape[1:])


def merge_heads(parts, lay, heads):
    pairs = lay.cores * lay.group
    distinct = min(pairs, heads)
    rows = parts.shape[2]
    parts = parts.reshape(distinct, pairs // distinct, rows, -1)
    parts = jnp.sum(parts, 1) if pairs > distinct else parts[:, 0]
    return parts.transpose(1, 0, 2).reshape(rows, -1)


def split_ff(weight, lay, unit):
    rows = weight.shape[0]
    parts = weight.reshape(rows, lay.halves, lay.group, lay.shards, lay.cores, unit)
    return parts.transpose(4, 2, 0, 3, 1, 5).reshape(lay.cores, lay.group, rows, -1)


def merge_ff(parts, lay, unit):
    rows = parts.shape[2]
    parts = parts.reshape(lay.cores, lay.group, rows, lay.shards, lay.halves, unit)
    return parts.transpose(2, 4, 1, 3, 0, 5).reshape(rows, -1)


def pack_heads(query, key, value, lay):
    pairs = lay.cores * lay.group
    if pairs != KV_HEADS or query.shape[0] % 16:
        sides = [(query, HEADS), (key, KV_HEADS), (value, KV_HEADS)]
        return jnp.concatenate([split_heads(block, lay, heads) for block, heads in sides], -1)
    wide, slim = query.shape[1] // pairs, key.shape[1] // pairs
    plan = []
    for pair in range(pairs):
        pieces = [(0, (), pair * wide, wide), (1, (), pair * slim, slim), (2, (), pair * slim, slim)]
        plan.append(((pair // lay.group, pair % lay.group), pieces))
    shape = (lay.cores, lay.group, query.shape[0], wide + 2 * slim)
    return rearrange([query, key, value], [shape], [plan])[0]


def unpack_heads(parts, lay):
    pairs = lay.cores * lay.group
    q_cols = max(1, HEADS // pairs) * HEAD_DIM
    k_cols = max(1, KV_HEADS // pairs) * HEAD_DIM
    if pairs != KV_HEADS:
        sides = [(0, q_cols, HEADS), (q_cols, k_cols, KV_HEADS), (q_cols + k_cols, k_cols, KV_HEADS)]
        parts = jnp.stack(parts)
        return [merge_heads(parts[..., at : at + cols], lay, heads) for at, cols, heads in sides]
    rows = parts[0].shape[1]
    plans, shapes = [], []
    for first, cols in ((0, q_cols), (q_cols, k_cols), (q_cols + k_cols, k_cols)):
        pieces = [(pair // lay.group, (pair % lay.group,), first, cols) for pair in range(pairs)]
        plans.append([((slice(None), slice(None)), pieces)])
        shapes.append((rows, pairs * cols))
    return rearrange(parts, shapes, plans)


def ff_columns(lay, core, member, unit):
    for shard in range(lay.shards):
        for half in range(lay.halves):
            block = (half * lay.group + member) * lay.shards + shard
            yield (block * lay.cores + core) * unit, shard * lay.halves + half


def pack_ff(gate, up, lay, unit):
    if not kernel_width(unit):
        return jnp.concatenate([split_ff(gate, lay, unit), split_ff(up, lay, unit)], -1)
    plan = []
    for core in range(lay.cores):
        for member in range(lay.group):
            columns = [column for column, _ in ff_columns(lay, core, member, unit)]
            pieces = [(side, (), column, unit) for side in (0, 1) for column in columns]
            plan.append(((core, member), pieces))
    shape = (lay.cores, lay.group, gate.shape[0], 8 * unit)
    return rearrange([gate, up], [shape], [plan])[0]


def unpack_ff(parts, lay, unit):
    ff = 4 * unit
    if not kernel_width(unit):
        parts = jnp.stack(parts)
        return [merge_ff(parts[..., :ff], lay, unit), merge_ff(parts[..., ff:], lay, unit)]
    rows = parts[0].shape[1]
    plans = []
    for side in (0, 1):
        found = {}
        for core in range(lay.cores):
            for member in range(lay.group):
                for column, place in ff_columns(lay, core, member, unit):
                    found[column] = (core, (member,), side * ff + place * unit, unit)
        pieces = [found[column] for column in sorted(found)]
        plans.append([((slice(None), slice(None)), pieces)])
    return rearrange(parts, [(rows, len(found) * unit)] * 2, plans)


def place(own, others, member):
    group = 1 + len(others)
    stacked = jnp.zeros((group,) + own.shape, own.dtype)
    for step, block in enumerate((own,) + tuple(others)):
        stacked = lax.dynamic_update_index_in_dim(stacked, block, member ^ step, 0)
    return stacked


def split_cores(parts, lay, order):
    return lay.to_core(order(pick(parts, 1 - lay.core)))


def core_layers(parts, other, lay):
    kept = pick(parts, lay.core)
    return jnp.where(lay.core == 0, kept, other), jnp.where(lay.core == 0, other, kept)


def to_members(parts, lay, order):
    sent = order.each([pick(parts, lay.member ^ step) for step in range(1, lay.group)])
    return [lay.to_member(block, step) for step, block in enumerate(sent, 1)]


def member_rows(parts, others, lay):
    return place(pick(parts, lay.member), others, lay.member).reshape(-1, parts.shape[-1])


class Spread:
    def __init__(self, block, lay, order):
        self.block, self.lay, self.order = block, lay, order

    def half(self):
        self.got = self.lay.to_half(self.order(self.block))

    def half_done(self):
        self.pair = jnp.concatenate([self.block, self.order(self.got)], 0)

    def shard(self):
        self.got = self.lay.to_shard(self.order(self.pair))

    def shard_done(self):
        self.full = jnp.concatenate([self.pair, self.order(self.got)], 0)


class Collect:
    def __init__(self, left, right, lay, order):
        self.left, self.right, self.lay, self.order = left, right, lay, order
        self.rows = left.shape[1] // 4

    def shard(self):
        block = mm_tn(self.left[:, 2 * self.rows :], self.right).astype(BF16)
        self.got = self.lay.to_shard(self.order(block))

    def shard_done(self):
        self.got, self.left = self.order(self.got, self.left)

    def half(self):
        rows, got = self.rows, self.got.astype(F32)
        kept = mm_tn(self.left[:, : 2 * rows], self.right)
        self.kept = kept[:rows] + got[:rows]
        self.got = self.lay.to_half(self.order((kept[rows:] + got[rows:]).astype(BF16)))

    def half_done(self):
        self.total = self.kept + self.order(self.got).astype(F32)


def join_cores(first, second, lay, order):
    sent = order(jnp.where(lay.core == 0, second, first).astype(BF16))
    return jnp.where(lay.core == 0, first, second), lay.to_core(sent)


def joined_cores(pair, lay, order):
    kept, other = pair[0], order(pair[1]).astype(F32)
    return [jnp.where(lay.core == 0, kept, other), jnp.where(lay.core == 0, other, kept)]


def out_aligned(lay, block_rows):
    return block_rows == HEAD_DIM and lay.cores * lay.group == KV_HEADS and lay.cores == lay.halves


class SpreadOut:
    def __init__(self, w_out, lay, order):
        self.lay, self.order, self.width = lay, order, w_out.shape[-1]
        self.aligned = out_aligned(lay, w_out.shape[0])
        if not self.aligned:
            w_out = lax.all_gather(w_out, MESH_AXES[1:], axis=0, tiled=True)
        self.own = w_out

    def core(self):
        self.got = self.lay.to_core(self.order(self.own))

    def core_done(self):
        lay, other = self.lay, self.order(self.got)
        self.block = jnp.stack(
            [jnp.where(lay.core == 0, self.own, other), jnp.where(lay.core == 0, other, self.own)]
        )

    def half(self):
        if self.aligned:
            self.got = self.lay.move_some(
                self.order(self.block),
                lambda core, half, member, shard: half == core,
                lambda core, half, member, shard: (core, 1 - half, member, shard),
            )

    def half_done(self):
        if self.aligned:
            lay = self.lay
            self.block = jnp.where(lay.half == lay.core, self.block, self.order(self.got))

    def shard(self):
        if self.aligned:
            self.got = self.lay.to_shard(self.order(self.block))

    def shard_done(self):
        if self.aligned:
            self.full = jnp.concatenate([self.block, self.order(self.got)], 1)
            return
        lay = self.lay
        head = (lay.core * lay.group + lay.member) // head_copies(lay)
        count = max(1, HEADS // (lay.cores * lay.group)) * HEAD_DIM
        self.full = lax.dynamic_slice_in_dim(self.block, head * count, count, 1)


def out_pair(which, spread_out):
    return mm_nt(joined(which.attn_out), spread_out).astype(BF16), joined(which.mid_low)


class CollectOut:
    def __init__(self, pairs, lay, order, block_rows):
        self.pairs, self.lay, self.order = pairs, lay, order
        self.aligned = out_aligned(lay, block_rows)
        self.rows = pairs[0][0].shape[1] // 2

    def shard(self):
        if not self.aligned:
            self.total = [mm_tn(left, right) for left, right in self.pairs]
            return
        blocks = [mm_tn(left[:, self.rows :], right).astype(BF16) for left, right in self.pairs]
        self.got = self.lay.to_shard(self.order(jnp.concatenate(blocks, 0)))

    def shard_done(self):
        if self.aligned:
            self.got = self.order(self.got)

    def half(self):
        if not self.aligned:
            return
        blocks = [mm_tn(left[:, : self.rows], right) for left, right in self.pairs]
        self.kept = jnp.concatenate(blocks, 0) + self.got.astype(F32)
        self.got = self.lay.move_some(
            self.order(self.kept.astype(BF16)),
            lambda core, half, member, shard: half != core,
            lambda core, half, member, shard: (core, 1 - half, member, shard),
        )

    def half_done(self):
        if self.aligned:
            total = self.kept + self.order(self.got).astype(F32)
            self.total = total[: self.rows], total[self.rows :]


def join_out_start(first, second, lay, order, block_rows):
    if not out_aligned(lay, block_rows):
        width = first.shape[1]
        head = (lay.core * lay.group + lay.member) // head_copies(lay)
        full = jnp.zeros((2, HEADS * HEAD_DIM, width), F32)
        full = lax.dynamic_update_slice_in_dim(
            full, jnp.stack([first, second]), head * first.shape[0], 1
        )
        full = pick(lax.psum(full, MESH_AXES), lay.core)
        block = (lay.half * lay.group + lay.member) * lay.shards + lay.shard
        return lax.dynamic_slice_in_dim(full, block * block_rows, block_rows, 0), None
    return join_cores(first, second, lay, order)


def join_out(pair, lay, order):
    kept, other = pair
    if other is None:
        return kept
    return jnp.where(lay.half == lay.core, kept, order(other).astype(F32))


def lane_matrix(heads):
    source = jnp.arange(heads * HEAD_DIM)
    head, offset = source // HEAD_DIM, source % HEAD_DIM
    target = head * LANES + (offset // HALF) * HALF_LANES + offset % HALF
    return (target[:, None] == jnp.arange(heads * LANES)[None, :]).astype(BF16)


def rot(vec, cos_t, sin_t):
    return vec * cos_t + pltpu.roll(vec, HALF_LANES, 1) * sin_t


def rot_back(vec, cos_t, sin_t):
    return vec * cos_t - pltpu.roll(vec, HALF_LANES, 1) * sin_t


def mm(a, b):
    return lax.dot_general(a, b, (((1,), (0,)), ((), ())), preferred_element_type=F32)


def mm_nt(a, b):
    return lax.dot_general(a, b, (((1,), (1,)), ((), ())), preferred_element_type=F32)


def mm_tn(a, b):
    return lax.dot_general(a, b, (((0,), (0,)), ((), ())), preferred_element_type=F32)


def heads_of(block, count):
    return jnp.concatenate([block[:, i * LANES : (i + 1) * LANES] for i in range(count)], 0)


def lanes_of(index, count=1):
    return slice(index * LANES, (index + count) * LANES)


def attend_kernel(
    n_query, n_key, raw_own, raw_sib, cos_t, sin_t, pos_q, pos_k, out_own, out_sib, lse_out, own, sib
):
    scale = HEAD_DIM ** (-0.5)
    per_key = n_query // n_key
    half = raw_own.shape[0]
    rows = 2 * half
    cos_v, sin_v = cos_t[...], sin_t[...]
    mask = pos_q[...] >= pos_k[...]
    mask = jnp.concatenate([mask] * per_key, 0)

    def both(index, turned):
        block = jnp.concatenate([raw_own[:, lanes_of(index)], raw_sib[:, lanes_of(index)]], 0)
        block = (rot(block, cos_v, sin_v) if turned else block).astype(BF16)
        own[:, lanes_of(index)] = block[:half]
        sib[:, lanes_of(index)] = block[half:]
        return block

    for kv_head in range(n_key):
        key, value = both(n_query + kv_head, True), both(n_query + n_key + kv_head, False)
        q_first = kv_head * per_key
        query = jnp.concatenate([both(q_first + i, True) for i in range(per_key)], 0)
        scores = jnp.where(mask, mm_nt(query, key) * scale, MASK_FILL)
        row_max = jnp.max(scores, -1, keepdims=True)
        weights = jnp.exp(scores - row_max)
        total = jnp.sum(weights, -1, keepdims=True)
        probs = (weights * (1.0 / total)).astype(BF16)
        out = mm(probs, value).astype(BF16)
        for i in range(per_key):
            out_own[:, lanes_of(q_first + i)] = out[i * rows : i * rows + half]
            out_sib[:, lanes_of(q_first + i)] = out[i * rows + half : (i + 1) * rows]
        lse_out[kv_head] = row_max + jnp.log(total)


def attend(raw_own, raw_sib, tables, n_query, n_key):
    half, lanes = raw_own.shape
    return pl.pallas_call(
        lambda *refs: attend_kernel(n_query, n_key, *refs),
        out_shape=[
            jax.ShapeDtypeStruct((half, n_query * LANES), BF16),
            jax.ShapeDtypeStruct((half, n_query * LANES), BF16),
            jax.ShapeDtypeStruct((n_key, n_query // n_key * 2 * half, 1), F32),
            jax.ShapeDtypeStruct((half, lanes), BF16),
            jax.ShapeDtypeStruct((half, lanes), BF16),
        ],
        compiler_params=VMEM_LIMIT,
        cost_estimate=pl.CostEstimate(flops=0, bytes_accessed=0, transcendentals=0),
        name="attend",
    )(raw_own, raw_sib, *tables)


def attend_back_kernel(
    n_query, n_key, own, sib, do_own, do_sib, lse, cos_t, sin_t, pos_q, pos_k, low_own, low_sib
):
    scale = HEAD_DIM ** (-0.5)
    per_key = n_query // n_key
    half = own.shape[0]
    rows = 2 * half
    cos_v, sin_v = cos_t[...], sin_t[...]
    mask = pos_q[...] >= pos_k[...]
    mask = jnp.concatenate([mask] * per_key, 0)

    def put(index, block):
        low_own[:, lanes_of(index)] = block[:half].astype(BF16)
        low_sib[:, lanes_of(index)] = block[half:].astype(BF16)

    def both(a, b, index):
        return jnp.concatenate([a[:, lanes_of(index)], b[:, lanes_of(index)]], 0)

    for kv_head in range(n_key):
        key, value = both(own, sib, n_query + kv_head), both(own, sib, n_query + n_key + kv_head)
        q_first = kv_head * per_key
        query = jnp.concatenate([both(own, sib, q_first + i) for i in range(per_key)], 0)
        grad = jnp.concatenate([both(do_own, do_sib, q_first + i) for i in range(per_key)], 0)
        scores = jnp.where(mask, mm_nt(query, key) * scale, MASK_FILL)
        probs = jnp.exp(scores - lse[kv_head])
        prob_grad = mm_nt(grad, value)
        delta = jnp.sum(probs * prob_grad, -1, keepdims=True)
        score_grad = (probs * (prob_grad - delta)).astype(BF16)
        dq = mm(score_grad, key) * scale
        for i in range(per_key):
            put(q_first + i, rot_back(dq[i * rows : (i + 1) * rows], cos_v, sin_v))
        put(n_query + kv_head, rot_back(mm_tn(score_grad, query) * scale, cos_v, sin_v))
        put(n_query + n_key + kv_head, mm_tn(probs.astype(BF16), grad))


def attend_back(kept, out_grads, tables, n_query, n_key):
    own, sib, lse = kept
    half, lanes = own.shape
    return pl.pallas_call(
        lambda *refs: attend_back_kernel(n_query, n_key, *refs),
        out_shape=[
            jax.ShapeDtypeStruct((half, lanes), BF16),
            jax.ShapeDtypeStruct((half, lanes), BF16),
        ],
        compiler_params=VMEM_LIMIT,
        cost_estimate=pl.CostEstimate(flops=0, bytes_accessed=0, transcendentals=0),
        name="attend_back",
    )(own, sib, *out_grads, lse, *tables)


def rows_start(block, lay, order):
    block = order(block)
    return block, [lay.to_member(block, step) for step in range(1, lay.group)]


def rows_middle(begun, lay, order):
    block, others = begun
    own = order(jnp.concatenate([block] + order.each(others), 0))
    return [own, lay.to_core(own)]


def rows_done(rows, order):
    rows[1] = order(rows[1])
    return rows


def sums_start(own, sib, lay, order):
    return own, lay.to_core(order(sib.astype(BF16)))


def sums_middle(begun, lay, order):
    own, got = begun
    own = own + order(got).astype(F32)
    rows = own.shape[0] // lay.group
    parts = own.reshape(lay.group, rows, -1)
    sent = order.each([parts[step].astype(BF16) for step in range(1, lay.group)])
    return parts[0], [lay.to_member(block, step) for step, block in enumerate(sent, 1)]


def sums_done(begun, order):
    total, others = begun
    for block in order.each(others):
        total = total + block.astype(F32)
    return total


def norm_forward(inputs, gain_vec):
    inverse_rms = lax.rsqrt(jnp.mean(inputs * inputs, -1, keepdims=True) + NORM_EPS)
    return (inputs * inverse_rms * gain_vec).astype(BF16), inverse_rms


def norm_backward(inputs, inverse_rms, gain_vec, upstream):
    scaled = upstream * gain_vec
    input_grad = inverse_rms * scaled - inputs * inverse_rms**3 * jnp.mean(
        scaled * inputs, -1, keepdims=True
    )
    gain_grad = jnp.sum(upstream * inputs * inverse_rms, 0)
    return input_grad, gain_grad


def out_order(block, lay, n_query):
    if head_copies(lay) > 1:
        share = (lay.core * lay.group + lay.member) % head_copies(lay) == 0
        return jnp.where(share, block, jnp.zeros_like(block))
    if n_query != 2 or lay.cores * lay.group != KV_HEADS:
        return block
    swapped = jnp.concatenate([block[:, LANES:], block[:, :LANES]], 1)
    return jnp.where(lay.shard == 0, block, swapped)


class Layer:
    def __init__(self, lay, tables, n_query, n_key, gain_one, gain_two):
        self.lay, self.tables, self.n_query, self.n_key = lay, tables, n_query, n_key
        self.gain_one, self.gain_two = gain_one, gain_two

    def first_norm(self, inputs):
        self.inputs = inputs
        normed, self.inverse_first = norm_forward(inputs, self.gain_one)
        return relative(normed, self.lay)

    def attend(self):
        raw = [mm(block, self.qkv_w) for block in self.normed]
        out_own, out_sib, lse, own, sib = attend(*raw, self.tables, self.n_query, self.n_key)
        self.attn_kept = own, sib, lse
        self.attn_out = [out_order(block, self.lay, self.n_query) for block in (out_own, out_sib)]

    def out_partial(self):
        return [mm(block, self.out_w) for block in self.attn_out]

    def second_norm(self, attended):
        self.mid_stream = self.inputs + attended
        normed, self.inverse_second = norm_forward(self.mid_stream, self.gain_two)
        return relative(normed, self.lay)

    def hide(self):
        self.gate_up, self.hidden = [], []
        for block in self.normed_mid:
            gate_pre, up_pre = mm(block, self.gate_w), mm(block, self.up_w)
            self.gate_up.append((gate_pre, up_pre))
            hidden = (jax.nn.silu(gate_pre) * up_pre).astype(BF16)
            self.hidden.append(relative(hidden, self.lay))

    def down_partial(self):
        return [mm(block, self.down_w) for block in self.hidden]

    def feed_forward_back(self):
        self.gate_grad, self.up_grad, partial = [], [], []
        for block, (gate_pre, up_pre) in zip(self.down_in, self.gate_up):
            hidden_grad = relative(mm_nt(block, self.down_w), self.lay)
            sigmoid_gate = jax.nn.sigmoid(gate_pre)
            gate_grad_in = (
                hidden_grad * up_pre * sigmoid_gate * (1.0 + gate_pre * (1.0 - sigmoid_gate))
            ).astype(BF16)
            up_grad_in = (hidden_grad * gate_pre * sigmoid_gate).astype(BF16)
            self.gate_grad.append(gate_grad_in)
            self.up_grad.append(up_grad_in)
            partial.append(mm_nt(gate_grad_in, self.gate_w) + mm_nt(up_grad_in, self.up_w))
        return partial

    def second_norm_back(self, out_grad, upstream):
        part, self.gain_two_grad = norm_backward(
            self.mid_stream, self.inverse_second, self.gain_two, relative(upstream, self.lay)
        )
        self.mid_grad = out_grad + part
        return self.mid_grad.astype(BF16)

    def attention_back(self, order):
        grads = [
            out_order(mm_nt(block, self.out_w).astype(BF16), self.lay, self.n_query)
            for block in self.mid_low
        ]
        self.lows = attend_back(self.attn_kept, grads, self.tables, self.n_query, self.n_key)
        self.lows = order.each(self.lows)
        return [mm_nt(block, self.qkv_w) for block in self.lows]

    def first_norm_back(self, upstream):
        part, gain_one_grad = norm_backward(
            self.inputs, self.inverse_first, self.gain_one, relative(upstream, self.lay)
        )
        self.gain_grads = jnp.stack([gain_one_grad, self.gain_two_grad])
        return self.mid_grad + part


def joined(pair):
    return jnp.concatenate(pair, 0)


def row_tables(pair_table, block_rows, lay):
    cores = []
    for core in (lay.core, 1 - lay.core):
        ctx_ids = jnp.stack([core * lay.group + (lay.member ^ step) for step in range(lay.group)])
        owned = jnp.sum(
            jnp.where(ctx_ids[:, None] == jnp.arange(lay.ctx)[None, :], pair_table[None, :], 0), 1
        )
        blocks = jnp.stack([owned, 2 * lay.ctx - 1 - owned], 1)
        rows = blocks[:, :, None] * block_rows + jnp.arange(block_rows)[None, None, :]
        cores.append(rows.reshape(-1))
    positions = jnp.concatenate(cores)
    freq_idx = jnp.arange(HALF, dtype=F32)
    inverse = ROPE_BASE ** (-2.0 * freq_idx / HEAD_DIM)
    angles = positions.astype(F32)[:, None] * inverse[None, :]
    pad = ((0, 0), (0, HALF_LANES - HALF))
    cos_h, sin_h = jnp.pad(jnp.cos(angles), pad), jnp.pad(jnp.sin(angles), pad)
    cos_t = jnp.concatenate([cos_h, cos_h], 1)
    sin_t = jnp.concatenate([-sin_h, sin_h], 1)
    return cos_t, sin_t, positions[:, None], positions[None, :]


def deal_rows(local, lay, order):
    turn = lay.half ^ lay.core
    sent = order(pick(local, turn), pick(local, 1 - turn))
    straight = lay.move(
        sent[0], lambda core, half, member, shard: (half, half ^ core, member, shard)
    )
    crossed = lay.move(
        sent[1], lambda core, half, member, shard: (half, 1 - (half ^ core), member, shard)
    )
    return straight, crossed


def dealt(straight, crossed, lay):
    turn = lay.half ^ lay.core
    return jnp.where(turn == 0, straight, crossed), jnp.where(turn == 0, crossed, straight)


def return_rows(input_grad, outputs, lay, order):
    turn = lay.half ^ lay.core
    sent = order(
        jnp.where(turn == 0, input_grad, outputs), jnp.where(turn == 0, outputs, input_grad)
    )
    straight = lay.move(
        sent[0], lambda core, half, member, shard: (core ^ half, core, member, shard)
    )
    crossed = lay.move(
        sent[1], lambda core, half, member, shard: (1 - (core ^ half), core, member, shard)
    )
    return straight, crossed


def body(
    ends_in, pair_table, norm_attn, w_query, w_key, w_value, w_out, norm_mlp, w_gate, w_up, w_down
):
    lay = Layout()
    rows = ends_in.shape[3]
    width = ends_in.shape[4]
    row_block = w_query.shape[1]
    pairs = lay.cores * lay.group
    n_query = max(1, HEADS // pairs)
    n_key = max(1, KV_HEADS // pairs)
    ff_unit = w_down.shape[1] // lay.cores
    q_cols, k_cols = n_query * HEAD_DIM, n_key * HEAD_DIM
    spread_lanes = lane_matrix(n_query + 2 * n_key)
    spread_out = lane_matrix(n_query)
    cols = q_cols + 2 * k_cols
    ff = ff_unit * 4
    order = Order()

    def by_member(*blocks):
        return jnp.concatenate(blocks, 1).reshape(lay.group, row_block, -1)

    tables = row_tables(pair_table, rows // 2, lay)
    gains = jnp.stack([norm_attn[0], norm_mlp[0]])
    gain_parts = [lay.to_member(gains, step) for step in range(1, lay.group)]
    heads = pack_heads(w_query[0], w_key[0], w_value[0], lay)
    heads_other = split_cores(heads, lay, order)
    heads_other, *gain_parts = order(heads_other, *gain_parts)
    qkv_layers = core_layers(heads, heads_other, lay)
    qkv_others = to_members(qkv_layers[0], lay, order)
    gains = order(place(gains, gain_parts, lay.member))
    gains_other = lay.to_half(gains)
    w_gate, w_up, ends_in = order(w_gate, w_up, ends_in)
    own_rows = to_inner(ends_in[0, :, 0], lay)
    gate_up_own = pack_ff(w_gate[0], w_up[0], lay, ff_unit)
    gate_up_other = split_cores(gate_up_own, lay, order)
    rows_other = deal_rows(own_rows, lay, order)
    qkv_0 = Spread(member_rows(qkv_layers[0], order.each(qkv_others), lay), lay, order)
    qkv_0.half()
    gains = order(two_way(lay.half, gains, order(gains_other), 0))
    gains_other = lay.to_shard(gains)
    gains = order(two_way(lay.shard, gains, order(gains_other), 0))
    gains_other = lay.to_core(gains)
    out = SpreadOut(to_inner(order(w_out)[0], lay), lay, order)
    out.core()
    gains = two_way(lay.core, gains, order(gains_other), 0)
    gains = gains.transpose(0, 4, 1, 2, 3, 5).reshape(2, 2, -1).astype(F32)
    gate_up_layers = core_layers(gate_up_own, order(gate_up_other), lay)
    out.core_done()
    own_in, own_cot = dealt(*order(*rows_other), lay)
    first = Layer(lay, tables, n_query, n_key, gains[0, 0], gains[0, 1])
    second = Layer(lay, tables, n_query, n_key, gains[1, 0], gains[1, 1])
    normed = rows_start(first.first_norm(own_in.astype(F32)), lay, order)
    qkv_0.half_done()
    qkv_0.shard()
    out.half()
    normed = rows_middle(normed, lay, order)
    gate_up_others = to_members(gate_up_layers[0], lay, order)
    qkv_0.shard_done()
    out.half_done()
    out.shard()
    first.qkv_w = mm(qkv_0.full, spread_lanes).astype(BF16)
    first.normed = rows_done(normed, order)
    first.attend()
    first.attn_out = order.each(first.attn_out)
    gate_up = member_rows(gate_up_layers[0], order.each(gate_up_others), lay)
    gate_0 = Spread(gate_up[:, :ff], lay, order)
    up_0 = Spread(gate_up[:, ff:], lay, order)
    gate_0.half()
    down_own = to_inner(order(w_down)[0], lay).reshape(lay.cores, ff_unit, width)
    down_other = split_cores(down_own, lay, order)
    out.shard_done()
    first.out_w = mm_tn(spread_out, out.full[0]).astype(BF16)
    second.out_w = mm_tn(spread_out, out.full[1]).astype(BF16)
    sums = sums_middle(sums_start(*first.out_partial(), lay, order), lay, order)
    down_layers = core_layers(down_own, order(down_other), lay)
    down_0, down_1 = Spread(down_layers[0], lay, order), Spread(down_layers[1], lay, order)
    attended = sums_done(sums, order)
    gate_0.half_done()
    gate_0.shard()
    up_0.half()
    normed = rows_start(first.second_norm(attended), lay, order)
    normed = rows_middle(normed, lay, order)
    rest = jnp.concatenate([qkv_layers[1], gate_up_layers[1]], -1)
    rest_others = to_members(rest, lay, order)
    up_0.half_done()
    gate_0.shard_done()
    up_0.shard()
    down_0.half()
    first.normed_mid = rows_done(normed, order)
    rest = member_rows(rest, order.each(rest_others), lay)
    qkv_1 = Spread(rest[:, :cols], lay, order)
    gate_up_1 = Spread(rest[:, cols:], lay, order)
    up_0.shard_done()
    down_0.half_done()
    down_0.shard()
    own_cot = own_cot.astype(F32)
    cot = rows_start(own_cot.astype(BF16), lay, order)
    qkv_1.half()
    first.gate_w, first.up_w = gate_0.full, up_0.full
    first.hide()
    second.down_in = rows_middle(cot, lay, order)
    qkv_1.half_done()
    gate_up_1.half()
    down_0.shard_done()
    qkv_1.shard()
    first.down_w = down_0.full
    sums = sums_middle(sums_start(*first.down_partial(), lay, order), lay, order)
    first_out = first.mid_stream + sums_done(sums, order)
    normed = rows_start(second.first_norm(first_out.astype(BF16).astype(F32)), lay, order)
    normed = rows_middle(normed, lay, order)
    gate_up_1.half_done()
    gate_up_1.shard()
    down_1.half()
    qkv_1.shard_done()
    second.qkv_w = mm(qkv_1.full, spread_lanes).astype(BF16)
    second.normed = rows_done(normed, order)
    second.attend()
    sums = sums_start(*second.out_partial(), lay, order)
    sums = sums_middle(sums, lay, order)
    attended = sums_done(sums, order)
    gate_up_1.shard_done()
    down_1.half_done()
    down_1.shard()
    normed = rows_start(second.second_norm(attended), lay, order)
    normed = rows_middle(normed, lay, order)
    second.gate_w, second.up_w = gate_up_1.full[:, :ff], gate_up_1.full[:, ff:]
    second.normed_mid = rows_done(normed, order)
    second.down_in = rows_done(second.down_in, order)
    second.hide()

    down_g1 = Collect(joined(second.hidden), joined(second.down_in), lay, order)
    down_g1.shard()
    down_1.shard_done()
    second.down_w = down_1.full
    partial = second.feed_forward_back()
    sums = sums_start(*partial, lay, order)
    grads = [jnp.concatenate(pair, 1) for pair in zip(second.gate_grad, second.up_grad)]
    gate_up_g1 = Collect(joined(second.normed_mid), joined(grads), lay, order)
    sums = sums_middle(sums, lay, order)
    gate_up_g1.shard()
    upstream = sums_done(sums, order)
    low = second.second_norm_back(own_cot, upstream)
    down_g1.shard_done()
    low = rows_start(low, lay, order)
    low = rows_middle(low, lay, order)
    down_g1.half()
    second.mid_low = rows_done(low, order)
    partial = second.attention_back(order)
    sums = sums_start(*partial, lay, order)
    low = mm_nt(joined(second.lows), spread_lanes).astype(BF16)
    qkv_g1 = Collect(joined(second.normed), low, lay, order)
    gate_up_g1.shard_done()
    qkv_g1.shard()
    sums = sums_middle(sums, lay, order)
    upstream = sums_done(sums, order)
    down_g1.half_done()
    gate_up_g1.half()
    second_grad = second.first_norm_back(upstream)

    first_cot = second_grad.astype(BF16)
    down_in = rows_start(first_cot, lay, order)
    down_in = rows_middle(down_in, lay, order)
    first.down_in = rows_done(down_in, order)
    down_g0 = Collect(joined(first.hidden), joined(first.down_in), lay, order)
    qkv_g1.shard_done()
    down_g0.shard()
    partial = first.feed_forward_back()
    sums = sums_start(*partial, lay, order)
    left = joined(first.normed_mid)
    gate_g0 = Collect(left, joined(first.gate_grad), lay, order)
    up_g0 = Collect(left, joined(first.up_grad), lay, order)
    sums = sums_middle(sums, lay, order)
    upstream = sums_done(sums, order)
    gate_up_g1.half_done()
    qkv_g1.half()
    low = rows_start(first.second_norm_back(first_cot.astype(F32), upstream), lay, order)
    down_g0.shard_done()
    gate_g0.shard()
    low = rows_middle(low, lay, order)
    qkv_g1.half_done()
    down_g0.half()
    first.mid_low = rows_done(low, order)
    partial = first.attention_back(order)
    gate_g0.shard_done()
    up_g0.shard()
    down_g0.half_done()
    gate_g0.half()
    sums = sums_start(*partial, lay, order)
    low = mm_nt(joined(first.lows), spread_lanes).astype(BF16)
    qkv_g0 = Collect(joined(first.normed), low, lay, order)
    sums = sums_middle(sums, lay, order)
    upstream = sums_done(sums, order)
    first_grad = first.first_norm_back(upstream)

    out_both = CollectOut(
        [out_pair(which, spread_out) for which in (first, second)], lay, order, row_block
    )
    up_g0.shard_done()
    up_g0.half()
    qkv_g0.shard()
    mlp_1 = by_member(gate_up_g1.total)
    others_1 = to_members(mlp_1.astype(BF16), lay, order)
    gate_g0.half_done()
    up_g0.half_done()
    others_1 = order.each(others_1)
    gains = jnp.stack([first.gain_grads, second.gain_grads])
    gains_other = lay.to_core(order(pick(gains, 1 - lay.core)))
    mlp_0 = by_member(gate_g0.total, up_g0.total)
    others_0 = to_members(mlp_0.astype(BF16), lay, order)
    qkv_g0.shard_done()
    qkv_g0.half()
    out_both.shard()
    outputs = sums_start(*second.down_partial(), lay, order)
    down_join = join_cores(down_g0.total, down_g1.total, lay, order)
    back_1 = place(pick(mlp_1, lay.member), [block.astype(F32) for block in others_1], lay.member)
    others_0 = order.each(others_0)
    gains = pick(gains, lay.core) + order(gains_other)
    gains = gains.reshape(2, lay.shards, lay.halves, lay.group, -1).transpose(1, 2, 3, 0, 4)
    outputs = sums_middle(outputs, lay, order)
    back_0 = place(pick(mlp_0, lay.member), [block.astype(F32) for block in others_0], lay.member)
    ff_join = join_cores(back_0, back_1, lay, order)
    out_both.shard_done()
    out_both.half()
    gains_other = lay.to_shard(order(pick(gains, 1 - lay.shard)))
    second_out = second.mid_stream + sums_done(outputs, order)
    qkv_g0.half_done()
    attn = by_member(qkv_g0.total, qkv_g1.total)
    others_q = to_members(attn.astype(BF16), lay, order)
    rows_other = return_rows(first_grad.astype(BF16), second_out.astype(BF16), lay, order)
    gains = pick(gains, lay.shard) + order(gains_other)
    gains_other = lay.to_half(order(pick(gains, 1 - lay.half)))
    gate_up_g = order.each(unpack_ff(joined_cores(ff_join, lay, order), lay, ff_unit))
    others_q = order.each(others_q)
    back_q = place(pick(attn, lay.member), [block.astype(F32) for block in others_q], lay.member)
    qkv_join = join_cores(back_q[..., :cols], back_q[..., cols:], lay, order)
    out_both.half_done()
    out_join = join_out_start(*out_both.total, lay, order, row_block)
    gains = pick(gains, lay.half) + order(gains_other)
    gain_g = pick(gains, lay.member)
    gain_others = to_members(gains, lay, order)
    down_g = to_outer(jnp.concatenate(joined_cores(down_join, lay, order), 0).reshape(-1, width), lay)
    qkv_g = unpack_heads(joined_cores(qkv_join, lay, order), lay)
    straight, crossed = order(*rows_other)
    ends = two_way(lay.half ^ lay.core, straight, crossed, 0)
    out_g = to_outer(join_out(out_join, lay, order), lay)
    for block in order.each(gain_others):
        gain_g = gain_g + block
    ends = to_outer(ends, lay)
    return (
        ends[None, :, None],
        gain_g[0][None],
        qkv_g[0][None],
        qkv_g[1][None],
        qkv_g[2][None],
        out_g[None],
        gain_g[1][None],
        gate_up_g[0][None],
        gate_up_g[1][None],
        down_g[None],
    )


def solution(mesh):
    rows = P("section", None, "shard", "ctx", None)
    vector = P("section", ("ctx", "shard"))
    matrix = P("section", ("ctx", "shard"), None)
    return jax.shard_map(
        body,
        mesh=mesh,
        in_specs=(rows, P(), vector, matrix, matrix, matrix, matrix, vector, matrix, matrix, matrix),
        out_specs=(rows, vector, matrix, matrix, matrix, matrix, vector, matrix, matrix, matrix),
        check_vma=False,
    )
```
